32 devices in a mesh: dp: 32 (over z, y, x, core).
Axes of the slice: x: 2, y: 2, z: 4, core: 2. Of those that a mesh axis runs over, the one named last changes fastest.
Arguments:
- visual: bfloat16 [32, 512, 768], P('dp'), may hold values from -40 to 40
- text: bfloat16 [32, 512, 768], P('dp'), may hold values from -6 to 6
- lengths: int32 [32], P('dp'), may hold values from 20 to 512, as said below
- text_boxes: int32 [32, 2, 512], P('dp'), may hold values from 0 to 127
- cot_visual: bfloat16 [32, 512, 768], P('dp'), may hold values from -6 to 6
- cot_text: bfloat16 [32, 512, 768], P('dp'), may hold values from -6 to 6
- attn_w: float32 [2, 4, 768, 768], P(None, None, 'dp'), may hold values from -4 to 4
- ffn_in: float32 [2, 768, 3072], P(None, 'dp'), may hold values from -0.21875 to 0.21875
- ffn_out: float32 [2, 3072, 768], P(None, 'dp'), may hold values from -0.109375 to 0.109375
- bias_in: float32 [2, 3072], P(None, 'dp'), may hold values from -4 to 4
- vectors: float32 [12, 768], P(None, 'dp'), may hold values from -2 to 2
- pos_tables: float32 [2, 3, 12, 128], P(None, None, None, 'dp'), may hold values from -3 to 3
- spatial: float32 [2, 128, 768], P(None, 'dp'), may hold values from -3 to 3
- attn_mom: float32 [2, 4, 768, 768], P(None, None, 'dp'), may hold values from -1 to 1
- attn_sec: float32 [2, 4, 768, 768], P(None, None, 'dp'), may hold values from 0 to 1, as said below
- in_mom: float32 [2, 768, 3072], P(None, 'dp'), may hold values from -1 to 1
- in_sec: float32 [2, 768, 3072], P(None, 'dp'), may hold values from 0 to 1, as said below
- out_mom: float32 [2, 3072, 768], P(None, 'dp'), may hold values from -1 to 1
- out_sec: float32 [2, 3072, 768], P(None, 'dp'), may hold values from 0 to 1, as said below
- bias_mom: float32 [2, 3072], P(None, 'dp'), may hold values from -1 to 1
- bias_sec: float32 [2, 3072], P(None, 'dp'), may hold values from 0 to 1, as said below
- vec_mom: float32 [12, 768], P(None, 'dp'), may hold values from -1 to 1
- vec_sec: float32 [12, 768], P(None, 'dp'), may hold values from 0 to 1, as said below
- pos_mom: float32 [2, 3, 12, 128], P(None, None, None, 'dp'), may hold values from -1 to 1
- pos_sec: float32 [2, 3, 12, 128], P(None, None, None, 'dp'), may hold values from 0 to 1, as said below
- spatial_mom: float32 [2, 128, 768], P(None, 'dp'), may hold values from -1 to 1
- spatial_sec: float32 [2, 128, 768], P(None, 'dp'), may hold values from 0 to 1, as said below
Outputs:
- out_visual: bfloat16 [32, 512, 768], P('dp')
- out_text: bfloat16 [32, 512, 768], P('dp')
- grad_visual: float32 [32, 512, 768], P('dp')
- grad_text: float32 [32, 512, 768], P('dp')
- grad_norm: float32 [], replicated
- attn_mom_new: float32 [2, 4, 768, 768], P(None, None, 'dp')
- attn_sec_new: float32 [2, 4, 768, 768], P(None, None, 'dp')
- attn_new: float32 [2, 4, 768, 768], P(None, None, 'dp')
- attn_copy: bfloat16 [2, 4, 768, 768], P(None, None, 'dp')
- in_mom_new: float32 [2, 768, 3072], P(None, 'dp')
- in_sec_new: float32 [2, 768, 3072], P(None, 'dp')
- in_new: float32 [2, 768, 3072], P(None, 'dp')
- in_copy: bfloat16 [2, 768, 3072], P(None, 'dp')
- out_mom_new: float32 [2, 3072, 768], P(None, 'dp')
- out_sec_new: float32 [2, 3072, 768], P(None, 'dp')
- out_new: float32 [2, 3072, 768], P(None, 'dp')
- out_copy: bfloat16 [2, 3072, 768], P(None, 'dp')
- bias_mom_new: float32 [2, 3072], P(None, 'dp')
- bias_sec_new: float32 [2, 3072], P(None, 'dp')
- bias_new: float32 [2, 3072], P(None, 'dp')
- vec_mom_new: float32 [12, 768], P(None, 'dp')
- vec_sec_new: float32 [12, 768], P(None, 'dp')
- vec_new: float32 [12, 768], P(None, 'dp')
- pos_mom_new: float32 [2, 3, 12, 128], P(None, None, None, 'dp')
- pos_sec_new: float32 [2, 3, 12, 128], P(None, None, None, 'dp')
- pos_new: float32 [2, 3, 12, 128], P(None, None, None, 'dp')
- spatial_mom_new: float32 [2, 128, 768], P(None, 'dp')
- spatial_sec_new: float32 [2, 128, 768], P(None, 'dp')
- spatial_new: float32 [2, 128, 768], P(None, 'dp')
The draws below stay inside these ranges and needn't reach their ends.
Inputs may be any that keep to these rules, and one draw needn't show every extreme that they name: `lengths`: at least one page has 512 text tokens. `attn_sec`: positive. `in_sec`: positive. `out_sec`: positive. `bias_sec`: positive. `vec_sec`: positive. `pos_sec`: positive. `spatial_sec`: positive.
All inputs are finite; a program needn't handle non-finite values.
Results may differ from the reference program's by a relative error of at most 0.015.
The reference program's roundings to bfloat16 on the way count: a program that leaves them out, or rounds other values in their place, can miss the bound.
Values may be sent and summed in bfloat16 or wider, within the bound.
No kernel may reach another device: no remote copies, remote signals or barrier semaphores. Data moves between devices by JAX's collectives and lax.ppermute only.
A program may use at most 256 MiB of HBM per device.

```python
import math
import jax
import jax.numpy as jnp
from jax import lax

D = 768
H = 12
FF = 3072
HD = 64
VROWS = 16
VCOLS = 32
NV = 512
MINLEN = 20
NB = 128
NR = 128
STEP = 10
PAGES = 32


def grad_size(factor):
    return factor / math.sqrt(8 * D * D + 4 * D * FF + 2 * FF + 12 * D + 6 * H * NR + 2 * NB * D)


def first_moment(key, shape, factor):
    noise = jax.random.truncated_normal(key, -3.0, 3.0, shape, jnp.float32)
    return noise * (0.1 / 0.9) * grad_size(factor)


def second_moment(key, shape, factor):
    spread = jax.random.uniform(key, shape, jnp.float32, 1.0, 4.0)
    return spread * (0.05 / 0.95) * grad_size(factor) ** 2


def draw_visual(key, part):
    key = jax.random.fold_in(key, 11)
    first_key, second_key = jax.random.split(key)
    shape = (PAGES, NV, D)
    channel = jnp.exp(jax.random.uniform(second_key, (D,), jnp.float32, 0.0, math.log(3.0)))
    ramp = jnp.arange(PAGES, dtype=jnp.float32) / max(PAGES - 1, 1)
    noise = jax.random.truncated_normal(first_key, -4.0, 4.0, shape, jnp.float32)
    rising = 1.0 + 2.0 * ramp
    return (noise * rising[:, None, None] * channel).astype(jnp.bfloat16)


def draw_lengths(key, part):
    key = jax.random.fold_in(key, 12)
    first_key, second_key = jax.random.split(key)
    base = jax.random.randint(first_key, (PAGES,), MINLEN, NV + 1)
    chosen = jax.random.randint(second_key, (), 0, PAGES)
    return jnp.where(jnp.arange(PAGES) == chosen, NV, base).astype(jnp.int32)


def draw_attn_w(key, part):
    key = jax.random.fold_in(key, 13)
    shape = (2, 4, D, D)
    noise = jax.random.truncated_normal(key, -4.0, 4.0, shape, jnp.float32)
    scales = jnp.array([1.3, 1.3, 1.0, math.sqrt(NV)], jnp.float32) / math.sqrt(D)
    return noise * scales[None, :, None, None]


def draw_vectors(key, part):
    key = jax.random.fold_in(key, 14)
    first_key, second_key = jax.random.split(key)
    ramp = jnp.arange(D, dtype=jnp.float32) / D
    rising = 0.5 + ramp
    gains = rising[None, :] * jax.random.uniform(first_key, (12, D), jnp.float32, 0.8, 1.2)
    shifts = 0.2 * jax.random.truncated_normal(second_key, -4.0, 4.0, (12, D), jnp.float32)
    rows = jnp.arange(12)
    is_gain = (rows % 2 == 0) & (rows < 10)
    return jnp.where(is_gain[:, None], gains, shifts)


def draw_attn_mom(key, part):
    return first_moment(jax.random.fold_in(key, 21), (2, 4, D, D), 1.0)


def draw_attn_sec(key, part):
    return second_moment(jax.random.fold_in(key, 22), (2, 4, D, D), 1.0)


def draw_in_mom(key, part):
    return first_moment(jax.random.fold_in(key, 23), (2, D, FF), 1.0)


def draw_in_sec(key, part):
    return second_moment(jax.random.fold_in(key, 24), (2, D, FF), 1.0)


def draw_out_mom(key, part):
    return first_moment(jax.random.fold_in(key, 25), (2, FF, D), 1.0)


def draw_out_sec(key, part):
    return second_moment(jax.random.fold_in(key, 26), (2, FF, D), 1.0)


def draw_bias_mom(key, part):
    return first_moment(jax.random.fold_in(key, 27), (2, FF), 0.8)


def draw_bias_sec(key, part):
    return second_moment(jax.random.fold_in(key, 28), (2, FF), 0.8)


def draw_vec_mom(key, part):
    return first_moment(jax.random.fold_in(key, 29), (12, D), 5.0)


def draw_vec_sec(key, part):
    return second_moment(jax.random.fold_in(key, 30), (12, D), 5.0)


def draw_pos_mom(key, part):
    return first_moment(jax.random.fold_in(key, 31), (2, 3, H, NR), 2.0)


def draw_pos_sec(key, part):
    return second_moment(jax.random.fold_in(key, 32), (2, 3, H, NR), 2.0)


def draw_spatial_mom(key, part):
    return first_moment(jax.random.fold_in(key, 33), (2, NB, D), 0.5)


def draw_spatial_sec(key, part):
    return second_moment(jax.random.fold_in(key, 34), (2, NB, D), 0.5)


def with_ends(values, own_key, low, top_value):
    longest = values.shape.index(max(values.shape))
    spots = []
    for shift in (0, 1):
        where = [jax.random.randint(jax.random.fold_in(own_key, axis), (), 0, length) for axis, length in enumerate(values.shape)]
        where[longest] = (where[longest] + shift) % values.shape[longest]
        spots.append(tuple(where))
    return values.at[spots[0]].set(low).at[spots[1]].set(top_value)


def block_levels(stream_key, extent, cuts, least, largest):
    level = 1.0
    for position, parts in cuts:
        heights = jax.random.uniform(jax.random.fold_in(jax.random.fold_in(stream_key, 6), position), (parts,), jnp.float32, least / len(cuts), largest / len(cuts))
        level = level * jnp.repeat(jnp.exp(heights), extent[position] // parts).reshape((-1,) + (1,) * (len(extent) - 1 - position))
    return level


def bell_draw(rng, shape, scale, limit, pieces=(), held_as=jnp.bfloat16):
    entries = jax.random.normal(rng, shape, jnp.float32) * scale
    if len(pieces) > 0:
        entries = block_levels(rng, shape, pieces, -0.22, 0.18) * entries
    return jnp.clip(entries, min=-limit, max=limit).astype(held_as)


def setup_inputs(seed: int = 0) -> dict:
    keys = jax.random.split(jax.random.key(seed), 28)
    visual = draw_visual(jax.random.fold_in(keys[27], 71), 0)
    text = bell_draw(keys[1], (PAGES, NV, D), 1.0, 6.0, ((0, 32),))
    lengths = draw_lengths(jax.random.fold_in(keys[27], 71), 0)
    text_boxes = with_ends(jax.random.randint(keys[3], (PAGES, 2, NV), 0, NB), jax.random.fold_in(keys[3], 1), 0, NB - 1).astype(jnp.int32)
    cot_visual = bell_draw(keys[4], (PAGES, NV, D), 1.0, 6.0, ((0, 32),))
    cot_text = bell_draw(keys[5], (PAGES, NV, D), 1.0, 6.0, ((0, 32),))
    attn_w = draw_attn_w(jax.random.fold_in(keys[27], 71), 0)
    ffn_in = bell_draw(keys[7], (2, D, FF), D ** -0.5, 0.21875, ((1, 32),), jnp.float32)
    ffn_out = bell_draw(keys[8], (2, FF, D), FF ** -0.5, 0.109375, ((1, 32),), jnp.float32)
    bias_in = bell_draw(keys[9], (2, FF), 0.3, 4.0, ((1, 32),), jnp.float32)
    vectors = draw_vectors(jax.random.fold_in(keys[27], 71), 0)
    pos_tables = bell_draw(keys[11], (2, 3, H, NR), 0.5, 3.0, ((3, 32),), jnp.float32)
    spatial = bell_draw(keys[12], (2, NB, D), 0.5, 3.0, ((1, 32),), jnp.float32)
    attn_mom = draw_attn_mom(jax.random.fold_in(keys[27], 71), 0)
    attn_sec = draw_attn_sec(jax.random.fold_in(keys[27], 71), 0)
    in_mom = draw_in_mom(jax.random.fold_in(keys[27], 71), 0)
    in_sec = draw_in_sec(jax.random.fold_in(keys[27], 71), 0)
    out_mom = draw_out_mom(jax.random.fold_in(keys[27], 71), 0)
    out_sec = draw_out_sec(jax.random.fold_in(keys[27], 71), 0)
    bias_mom = draw_bias_mom(jax.random.fold_in(keys[27], 71), 0)
    bias_sec = draw_bias_sec(jax.random.fold_in(keys[27], 71), 0)
    vec_mom = draw_vec_mom(jax.random.fold_in(keys[27], 71), 0)
    vec_sec = draw_vec_sec(jax.random.fold_in(keys[27], 71), 0)
    pos_mom = draw_pos_mom(jax.random.fold_in(keys[27], 71), 0)
    pos_sec = draw_pos_sec(jax.random.fold_in(keys[27], 71), 0)
    spatial_mom = draw_spatial_mom(jax.random.fold_in(keys[27], 71), 0)
    spatial_sec = draw_spatial_sec(jax.random.fold_in(keys[27], 71), 0)
    return {"visual": visual, "text": text, "lengths": lengths, "text_boxes": text_boxes, "cot_visual": cot_visual, "cot_text": cot_text, "attn_w": attn_w, "ffn_in": ffn_in, "ffn_out": ffn_out, "bias_in": bias_in, "vectors": vectors, "pos_tables": pos_tables, "spatial": spatial, "attn_mom": attn_mom, "attn_sec": attn_sec, "in_mom": in_mom, "in_sec": in_sec, "out_mom": out_mom, "out_sec": out_sec, "bias_mom": bias_mom, "bias_sec": bias_sec, "vec_mom": vec_mom, "vec_sec": vec_sec, "pos_mom": pos_mom, "pos_sec": pos_sec, "spatial_mom": spatial_mom, "spatial_sec": spatial_sec}


HIGH = lax.Precision.HIGHEST
EPSILON = 1e-05
NEGATIVE = -1000000000.0
CLIP = 1.0
BETA_ONE = 0.9
BETA_TWO = 0.95
ADAM_EPS = 1e-08
DECAY = 0.1
RATE_ATTN = 0.15
RATE_FEED = 0.04
RATE_OTHER = 0.2

@jax.custom_vjp
def low(v):
    return lax.optimization_barrier(v.astype(jnp.bfloat16)).astype(jnp.float32)

@jax.custom_vjp
def low_back(v):
    return v

def low_keep(v):
    return (low(v), None)

def low_pass(kept, grad):
    return (grad,)

def back_keep(v):
    return (v, None)

def back_low(kept, grad):
    return (low(grad),)
low.defvjp(low_keep, low_pass)
low_back.defvjp(back_keep, back_low)

def matmul(left, right):
    return jnp.dot(left, right, precision=HIGH)

def layer_norm(rows, gain, shift):
    center = rows - lax.optimization_barrier(jnp.mean(rows, axis=-1, keepdims=True))
    spread = lax.optimization_barrier(jnp.mean(center * center, axis=-1, keepdims=True))
    return center * lax.rsqrt(spread + EPSILON) * gain + shift

def relative(first, second):
    return jnp.clip(second[None, :] - first[:, None], -(NR // 2), NR // 2 - 1) + NR // 2

def one_hot(index):
    return (index[..., None] == jnp.arange(NB)).astype(jnp.float32)

def attend(inputs, place, weights, bias, keep):
    joint = low(inputs + low_back(place))
    plain = low(inputs)
    queries = low(low_back(matmul(joint, weights[0]))).reshape(NV, H, HD)
    key_rows = low(low_back(matmul(joint, weights[1]))).reshape(NV, H, HD)
    values = low(low_back(matmul(plain, weights[2]))).reshape(NV, H, HD)
    scores = jnp.einsum('ihd,jhd->hij', queries, key_rows, precision=HIGH) * HD ** (-0.5) + bias
    scores = jnp.where(keep[None, None, :], low_back(scores), NEGATIVE)
    probs = low(jax.nn.softmax(scores, axis=-1))
    mixed = jnp.einsum('hij,jhd->ihd', probs, values, precision=HIGH).reshape(NV, D)
    mixed = low(low_back(mixed))
    return low_back(matmul(mixed, weights[3]))

def feed(rows, first, first_bias, second, second_bias):
    hidden = low(rows)
    before = low_back(matmul(hidden, first) + first_bias)
    active = low(jax.nn.gelu(before, approximate=False))
    return low_back(matmul(active, second) + second_bias)

def page(params, visual_in, text_in, length, boxes):
    attn_w, ffn_in, ffn_out, bias_in, vectors, pos_tables, spatial = params
    index = jnp.arange(NV)
    keep_text = index < length
    keep_all = index >= 0
    grid_x = index % VCOLS * (NB // VCOLS) + NB // VCOLS // 2
    grid_y = index // VCOLS * (NB // VROWS) + NB // VROWS // 2
    line = relative(index, index)
    vis_bias = pos_tables[0, 0][:, line] + pos_tables[0, 1][:, relative(grid_x, grid_x)] + pos_tables[0, 2][:, relative(grid_y, grid_y)]
    txt_bias = pos_tables[1, 0][:, line] + pos_tables[1, 1][:, relative(boxes[0], boxes[0])] + pos_tables[1, 2][:, relative(boxes[1], boxes[1])]
    vis_place = matmul(one_hot(grid_x), spatial[0]) + matmul(one_hot(grid_y), spatial[1])
    txt_place = matmul(one_hot(boxes[0]), spatial[0]) + matmul(one_hot(boxes[1]), spatial[1])
    vis_att = attend(visual_in, vis_place, attn_w[0], vis_bias, keep_all)
    txt_att = attend(text_in, txt_place, attn_w[1], txt_bias, keep_text)
    mask = keep_text.astype(jnp.float32)[:, None]
    merged = vis_att + mask * txt_att
    vis_u = layer_norm(visual_in + merged, vectors[2], vectors[3])
    txt_u = layer_norm(text_in + merged, vectors[4], vectors[5])
    vis_out = layer_norm(vis_u + feed(vis_u, ffn_in[0], bias_in[0], ffn_out[0], vectors[10]), vectors[6], vectors[7])
    txt_out = layer_norm(txt_u + feed(txt_u, ffn_in[1], bias_in[1], ffn_out[1], vectors[11]), vectors[8], vectors[9]) * mask
    return (vis_out, txt_out)

def adam(weight, grad, first, second, rate, decay):
    first_new = BETA_ONE * first + (1 - BETA_ONE) * grad
    second_new = BETA_TWO * second + (1 - BETA_TWO) * grad * grad
    ratio = first_new / (1 - BETA_ONE ** STEP) / (jnp.sqrt(second_new / (1 - BETA_TWO ** STEP)) + ADAM_EPS)
    return (first_new, second_new, weight - rate * (ratio + decay * weight))

def reference(visual, text, lengths, text_boxes, cot_visual, cot_text, attn_w, ffn_in, ffn_out, bias_in, vectors, pos_tables, spatial, attn_mom, attn_sec, in_mom, in_sec, out_mom, out_sec, bias_mom, bias_sec, vec_mom, vec_sec, pos_mom, pos_sec, spatial_mom, spatial_sec):
    raw = visual.astype(jnp.float32)
    mean = lax.optimization_barrier(jnp.mean(raw, axis=(0, 1)))
    variance = lax.optimization_barrier(jnp.mean(raw * raw, axis=(0, 1))) - mean * mean
    inverse = lax.rsqrt(variance + EPSILON)

    def forward(params, visual_f, text_f):
        lowered = (low(params[0]), low(params[1]), low(params[2]), params[3], params[4], low(params[5]), low(params[6]))
        gains = params[4]
        visual_in = (visual_f - mean) * inverse * gains[0] + gains[1]

        def one_page(items):
            return page(lowered, items[0], items[1], items[2], items[3])
        return lax.map(jax.checkpoint(one_page), (visual_in, text_f, lengths, text_boxes))
    params = (attn_w, ffn_in, ffn_out, bias_in, vectors, pos_tables, spatial)
    outputs, pullback = jax.vjp(forward, params, raw, text.astype(jnp.float32))
    grads, grad_visual, grad_text = pullback((cot_visual.astype(jnp.float32), cot_text.astype(jnp.float32)))
    squares = jnp.float32(0.0)
    for grad in grads:
        squares = squares + jnp.sum(grad * grad)
    grad_norm = jnp.sqrt(squares)
    factor = CLIP / jnp.maximum(grad_norm, CLIP)
    states = ((attn_mom, attn_sec), (in_mom, in_sec), (out_mom, out_sec), (bias_mom, bias_sec), (vec_mom, vec_sec), (pos_mom, pos_sec), (spatial_mom, spatial_sec))
    rates = (RATE_ATTN, RATE_FEED, RATE_FEED, RATE_OTHER, RATE_OTHER, RATE_OTHER, RATE_OTHER)
    decays = (DECAY, DECAY, DECAY, 0.0, 0.0, 0.0, DECAY)
    results = []
    for weight, grad, state, rate, decay in zip(params, grads, states, rates, decays):
        results.append(adam(weight, grad * factor, state[0], state[1], rate, decay))
    return (outputs[0].astype(jnp.bfloat16), outputs[1].astype(jnp.bfloat16), grad_visual, grad_text, grad_norm, results[0][0], results[0][1], results[0][2], results[0][2].astype(jnp.bfloat16), results[1][0], results[1][1], results[1][2], results[1][2].astype(jnp.bfloat16), results[2][0], results[2][1], results[2][2], results[2][2].astype(jnp.bfloat16), results[3][0], results[3][1], results[3][2], results[4][0], results[4][1], results[4][2], results[5][0], results[5][1], results[5][2], results[6][0], results[6][1], results[6][2])
```

```python
import functools

import jax
import jax.numpy as jnp
import numpy as np
from jax import lax
from jax.experimental import pallas as pl
from jax.experimental.pallas import tpu as pltpu
from jax.sharding import Mesh
from jax.sharding import PartitionSpec as P

H = 12
HD = 64
VROWS = 16
VCOLS = 32
NB = 128
NR = 128
STEP = 10

EPSILON = 1e-05
NEGATIVE = -1000000000.0
CLIP = 1.0
BETA_ONE = 0.9
BETA_TWO = 0.95
ADAM_EPS = 1e-08
DECAY = 0.1
RATE_ATTN = 0.15
RATE_FEED = 0.04
RATE_OTHER = 0.2

BF = jnp.bfloat16
F32 = jnp.float32
AXES = ("z", "y", "x", "c")
CHIP = ("z", "y", "x")
FEED_BLOCK = 512
VMEM_LIMIT = 56 * 1024 * 1024
NT = (((1,), (1,)), ((), ()))


def dot(left, right):
    return jnp.dot(left, right, preferred_element_type=F32)


def dot_nt(left, right):
    return lax.dot_general(left, right, NT, preferred_element_type=F32)


def swap(value):
    return lax.ppermute(value, "c", [(0, 1), (1, 0)])


def shift(value, axis, step):
    size = lax.axis_size(axis)
    return lax.ppermute(value, axis, [(i, (i + step) % size) for i in range(size)])


def diagonal(value, step_y, step_x):
    ny, nx = lax.axis_size("y"), lax.axis_size("x")
    pairs = [
        (y * nx + x, (y + step_y) % ny * nx + (x + step_x) % nx)
        for y in range(ny)
        for x in range(nx)
    ]
    return lax.ppermute(value, ("y", "x"), pairs)


def chip_of(dz, dy, dx):
    nz, ny, nx = (lax.axis_size(a) for a in CHIP)
    z = (lax.axis_index("z") - dz) % nz
    y = (lax.axis_index("y") - dy) % ny
    x = (lax.axis_index("x") - dx) % nx
    return (z * ny + y) * nx + x


def gather_pieces(piece, order):
    nz = lax.axis_size("z")
    stack = jnp.stack([piece] + [shift(piece, "z", k) for k in range(1, nz)])
    first, second = ("x", "y") if order == 0 else ("y", "x")
    found = []
    firsts = [stack] + [shift(stack, first, k) for k in range(1, lax.axis_size(first))]
    for one, part in enumerate(firsts):
        for two in range(lax.axis_size(second)):
            moved = part if two == 0 else shift(part, second, two)
            found.append((moved, (two, one) if order == 0 else (one, two)))
    return found


def place_kernel(parts, count, lead, *refs):
    where, sources, out = refs[0], refs[1 : 1 + parts], refs[1 + parts]
    size = sources[0].shape[1] if lead else sources[0].shape[-1]
    for part in range(parts):
        begin = 2 * part // parts * size
        for k in range(count):
            spot = where[part * count + k]
            if lead:
                for row in range(size):
                    out[begin + row, spot] = sources[part][k, row]
            else:
                out[spot, :, begin : begin + size] = sources[part][k]


def gather_matrix(halves, chips, lead):
    nz = lax.axis_size("z")
    found = gather_pieces(halves[0], 0) + gather_pieces(halves[1], 1)
    where = jnp.stack([chip_of(k, sy, sx) for _, (sy, sx) in found for k in range(nz)])
    parts = [part for part, _ in found]
    shape = halves[0].shape
    if lead:
        whole = (2 * shape[0], chips) + shape[1:]
    else:
        whole = (chips,) + shape[:-1] + (2 * shape[-1],)
    return pl.pallas_call(
        functools.partial(place_kernel, len(parts), nz, lead),
        out_shape=jax.ShapeDtypeStruct(whole, halves[0].dtype),
        in_specs=[pl.BlockSpec(memory_space=pltpu.SMEM)]
        + [pl.BlockSpec(memory_space=pltpu.VMEM)] * len(parts),
        out_specs=pl.BlockSpec(memory_space=pltpu.VMEM),
        compiler_params=pltpu.CompilerParams(vmem_limit_bytes=VMEM_LIMIT),
        name="place",
    )(where.astype(jnp.int32), *parts)


def slot_table(order):
    nz, ny, nx = (lax.axis_size(a) for a in CHIP)
    chips = jnp.arange(nz * ny * nx)
    zr = (chips // (ny * nx) - lax.axis_index("z")) % nz
    yr = (chips // nx % ny - lax.axis_index("y")) % ny
    xr = (chips % nx - lax.axis_index("x")) % nx
    if order == 0:
        return ((xr * ny + yr) * nz + zr).astype(jnp.int32)
    return ((yr * nx + xr) * nz + zr).astype(jnp.int32)


def scatter_plane(slots, order):
    first, second = ("x", "y") if order == 0 else ("y", "x")
    nz = lax.axis_size("z")
    for axis in (first, second):
        size = lax.axis_size(axis)
        parts = slots.reshape((size, -1) + slots.shape[1:])
        total = parts[0].astype(F32)
        for k in range(1, size):
            total = total + shift(parts[k], axis, k).astype(F32)
        slots = total.astype(BF)
    return slots.reshape((nz,) + slots.shape[1:])


def scatter_line(column):
    total = column[0].astype(F32)
    for k in range(1, lax.axis_size("z")):
        total = total + shift(column[k], "z", k).astype(F32)
    return total


def split_three(value):
    high = lax.reduce_precision(value, 8, 7)
    rest = value - high
    mid = lax.reduce_precision(rest, 8, 7)
    return [high.astype(BF), mid.astype(BF), (rest - mid).astype(BF)]


def join_three(parts):
    high, mid, small = (part.astype(F32) for part in parts)
    return high + (mid + small)


def base_rows(tables):
    half = NR // 2
    low, high = tables[:, :, :1], tables[:, :, -1:]
    one = tables.shape[:2]

    def many(edge, count):
        return jnp.broadcast_to(edge, one + (count,))

    line = jnp.concatenate(
        [many(high, NB - half + 1), tables[:, :, ::-1], many(low, 255 - half), many(high, 128)],
        axis=2,
    )[0]
    plane = jnp.concatenate(
        [tables[:, :, half:], many(high, NB - half), many(low, NB - half), tables[:, :, :half]], axis=2
    )
    pair = jnp.concatenate([plane[1], plane[2]], axis=1)
    rows = jnp.stack([line, pair], axis=1)
    return jnp.pad(rows, ((0, 0), (0, 6), (0, 0)))


def table_sums(sums):
    half = NR // 2
    line = jnp.concatenate([sums[:, 0, 384:], sums[:, 0, :384]], axis=1)[:, ::-1]
    far = jnp.sum(sums[:, 2, 256:], axis=1) + jnp.sum(line[:, : 256 - half], axis=1)
    near = jnp.sum(sums[:, 2, :256], axis=1) + jnp.sum(line[:, 254 + half :], axis=1)
    middle = line[:, 256 - half : 254 + half]
    first = jnp.concatenate([far[:, None], middle, near[:, None]], axis=1)

    def plane(part):
        ordered = jnp.concatenate([part[:, 128:], part[:, :128]], axis=1)[:, ::-1]
        low = jnp.sum(ordered[:, : 128 - half], axis=1)
        high = jnp.sum(ordered[:, 126 + half :], axis=1)
        return jnp.concatenate(
            [low[:, None], ordered[:, 128 - half : 126 + half], high[:, None]], axis=1
        )

    return jnp.stack([first, plane(sums[:, 1, :256]), plane(sums[:, 1, 256:])])


def build_tables(base, strip, planes, head):
    line = jnp.broadcast_to(base[head, 0:1, :], (128, 512))
    middle = pltpu.roll(line, 0, 1, stride=1, stride_axis=0)[:, :384]
    strip[head, :, 256:640] = middle
    strip[head, :, :256] = jnp.broadcast_to(base[head, 0:1, 0:1], (128, 256))
    strip[head, :, 640:] = jnp.broadcast_to(base[head, 0:1, 383:384], (128, 256))
    for k in range(2):
        row = jnp.broadcast_to(base[head, 1:2, 256 * k : 256 * k + 256], (128, 256))
        rolled = pltpu.roll(row, 0, 1, stride=1, stride_axis=0)
        planes[head, k] = rolled[:, :128].astype(BF)


def left_side(both, planes, head):
    return jnp.concatenate(
        [
            dot(both[:, :NB], planes[head, 0]).astype(BF),
            dot(both[:, NB:], planes[head, 1]).astype(BF),
        ],
        axis=1,
    )


def head_lanes(value, head):
    lanes = lax.broadcasted_iota(jnp.int32, value.shape, 1)
    return jnp.where((lanes >= HD) == (head == 1), value, jnp.zeros_like(value))


def scores_t(key_side, query_side, strip, head, valid):
    count = key_side.shape[0]
    raw = dot_nt(key_side, query_side)
    blocks = []
    for block in range(count // 128):
        start = 384 - 128 * block
        part = raw[128 * block : 128 * block + 128] + strip[head, :, start : start + count]
        rows = lax.broadcasted_iota(jnp.int32, (128, count), 0) + 128 * block
        blocks.append(jnp.where(rows < valid, part, NEGATIVE))
    return blocks


def attend_kernel(valid_ref, q_ref, k_ref, v_ref, both_ref, base_ref, mixed_ref, log_ref, strip, planes):
    page = pl.program_id(1)

    @pl.when(page == 0)
    def _():
        for head in range(2):
            build_tables(base_ref, strip, planes, head)

    valid = valid_ref[page]
    both = both_ref[...]
    key_side = jnp.concatenate([both, k_ref[...]], axis=1)
    values_t = v_ref[...].T
    mixed = []
    for head in range(2):
        query_side = jnp.concatenate(
            [left_side(both, planes, head), head_lanes(q_ref[...], head)], axis=1
        )
        blocks = scores_t(key_side, query_side, strip, head, valid)
        highest = functools.reduce(
            jnp.maximum, [jnp.max(block, axis=0, keepdims=True) for block in blocks]
        )
        raised = [jnp.exp(block - highest) for block in blocks]
        total = functools.reduce(
            jnp.add, [jnp.sum(part, axis=0, keepdims=True) for part in raised]
        )
        inverse = 1.0 / total
        probs = jnp.concatenate([(part * inverse).astype(BF) for part in raised], axis=0)
        mixed.append(dot(values_t[HD * head : HD * head + HD], probs))
        log_ref[0, 0, head : head + 1, :] = highest + jnp.log(total)
    mixed_ref[...] = jnp.concatenate(mixed, axis=0).T.astype(BF)


def attend_call(valid, queries, keys, values, both, base, count):
    pages = queries.shape[0] // count
    pairs = H // 2
    wide = pl.BlockSpec((count, 128), lambda pair, page: (page, pair))
    return pl.pallas_call(
        attend_kernel,
        grid=(pairs, pages),
        in_specs=[
            pl.BlockSpec(memory_space=pltpu.SMEM),
            wide,
            wide,
            wide,
            pl.BlockSpec((count, 2 * NB), lambda pair, page: (page, 0)),
            pl.BlockSpec((2, 8, 512), lambda pair, page: (pair, 0, 0)),
        ],
        out_specs=[
            wide,
            pl.BlockSpec((1, 1, 8, count), lambda pair, page: (page, pair, 0, 0)),
        ],
        out_shape=[
            jax.ShapeDtypeStruct(queries.shape, BF),
            jax.ShapeDtypeStruct((pages, pairs, 8, count), F32),
        ],
        scratch_shapes=[
            pltpu.VMEM((2, 128, count + 384), F32),
            pltpu.VMEM((2, 2, NB, NB), BF),
        ],
        compiler_params=pltpu.CompilerParams(vmem_limit_bytes=VMEM_LIMIT),
        name="attend",
    )(valid, queries, keys, values, both, base)


def fold_diagonals(value):
    rows, lanes = value.shape
    while rows > 1:
        rows //= 2
        value = value[:rows] + pltpu.roll(value[rows:], lanes - rows, 1)
    return value


def attend_back_kernel(
    valid_ref, q_ref, k_ref, v_ref, dm_ref, mixed_ref, log_ref, both_ref, both_t_ref, base_ref,
    dq_ref, dk_ref, dv_ref, sums_ref, strip, planes, d_strip, d_planes,
):
    page = pl.program_id(1)

    @pl.when(page == 0)
    def _():
        for head in range(2):
            build_tables(base_ref, strip, planes, head)
        d_strip[...] = jnp.zeros_like(d_strip)
        d_planes[...] = jnp.zeros_like(d_planes)

    valid = valid_ref[page]
    both = both_ref[...]
    both_t = both_t_ref[...]
    count = both.shape[0]
    key_side = jnp.concatenate([both, k_ref[...]], axis=1)
    values = v_ref[...]
    keys_t = k_ref[...].T
    d_mixed_t = dm_ref[...].T
    weighted = d_mixed_t.astype(F32) * mixed_ref[...].T.astype(F32)
    rows = lax.broadcasted_iota(jnp.int32, d_mixed_t.shape, 0)
    d_keys = d_values = None
    d_queries = []
    for head in range(2):
        masked_q = head_lanes(q_ref[...], head)
        query_side = jnp.concatenate([left_side(both, planes, head), masked_q], axis=1)
        blocks = scores_t(key_side, query_side, strip, head, valid)
        log_total = log_ref[0, 0, head : head + 1, :]
        inner = jnp.sum(weighted[HD * head : HD * head + HD], axis=0, keepdims=True)
        d_mixed_head = jnp.where(
            (rows >= HD) == (head == 1), d_mixed_t, jnp.zeros_like(d_mixed_t)
        )
        d_probs = dot(values, d_mixed_head)
        probs_low, scores_low = [], []
        for index, block in enumerate(blocks):
            probs = jnp.exp(block - log_total)
            d_scores = probs * (d_probs[128 * index : 128 * index + 128] - inner)
            start = 384 - 128 * index
            d_strip[head, :, start : start + count] += d_scores
            probs_low.append(probs.astype(BF))
            scores_low.append(d_scores.astype(BF))
        probs_low = jnp.concatenate(probs_low, axis=0)
        scores_low = jnp.concatenate(scores_low, axis=0)
        part_v = dot(probs_low, head_lanes(dm_ref[...], head))
        mixed_k = dot(scores_low, jnp.concatenate([both, masked_q], axis=1))
        part_k = mixed_k[:, 2 * NB :]
        d_values = part_v if d_values is None else d_values + part_v
        d_keys = part_k if d_keys is None else d_keys + part_k
        d_queries.append(dot(keys_t[HD * head : HD * head + HD], scores_low))
        for k in range(2):
            side = mixed_k[:, NB * k : NB * k + NB].astype(BF)
            d_planes[head, k] += dot(both_t[NB * k : NB * k + NB], side)
    dq_ref[...] = (jnp.concatenate(d_queries, axis=0).T * HD ** (-0.5)).astype(BF)
    dk_ref[...] = d_keys.astype(BF)
    dv_ref[...] = d_values.astype(BF)

    @pl.when(page == pl.num_programs(1) - 1)
    def _():
        blank = jnp.zeros((128, 128), F32)
        for head in range(2):
            middle = jnp.concatenate([d_strip[head, :, 256:640], blank], axis=1)
            sums_ref[head, 0:1, :] = fold_diagonals(middle)
            for k in range(2):
                padded = jnp.concatenate([d_planes[head, k], blank], axis=1)
                sums_ref[head, 1:2, 256 * k : 256 * k + 256] = fold_diagonals(padded)
            sums_ref[head, 2:3, :256] = jnp.sum(d_strip[head, :, :256], axis=0, keepdims=True)
            sums_ref[head, 2:3, 256:] = jnp.sum(d_strip[head, :, 640:], axis=0, keepdims=True)


def attend_back_call(valid, queries, keys, values, d_mixed, mixed, log_total, both, base, count):
    pages = queries.shape[0] // count
    pairs = H // 2
    both_t = both.T
    wide = pl.BlockSpec((count, 128), lambda pair, page: (page, pair))
    return pl.pallas_call(
        attend_back_kernel,
        grid=(pairs, pages),
        in_specs=[
            pl.BlockSpec(memory_space=pltpu.SMEM),
            wide,
            wide,
            wide,
            wide,
            wide,
            pl.BlockSpec((1, 1, 8, count), lambda pair, page: (page, pair, 0, 0)),
            pl.BlockSpec((count, 2 * NB), lambda pair, page: (page, 0)),
            pl.BlockSpec((2 * NB, count), lambda pair, page: (0, page)),
            pl.BlockSpec((2, 8, 512), lambda pair, page: (pair, 0, 0)),
        ],
        out_specs=[wide, wide, wide, pl.BlockSpec((2, 8, 512), lambda pair, page: (pair, 0, 0))],
        out_shape=[jax.ShapeDtypeStruct(queries.shape, BF)] * 3
        + [jax.ShapeDtypeStruct((H, 8, 512), F32)],
        scratch_shapes=[
            pltpu.VMEM((2, 128, count + 384), F32),
            pltpu.VMEM((2, 2, NB, NB), BF),
            pltpu.VMEM((2, 128, count + 384), F32),
            pltpu.VMEM((2, 2, NB, NB), F32),
        ],
        compiler_params=pltpu.CompilerParams(vmem_limit_bytes=VMEM_LIMIT),
        name="attend_back",
    )(valid, queries, keys, values, d_mixed, mixed, log_total, both, both_t, base)


def gelu_parts(before):
    size = jnp.abs(before) * (0.5**0.5)
    denominator = 1.0 + 0.3275911 * size
    t = pl.reciprocal(denominator, approx=True)
    t = t * (2.0 - denominator * t)
    bell = jnp.exp(-0.5 * before * before)
    tail = t * (
        0.5 * 0.254829592
        + t
        * (
            0.5 * -0.284496736
            + t * (0.5 * 1.421413741 + t * (0.5 * -1.453152027 + t * (0.5 * 1.061405429)))
        )
    )
    tail = tail * bell
    below = jnp.where(before >= 0.0, 1.0 - tail, tail)
    return before * below, below + before * (bell * 0.3989422804014327)


def feed_kernel(rows_ref, first_ref, bias_ref, active_ref, slope_ref):
    before = dot(rows_ref[...], first_ref[...]) + bias_ref[...]
    active, slope = gelu_parts(before)
    active_ref[...] = active.astype(BF)
    slope_ref[...] = slope.astype(BF)


def feed_call(rows, first, bias, block):
    tokens, width = rows.shape
    hidden = first.shape[1]
    out = pl.BlockSpec((tokens, block), lambda i: (0, i))
    return pl.pallas_call(
        feed_kernel,
        grid=(hidden // block,),
        in_specs=[
            pl.BlockSpec((tokens, width), lambda i: (0, 0)),
            pl.BlockSpec((width, block), lambda i: (0, i)),
            pl.BlockSpec((1, block), lambda i: (0, i)),
        ],
        out_specs=[out, out],
        out_shape=[jax.ShapeDtypeStruct((tokens, hidden), BF)] * 2,
        compiler_params=pltpu.CompilerParams(vmem_limit_bytes=VMEM_LIMIT),
        name="feed",
    )(rows, first, bias)


def store_slots(slots_ref, out_ref, total, half):
    chips = out_ref.shape[1]
    rows = total.shape[0] // chips
    for chip in range(chips):
        part = total[chip * rows : chip * rows + rows].astype(BF)
        out_ref[0, slots_ref[0, chip]] = part[:, :half]
        out_ref[1, slots_ref[1, chip]] = part[:, half:]


def feed_back_kernel(slots_ref, rows_t_ref, low_ref, second_ref, first_ref, slope_ref, rest_ref, du_ref, dfirst_ref, dbias_ref):
    step = pl.program_id(0)
    d_active = dot_nt(low_ref[...], second_ref[...])
    d_before = (slope_ref[...].astype(F32) * d_active).astype(BF)
    dbias_ref[...] = jnp.sum(d_before.astype(F32), axis=0, keepdims=True)
    part = dot_nt(d_before, first_ref[...])

    @pl.when(step == 0)
    def _():
        du_ref[...] = rest_ref[...] + part

    @pl.when(step > 0)
    def _():
        du_ref[...] += part

    total = dot(rows_t_ref[...], d_before)
    store_slots(slots_ref, dfirst_ref, total, total.shape[1] // 2)


def feed_back_call(slots, rows, low, second, first, slope, rest, chips, block):
    tokens, width = rows.shape
    hidden = second.shape[0]
    piece = width // chips
    whole = pl.BlockSpec((tokens, width), lambda i: (0, 0))
    return pl.pallas_call(
        feed_back_kernel,
        grid=(hidden // block,),
        in_specs=[
            pl.BlockSpec(memory_space=pltpu.SMEM),
            pl.BlockSpec((width, tokens), lambda i: (0, 0)),
            whole,
            pl.BlockSpec((block, width), lambda i: (i, 0)),
            pl.BlockSpec((width, block), lambda i: (0, i)),
            pl.BlockSpec((tokens, block), lambda i: (0, i)),
            whole,
        ],
        out_specs=[
            whole,
            pl.BlockSpec((2, chips, piece, block // 2), lambda i: (0, 0, 0, i)),
            pl.BlockSpec((1, block), lambda i: (0, i)),
        ],
        out_shape=[
            jax.ShapeDtypeStruct((tokens, width), F32),
            jax.ShapeDtypeStruct((2, chips, piece, hidden // 2), BF),
            jax.ShapeDtypeStruct((1, hidden), F32),
        ],
        compiler_params=pltpu.CompilerParams(vmem_limit_bytes=VMEM_LIMIT),
        name="feed_back",
    )(slots, rows.T, low, second, first, slope, rest)


def outer_kernel(slots_ref, left_ref, right_ref, out_ref):
    chips = out_ref.shape[1]
    step = pl.program_id(0)
    total = dot(left_ref[...], right_ref[...])
    rows = out_ref.shape[2]
    count = total.shape[0] // rows
    half = total.shape[1] // 2
    for index in range(count):
        part = total[index * rows : index * rows + rows].astype(BF)
        chip = step * count + index
        out_ref[0, slots_ref[0, chip]] = part[:, :half]
        out_ref[1, slots_ref[1, chip]] = part[:, half:]


def outer_call(slots, left_t, right, chips, steps):
    height, tokens = left_t.shape
    width = right.shape[1]
    block = height // steps
    return pl.pallas_call(
        outer_kernel,
        grid=(steps,),
        in_specs=[
            pl.BlockSpec(memory_space=pltpu.SMEM),
            pl.BlockSpec((block, tokens), lambda i: (i, 0)),
            pl.BlockSpec((tokens, width), lambda i: (0, 0)),
        ],
        out_specs=pl.BlockSpec((2, chips, height // chips, width // 2), lambda i: (0, 0, 0, 0)),
        out_shape=jax.ShapeDtypeStruct((2, chips, height // chips, width // 2), BF),
        compiler_params=pltpu.CompilerParams(vmem_limit_bytes=VMEM_LIMIT),
        name="outer",
    )(slots, left_t, right)


def layer_norm(rows, gain, shift_row):
    center = rows - jnp.mean(rows, axis=-1, keepdims=True)
    spread = jnp.mean(center * center, axis=-1, keepdims=True)
    scale = lax.rsqrt(spread + EPSILON)
    hat = center * scale
    return hat * gain + shift_row, hat, scale


def layer_norm_back(grad, hat, scale, gain):
    scaled = grad * gain
    first = jnp.mean(scaled, axis=-1, keepdims=True)
    second = jnp.mean(scaled * hat, axis=-1, keepdims=True)
    d_rows = scale * (scaled - first - hat * second)
    return d_rows, jnp.sum(grad * hat, axis=0), jnp.sum(grad, axis=0)


def adam(weight, grad, first, second, rate, decay):
    first_new = BETA_ONE * first + (1 - BETA_ONE) * grad
    second_new = BETA_TWO * second + (1 - BETA_TWO) * grad * grad
    ratio = (
        first_new / (1 - BETA_ONE**STEP) / (jnp.sqrt(second_new / (1 - BETA_TWO**STEP)) + ADAM_EPS)
    )
    return (first_new, second_new, weight - rate * (ratio + decay * weight))


def body(
    visual, text, lengths, text_boxes, cot_visual, cot_text,
    attn_w, ffn_in, ffn_out, bias_in, vectors, pos_tables, spatial,
    attn_mom, attn_sec, in_mom, in_sec, out_mom, out_sec, bias_mom, bias_sec,
    vec_mom, vec_sec, pos_mom, pos_sec, spatial_mom, spatial_sec,
):
    core = lax.axis_index("c")
    seen = core == 0
    nz, ny, nx = (lax.axis_size(a) for a in CHIP)
    chips = nz * ny * nx
    devices = 2 * chips
    _, count, width = visual.shape
    tokens = 2 * count

    def mine_of(first, second):
        return jnp.where(seen, first, second)

    def trade(first, second):
        return mine_of(first, second), swap(mine_of(second, first))

    def by_core(own, other):
        return jnp.where(seen, jnp.stack([own, other]), jnp.stack([other, own]))

    attn_low = attn_w.astype(BF)
    in_low = ffn_in.astype(BF)
    out_low = ffn_out.astype(BF)
    attn_own, attn_other = trade(attn_low[0], attn_low[1])
    in_own, in_other = trade(in_low[0], in_low[1])
    out_own, out_other = trade(out_low[0], out_low[1])
    rows_a = attn_w.shape[2]
    rows_o = ffn_out.shape[1]
    hidden = ffn_in.shape[2]
    attn_piece = jnp.where(
        seen,
        jnp.concatenate([attn_own, attn_other], axis=1),
        jnp.concatenate([attn_other, attn_own], axis=1),
    )
    in_piece = by_core(in_own, in_other).reshape(2 * rows_a, hidden)
    out_piece = by_core(out_own, out_other).reshape(2 * rows_o, width)

    raw_own = visual[0].astype(F32)
    sums = jnp.stack([jnp.sum(raw_own, axis=0), jnp.sum(raw_own * raw_own, axis=0)])
    vec_rows = [
        jnp.stack([vectors[0], vectors[1]] + [vectors[k + 2 * s] for k in (2, 3, 6, 7)] + [vectors[10 + s]])
        for s in range(2)
    ]

    def packed(s):
        def row(values):
            flat = values.reshape(1, -1)
            return jnp.pad(flat, ((0, 0), (0, -flat.shape[1] % width))).reshape(-1, width)

        return jnp.concatenate(
            [row(pos_tables[s].astype(BF)), row(jnp.concatenate(
                [part.reshape(1, -1) for part in split_three(vec_rows[s]) + split_three(bias_in[s])], axis=1
            ))], axis=0
        )

    pack_zero, pack_one = packed(0), packed(1)
    small_rows = pack_zero.shape[0]
    space = spatial.astype(BF).reshape(-1, width)
    space_rows = space.shape[0]
    pack_own, pack_other = trade(pack_zero, pack_one)
    space_other, sums_other = swap((space, sums))
    pack_both = by_core(pack_own, pack_other).reshape(2 * small_rows, width)
    space_both = by_core(space, space_other).reshape(2 * space_rows, width)
    small = jnp.concatenate(
        [space_both, pack_both, jnp.concatenate(split_three(sums + sums_other), axis=0)], axis=0
    )
    small = jnp.pad(small, ((0, -small.shape[0] % 8), (0, 0)))
    column = jnp.stack([small] + [shift(small, "z", k) for k in range(1, nz)])
    plane = [
        (column if sy == 0 and sx == 0 else diagonal(column, sy, sx), sy, sx)
        for sy in range(ny)
        for sx in range(nx)
    ]
    nearby = jnp.concatenate([part for part, _, _ in plane], axis=0)
    source = jnp.stack([chip_of(k, sy, sx) for _, sy, sx in plane for k in range(nz)])
    place_of = jnp.zeros((chips,), jnp.int32).at[source].set(jnp.arange(chips, dtype=jnp.int32))
    gathered = jnp.take(nearby, place_of, axis=0)
    wide_spatial = gathered[:, : 2 * space_rows].reshape(chips, 2, 2, -1, width)
    wide_spatial = wide_spatial.transpose(2, 0, 1, 3, 4).reshape(2 * NB, width)
    packs = gathered[:, 2 * space_rows : 2 * space_rows + 2 * small_rows]
    packs = packs.reshape(devices, small_rows, width)
    pos_size = pos_tables[0].size
    pos_lines = -(-pos_size // width)
    tables = packs[:, :pos_lines].reshape(devices, -1)[:, :pos_size]
    tables = tables.reshape(devices, 3, H, -1).transpose(1, 2, 0, 3).reshape(3, H, NR).astype(F32)
    params = packs[:, pos_lines:].reshape(devices, -1)
    vec_size = vec_rows[0].size
    bias_size = bias_in[0].size
    wide_vec = join_three([params[:, vec_size * k : vec_size * (k + 1)] for k in range(3)])
    wide_vec = wide_vec.reshape(devices, 7, -1).transpose(1, 0, 2).reshape(7, width)
    wide_bias = join_three(
        [params[:, 3 * vec_size + bias_size * k : 3 * vec_size + bias_size * (k + 1)] for k in range(3)]
    ).reshape(1, hidden)
    parts = gathered[:, 2 * space_rows + 2 * small_rows :]
    sums = jnp.sum(join_three([parts[:, 2 * k : 2 * k + 2] for k in range(3)]), axis=0)

    data_own, data_other = trade(visual[0], text[0])
    cot_own, cot_other = trade(cot_visual[0], cot_text[0])
    length_other, boxes_other = swap((lengths, text_boxes))
    total = count * devices
    mean = sums[0] / total
    variance = sums[1] / total - mean * mean
    inverse = lax.rsqrt(variance + EPSILON)
    stream_mean = jnp.where(seen, mean, 0.0)
    stream_inverse = jnp.where(seen, inverse, 1.0)
    stream_gain = jnp.where(seen, wide_vec[0], 1.0)
    stream_shift = jnp.where(seen, wide_vec[1], 0.0)
    raw = jnp.concatenate([data_own, data_other], axis=0).astype(F32)
    normed = (raw - stream_mean) * stream_inverse
    inputs = normed * stream_gain + stream_shift
    position = jnp.arange(count, dtype=jnp.int32)
    lengths_both = jnp.concatenate([lengths, length_other])
    keep_pages = (position[None, :] < lengths_both[:, None]).astype(F32).reshape(tokens, 1)
    keep_rows = jnp.where(seen, 1.0, keep_pages)
    valid = jnp.where(seen, count, lengths_both).astype(jnp.int32)
    grid_x = position % VCOLS * (NB // VCOLS) + NB // VCOLS // 2
    grid_y = position // VCOLS * (NB // VROWS) + NB // VROWS // 2
    boxes = jnp.concatenate([text_boxes, boxes_other], axis=0)
    boxes = jnp.where(seen, jnp.stack([grid_x, grid_y])[None], boxes)
    both = jnp.concatenate(
        [
            (boxes[:, k, :].reshape(tokens, 1) == jnp.arange(NB)[None, :]).astype(BF)
            for k in range(2)
        ],
        axis=1,
    )
    place = dot(both, wide_spatial)
    joint = (inputs + place).astype(BF)
    plain = inputs.astype(BF)
    base = base_rows(tables)

    wide_attn = gather_matrix((attn_piece[:2], attn_piece[2:]), chips, True)
    wide_attn = wide_attn.reshape(4, width, width)
    half_in, half_out = hidden // 2, width // 2
    wide_in = gather_matrix((in_piece[:, :half_in], in_piece[:, half_in:]), chips, False)
    wide_in = wide_in.reshape(width, hidden)
    wide_out = gather_matrix((out_piece[:, :half_out], out_piece[:, half_out:]), chips, False)
    wide_out = wide_out.reshape(hidden, width)

    scale = HD ** (-0.5)
    queries = (dot(joint, wide_attn[0]).astype(BF) * scale).astype(BF)
    keys = dot(joint, wide_attn[1]).astype(BF)
    values = dot(plain, wide_attn[2]).astype(BF)
    mixed, log_total = attend_call(valid, queries, keys, values, both, base, count)
    att = dot(mixed, wide_attn[3])
    own_att = att * keep_rows
    other_att = swap(own_att)
    other_att = jnp.concatenate([other_att[count:], other_att[:count]], axis=0)
    merged = own_att + other_att

    u, hat_one, scale_one = layer_norm(inputs + merged, wide_vec[2], wide_vec[3])
    u_low = u.astype(BF)
    active, slope = feed_call(u_low, wide_in, wide_bias, FEED_BLOCK)
    ff = dot(active, wide_out) + wide_vec[6]
    y, hat_two, scale_two = layer_norm(u + ff, wide_vec[4], wide_vec[5])
    out = (y * keep_rows).astype(BF)

    cot = jnp.concatenate([cot_own, cot_other], axis=0).astype(F32) * keep_rows
    dy, gain_two, shift_two = layer_norm_back(cot, hat_two, scale_two, wide_vec[4])
    dff = dy.astype(BF)
    dff_sum = jnp.sum(dff.astype(F32), axis=0)
    slots = jnp.stack([slot_table(0), slot_table(1)])
    d_out = outer_call(slots, active.T, dff, chips, 4)
    du, d_in, d_bias = feed_back_call(slots, u_low, dff, wide_out, wide_in, slope, dy, chips, FEED_BLOCK)
    d_pre, gain_one, shift_one = layer_norm_back(du, hat_one, scale_one, wide_vec[2])

    other_pre = swap(d_pre)
    other_pre = jnp.concatenate([other_pre[count:], other_pre[:count]], axis=0)
    d_merged = d_pre + other_pre
    d_att = (d_merged * keep_rows).astype(BF)
    d_w3 = outer_call(slots, mixed.T, d_att, chips, 1)
    d_mixed = dot_nt(d_att, wide_attn[3]).astype(BF)
    dq, dk, dv, table_parts = attend_back_call(
        valid, queries, keys, values, d_mixed, mixed, log_total, both, base, count
    )
    joint_t = joint.T
    d_w0 = outer_call(slots, joint_t, dq, chips, 1)
    d_w1 = outer_call(slots, joint_t, dk, chips, 1)
    d_w2 = outer_call(slots, plain.T, dv, chips, 1)
    d_joint = dot_nt(dq, wide_attn[0]) + dot_nt(dk, wide_attn[1])
    dx = d_joint + dot_nt(dv, wide_attn[2]) + d_pre
    d_space = dot(both.T, d_joint.astype(BF))
    d_tables = table_sums(table_parts)
    norm_shift = jnp.sum(dx, axis=0)
    norm_gain = jnp.sum(dx * normed, axis=0)
    grad_rows = dx * stream_gain * stream_inverse

    def reduced(halves, blocks=1):
        sums = [scatter_line(scatter_plane(halves[k], k)) for k in range(2)]
        cut = jnp.stack([part.reshape(part.shape[0], blocks, -1) for part in sums], axis=2)
        return cut.reshape(cut.shape[0], -1)

    sum_out = reduced(d_out)
    sum_in = reduced(d_in, hidden // FEED_BLOCK)
    sum_attn = jnp.stack([reduced(part) for part in (d_w0, d_w1, d_w2, d_w3)])

    def own_rows(value, axis):
        first, second = jnp.split(value, 2, axis=axis)
        return trade(first, second)

    def by_stream(own, other):
        return jnp.where(seen, jnp.stack([own, other]), jnp.stack([other, own]))

    is_norm = jnp.where(seen, 1.0, 0.0)
    vec_grad = jnp.stack(
        [norm_gain * is_norm, norm_shift * is_norm, gain_one, shift_one, gain_two, shift_two, dff_sum]
    )

    def lines(values):
        flat = values.reshape(chips, -1)
        flat = jnp.pad(flat, ((0, 0), (0, -flat.shape[1] % width)))
        return flat.reshape(chips, -1, width)

    space_grad = d_space.reshape(2, chips, 2, -1, width).transpose(1, 2, 0, 3, 4)
    pos_grad = d_tables.reshape(3, H, chips, 2, -1).transpose(2, 3, 0, 1, 4)
    vecs = vec_grad.reshape(7, chips, 2, -1).transpose(1, 2, 0, 3)
    pieces = [
        space_grad.reshape(chips, -1, width),
        lines(pos_grad),
        lines(vecs),
        lines(d_bias),
    ]
    bounds = np.cumsum([0] + [part.shape[1] for part in pieces])
    small_grad = jnp.concatenate(pieces, axis=1)
    small_grad = jnp.pad(small_grad, ((0, 0), (0, -small_grad.shape[1] % 8), (0, 0)))
    order = jnp.zeros((chips,), jnp.int32).at[slots[0]].set(jnp.arange(chips, dtype=jnp.int32))
    small_slots = jnp.take(small_grad.astype(BF), order, axis=0)
    small_sum = scatter_line(scatter_plane(small_slots, 0))
    own_space, other_space = own_rows(small_sum[: bounds[1]], 0)
    grad_spatial = (own_space + other_space).reshape(spatial.shape)

    def unline(index, shape):
        size = int(np.prod(shape))
        flat = small_sum[bounds[index] : bounds[index + 1]].reshape(-1)[: 2 * size]
        return own_rows(flat.reshape((2,) + shape), 0)

    own_pos, other_pos = unline(1, pos_tables.shape[1:])
    grad_pos = by_stream(own_pos[0], other_pos[0])
    own_vec, other_vec = unline(2, (7, vectors.shape[1]))
    pair_vec = by_stream(own_vec[0], other_vec[0])
    grad_vec = jnp.stack(
        [pair_vec[0, 0], pair_vec[0, 1]]
        + [pair_vec[0, 2], pair_vec[0, 3], pair_vec[1, 2], pair_vec[1, 3]]
        + [pair_vec[0, 4], pair_vec[0, 5], pair_vec[1, 4], pair_vec[1, 5]]
        + [pair_vec[0, 6], pair_vec[1, 6]]
    )
    own_bias, other_bias = unline(3, bias_in.shape[1:])
    grad_bias = by_stream(own_bias[0], other_bias[0])

    squares = jnp.sum(sum_out * sum_out) + jnp.sum(sum_in * sum_in) + jnp.sum(sum_attn * sum_attn)
    for grad in (grad_spatial, grad_pos, grad_vec, grad_bias):
        squares = squares + jnp.sum(grad * grad)
    tile = jnp.full((8, 128), squares, F32)
    tile = tile + swap(tile)
    around = tile
    for sy in range(ny):
        for sx in range(nx):
            if sy or sx:
                around = around + diagonal(tile, sy, sx)
    norm = around
    for k in range(1, nz):
        norm = norm + shift(around, "z", k)
    grad_norm = jnp.sqrt(norm[0, 0])
    factor = CLIP / jnp.maximum(grad_norm, CLIP)

    grad_attn = by_stream(*own_rows(sum_attn, 1))
    grad_in = by_stream(*own_rows(sum_in, 0))
    grad_out = by_stream(*own_rows(sum_out, 0))

    out_own, out_other = out[:count], swap(out[count:])
    grad_own, grad_other = grad_rows[:count], swap(grad_rows[count:])
    out_visual = mine_of(out_own, out_other)[None]
    out_text = mine_of(out_other, out_own)[None]
    grad_visual = mine_of(grad_own, grad_other)[None]
    grad_text = mine_of(grad_other, grad_own)[None]

    params = (attn_w, ffn_in, ffn_out, bias_in, vectors, pos_tables, spatial)
    grads = (grad_attn, grad_in, grad_out, grad_bias, grad_vec, grad_pos, grad_spatial)
    states = (
        (attn_mom, attn_sec), (in_mom, in_sec), (out_mom, out_sec), (bias_mom, bias_sec),
        (vec_mom, vec_sec), (pos_mom, pos_sec), (spatial_mom, spatial_sec),
    )
    rates = (RATE_ATTN, RATE_FEED, RATE_FEED, RATE_OTHER, RATE_OTHER, RATE_OTHER, RATE_OTHER)
    decays = (DECAY, DECAY, DECAY, 0.0, 0.0, 0.0, DECAY)
    results = [out_visual, out_text, grad_visual, grad_text, grad_norm]
    for index, (weight, grad, state, rate, decay) in enumerate(
        zip(params, grads, states, rates, decays)
    ):
        new = adam(weight, grad * factor, state[0], state[1], rate, decay)
        results.extend(new)
        if index < 3:
            results.append(new[2].astype(BF))
    return tuple(results)


def solution(mesh):
    devices = mesh.devices.reshape(-1)
    chips = devices.size // 2
    deep = 4 if chips % 4 == 0 else 1
    side = int(round((chips // deep) ** 0.5))
    if deep * side * side != chips:
        deep, side = chips, 1
    fine = Mesh(devices.reshape(deep, side, side, 2), AXES)
    every = AXES
    data = P(every, None, None)
    in_specs = (
        data, data, P(every), data, data, data,
        P(None, None, every, None), P(None, every, None), P(None, every, None),
        P(None, every), P(None, every), P(None, None, None, every), P(None, every, None),
        P(None, None, every, None), P(None, None, every, None),
        P(None, every, None), P(None, every, None), P(None, every, None), P(None, every, None),
        P(None, every), P(None, every), P(None, every), P(None, every),
        P(None, None, None, every), P(None, None, None, every),
        P(None, every, None), P(None, every, None),
    )
    weights = P(None, None, every, None)
    rows = P(None, every, None)
    flat = P(None, every)
    last = P(None, None, None, every)
    out_specs = (
        (data, data, data, data, P())
        + (weights,) * 4 + (rows,) * 8 + (flat,) * 6 + (last,) * 3 + (rows,) * 3
    )
    return jax.shard_map(body, mesh=fine, in_specs=in_specs, out_specs=out_specs, check_vma=False)
```

```python
import functools

import jax
import jax.numpy as jnp
import numpy as np
from jax import lax
from jax.experimental import pallas as pl
from jax.experimental.pallas import tpu as pltpu
from jax.sharding import Mesh
from jax.sharding import PartitionSpec as P

H = 12
HD = 64
VROWS = 16
VCOLS = 32
NB = 128
NR = 128
STEP = 10

EPSILON = 1e-05
NEGATIVE = -1000000000.0
CLIP = 1.0
BETA_ONE = 0.9
BETA_TWO = 0.95
ADAM_EPS = 1e-08
DECAY = 0.1
RATE_ATTN = 0.15
RATE_FEED = 0.04
RATE_OTHER = 0.2

BF = jnp.bfloat16
F32 = jnp.float32
AXES = ("z", "y", "x", "c")
CHIP = ("z", "y", "x")
VMEM_LIMIT = 56 * 1024 * 1024
NT = (((1,), (1,)), ((), ()))


def cost(microseconds):
    return pl.CostEstimate(
        flops=int(microseconds * 1.1e9), bytes_accessed=int(microseconds * 3.5e6), transcendentals=0
    )


def params_of():
    return pltpu.CompilerParams(vmem_limit_bytes=VMEM_LIMIT)


def dot(left, right):
    return jnp.dot(left, right, preferred_element_type=F32)


def dot_nt(left, right):
    return lax.dot_general(left, right, NT, preferred_element_type=F32)


def swap(value):
    return lax.ppermute(value, "c", [(0, 1), (1, 0)])


def shift(value, axis, step):
    size = lax.axis_size(axis)
    return lax.ppermute(value, axis, [(i, (i + step) % size) for i in range(size)])


def diagonal(value, step_y, step_x):
    ny, nx = lax.axis_size("y"), lax.axis_size("x")
    pairs = [
        (y * nx + x, (y + step_y) % ny * nx + (x + step_x) % nx)
        for y in range(ny)
        for x in range(nx)
    ]
    return lax.ppermute(value, ("y", "x"), pairs)


def after(value, others):
    return lax.optimization_barrier((value, others))[0]


def chip_of(dz, dy, dx):
    nz, ny, nx = (lax.axis_size(a) for a in CHIP)
    z = (lax.axis_index("z") - dz) % nz
    y = (lax.axis_index("y") - dy) % ny
    x = (lax.axis_index("x") - dx) % nx
    return (z * ny + y) * nx + x


def around(value):
    steps = [(y, x) for y in range(lax.axis_size("y")) for x in range(lax.axis_size("x"))]
    return [value] + [diagonal(value, sy, sx) for sy, sx in steps[1:]]


def plane_steps():
    return [(y, x) for y in range(lax.axis_size("y")) for x in range(lax.axis_size("x"))]


def line_of(piece):
    return [piece] + [shift(piece, "z", k) for k in range(1, lax.axis_size("z"))]


def sources_of():
    nz = lax.axis_size("z")
    return jnp.stack([chip_of(k, sy, sx) for sy, sx in plane_steps() for k in range(nz)]).astype(
        jnp.int32
    )


def relay(piece):
    line = jnp.stack(line_of(piece))
    nz = line.shape[0]
    sizes = {"x": lax.axis_size("x"), "y": lax.axis_size("y")}
    half = line.shape[-1] // 2
    halves, sources = [], []
    for part, (first, second) in enumerate((("x", "y"), ("y", "x"))):
        moved = line[..., half * part : half * part + half]
        near = jnp.concatenate([moved] + [shift(moved, first, k) for k in range(1, sizes[first])], axis=0)
        halves.append([near] + [shift(near, second, k) for k in range(1, sizes[second])])
        sources.append(
            [
                chip_of(k, two, one) if first == "x" else chip_of(k, one, two)
                for two in range(sizes[second])
                for one in range(sizes[first])
                for k in range(nz)
            ]
        )
    return halves, [jnp.stack(source).astype(jnp.int32) for source in sources]


def inverse_of(where):
    return jnp.zeros_like(where).at[where].set(jnp.arange(where.shape[0], dtype=jnp.int32))


def in_order(stacks, where, begin, end):
    found = jnp.concatenate([part[:, begin:end] for part in stacks], axis=0)
    return jnp.take(found, inverse_of(where), axis=0)


def grouped(whole, rows, groups, lead=0):
    width = whole.shape[2]
    first = whole[:, :lead].reshape(-1, width)
    others = whole[:, lead:].reshape(-1, groups, rows, width).transpose(1, 0, 2, 3).reshape(-1, width)
    return jnp.concatenate([first, others], axis=0)[None], others.shape[0] // groups


def place(where_ref, refs, target, begin=0):
    count, _, width = refs[0].shape
    for index, ref in enumerate(refs):
        for k in range(count):
            target[where_ref[index * count + k], :, begin : begin + width] = ref[k]


def slot_table():
    nz, ny, nx = (lax.axis_size(a) for a in CHIP)
    chips = jnp.arange(nz * ny * nx)
    zr = (chips // (ny * nx) - lax.axis_index("z")) % nz
    yr = (chips // nx % ny - lax.axis_index("y")) % ny
    xr = (chips % nx - lax.axis_index("x")) % nx
    return ((yr * nx + xr) * nz + zr).astype(jnp.int32)


def scatter_plane(slots, others=()):
    nz = lax.axis_size("z")
    total = after(slots[:nz], others).astype(F32)
    for index, (sy, sx) in enumerate(plane_steps()):
        if index:
            part = diagonal(slots[nz * index : nz * index + nz], sy, sx)
            total = total + part.astype(F32)
    return total.astype(BF)


def scatter_line(column):
    total = column[0].astype(F32)
    for k in range(1, lax.axis_size("z")):
        total = total + shift(column[k], "z", k).astype(F32)
    return total


def split_three(value):
    high = lax.reduce_precision(value, 8, 7)
    rest = value - high
    mid = lax.reduce_precision(rest, 8, 7)
    return [high.astype(BF), mid.astype(BF), (rest - mid).astype(BF)]


def join_three(parts):
    high, mid, small = (part.astype(F32) for part in parts)
    return high + (mid + small)


def base_rows(tables):
    half = NR // 2
    low, high = tables[:, :, :1], tables[:, :, -1:]
    one = tables.shape[:2]

    def many(edge, count):
        return jnp.broadcast_to(edge, one + (count,))

    line = jnp.concatenate(
        [many(high, NB - half + 1), tables[:, :, ::-1], many(low, 255 - half), many(high, 128)],
        axis=2,
    )[0]
    plane = jnp.concatenate(
        [tables[:, :, half:], many(high, NB - half), many(low, NB - half), tables[:, :, :half]], axis=2
    )
    pair = jnp.concatenate([plane[1], plane[2]], axis=1)
    rows = jnp.stack([line, pair], axis=1)
    return jnp.pad(rows, ((0, 0), (0, 6), (0, 0)))


def table_sums(sums):
    half = NR // 2
    line = jnp.concatenate([sums[:, 0, 384:], sums[:, 0, :384]], axis=1)[:, ::-1]
    far = jnp.sum(sums[:, 2, 256:], axis=1) + jnp.sum(line[:, : 256 - half], axis=1)
    near = jnp.sum(sums[:, 2, :256], axis=1) + jnp.sum(line[:, 254 + half :], axis=1)
    middle = line[:, 256 - half : 254 + half]
    first = jnp.concatenate([far[:, None], middle, near[:, None]], axis=1)

    def plane(part):
        ordered = jnp.concatenate([part[:, 128:], part[:, :128]], axis=1)[:, ::-1]
        low = jnp.sum(ordered[:, : 128 - half], axis=1)
        high = jnp.sum(ordered[:, 126 + half :], axis=1)
        return jnp.concatenate(
            [low[:, None], ordered[:, 128 - half : 126 + half], high[:, None]], axis=1
        )

    return jnp.stack([first, plane(sums[:, 1, :256]), plane(sums[:, 1, 256:])])


def build_tables(base, strip, planes, head):
    line = jnp.broadcast_to(base[head, 0:1, :], (128, 512))
    middle = pltpu.roll(line, 0, 1, stride=1, stride_axis=0)[:, :384]
    strip[head, :, 256:640] = middle
    strip[head, :, :256] = jnp.broadcast_to(base[head, 0:1, 0:1], (128, 256))
    strip[head, :, 640:] = jnp.broadcast_to(base[head, 0:1, 383:384], (128, 256))
    for k in range(2):
        row = jnp.broadcast_to(base[head, 1:2, 256 * k : 256 * k + 256], (128, 256))
        rolled = pltpu.roll(row, 0, 1, stride=1, stride_axis=0)
        planes[head, k] = rolled[:, :128].astype(BF)


def left_side(both, planes, head):
    return jnp.concatenate(
        [
            dot(both[:, :NB], planes[head, 0]).astype(BF),
            dot(both[:, NB:], planes[head, 1]).astype(BF),
        ],
        axis=1,
    )


def head_lanes(value, head):
    lanes = lax.broadcasted_iota(jnp.int32, value.shape, 1)
    return jnp.where((lanes >= HD) == (head == 1), value, jnp.zeros_like(value))


def scores_t(key_side, query_side, strip, head, valid):
    count = key_side.shape[0]
    raw = dot_nt(key_side, query_side)
    blocks = []
    for block in range(count // 128):
        start = 384 - 128 * block
        part = raw[128 * block : 128 * block + 128] + strip[head, :, start : start + count]
        rows = lax.broadcasted_iota(jnp.int32, (128, count), 0) + 128 * block
        blocks.append(jnp.where(rows < valid, part, NEGATIVE))
    return blocks


def attend_kernel(valid_ref, q_ref, k_ref, v_ref, both_ref, base_ref, mixed_ref, log_ref, strip, planes):
    page = pl.program_id(1)

    @pl.when(page == 0)
    def _():
        for head in range(2):
            build_tables(base_ref, strip, planes, head)

    valid = valid_ref[page]
    both = both_ref[...]
    key_side = jnp.concatenate([both, k_ref[...]], axis=1)
    values_t = v_ref[...].T
    mixed = []
    for head in range(2):
        query_side = jnp.concatenate(
            [left_side(both, planes, head), head_lanes(q_ref[...], head)], axis=1
        )
        blocks = scores_t(key_side, query_side, strip, head, valid)
        highest = functools.reduce(
            jnp.maximum, [jnp.max(block, axis=0, keepdims=True) for block in blocks]
        )
        raised = [jnp.exp(block - highest) for block in blocks]
        total = functools.reduce(
            jnp.add, [jnp.sum(part, axis=0, keepdims=True) for part in raised]
        )
        inverse = 1.0 / total
        probs = jnp.concatenate([(part * inverse).astype(BF) for part in raised], axis=0)
        mixed.append(dot(values_t[HD * head : HD * head + HD], probs))
        log_ref[0, 0, head : head + 1, :] = highest + jnp.log(total)
    mixed_ref[...] = jnp.concatenate(mixed, axis=0).T.astype(BF)


def attend_call(valid, projected, both, base, count):
    pages = projected.shape[1] // count
    pairs = H // 2

    def part(index):
        return pl.BlockSpec((None, count, 128), lambda pair, page: (index, page, pair))

    return pl.pallas_call(
        attend_kernel,
        grid=(pairs, pages),
        in_specs=[
            pl.BlockSpec(memory_space=pltpu.SMEM),
            part(0),
            part(1),
            part(2),
            pl.BlockSpec((count, 2 * NB), lambda pair, page: (page, 0)),
            pl.BlockSpec((2, 8, 512), lambda pair, page: (pair, 0, 0)),
        ],
        out_specs=[
            pl.BlockSpec((count, 128), lambda pair, page: (page, pair)),
            pl.BlockSpec((1, 1, 8, count), lambda pair, page: (page, pair, 0, 0)),
        ],
        out_shape=[
            jax.ShapeDtypeStruct(projected.shape[1:], BF),
            jax.ShapeDtypeStruct((pages, pairs, 8, count), F32),
        ],
        scratch_shapes=[
            pltpu.VMEM((2, 128, count + 384), F32),
            pltpu.VMEM((2, 2, NB, NB), BF),
        ],
        compiler_params=params_of(),
        name="attend",
        cost_estimate=cost(28),
    )(valid, projected, projected, projected, both, base)


def fold_diagonals(value):
    rows, lanes = value.shape
    while rows > 1:
        rows //= 2
        value = value[:rows] + pltpu.roll(value[rows:], lanes - rows, 1)
    return value


def attend_back_kernel(
    valid_ref, q_ref, k_ref, v_ref, dm_ref, mixed_ref, log_ref, both_ref, both_t_ref, base_ref,
    grad_ref, sums_ref, strip, planes, d_strip, d_planes,
):
    page = pl.program_id(1)

    @pl.when(page == 0)
    def _():
        for head in range(2):
            build_tables(base_ref, strip, planes, head)
        d_strip[...] = jnp.zeros_like(d_strip)
        d_planes[...] = jnp.zeros_like(d_planes)

    valid = valid_ref[page]
    both = both_ref[...]
    both_t = both_t_ref[...]
    count = both.shape[0]
    key_side = jnp.concatenate([both, k_ref[...]], axis=1)
    values = v_ref[...]
    keys_t = k_ref[...].T
    d_mixed_t = dm_ref[...].T
    weighted = d_mixed_t.astype(F32) * mixed_ref[...].T.astype(F32)
    rows = lax.broadcasted_iota(jnp.int32, d_mixed_t.shape, 0)
    d_keys = d_values = None
    d_queries = []
    for head in range(2):
        masked_q = head_lanes(q_ref[...], head)
        query_side = jnp.concatenate([left_side(both, planes, head), masked_q], axis=1)
        blocks = scores_t(key_side, query_side, strip, head, valid)
        log_total = log_ref[0, 0, head : head + 1, :]
        inner = jnp.sum(weighted[HD * head : HD * head + HD], axis=0, keepdims=True)
        d_mixed_head = jnp.where(
            (rows >= HD) == (head == 1), d_mixed_t, jnp.zeros_like(d_mixed_t)
        )
        d_probs = dot(values, d_mixed_head)
        probs_low, scores_low = [], []
        for index, block in enumerate(blocks):
            probs = jnp.exp(block - log_total)
            d_scores = probs * (d_probs[128 * index : 128 * index + 128] - inner)
            start = 384 - 128 * index
            d_strip[head, :, start : start + count] += d_scores
            probs_low.append(probs.astype(BF))
            scores_low.append(d_scores.astype(BF))
        probs_low = jnp.concatenate(probs_low, axis=0)
        scores_low = jnp.concatenate(scores_low, axis=0)
        part_v = dot(probs_low, head_lanes(dm_ref[...], head))
        mixed_k = dot(scores_low, jnp.concatenate([both, masked_q], axis=1))
        part_k = mixed_k[:, 2 * NB :]
        d_values = part_v if d_values is None else d_values + part_v
        d_keys = part_k if d_keys is None else d_keys + part_k
        d_queries.append(dot(keys_t[HD * head : HD * head + HD], scores_low))
        for k in range(2):
            side = mixed_k[:, NB * k : NB * k + NB].astype(BF)
            d_planes[head, k] += dot(both_t[NB * k : NB * k + NB], side)
    grad_ref[0] = (jnp.concatenate(d_queries, axis=0).T * HD ** (-0.5)).astype(BF)
    grad_ref[1] = d_keys.astype(BF)
    grad_ref[2] = d_values.astype(BF)

    @pl.when(page == pl.num_programs(1) - 1)
    def _():
        blank = jnp.zeros((128, 128), F32)
        for head in range(2):
            middle = jnp.concatenate([d_strip[head, :, 256:640], blank], axis=1)
            sums_ref[head, 0:1, :] = fold_diagonals(middle)
            for k in range(2):
                padded = jnp.concatenate([d_planes[head, k], blank], axis=1)
                sums_ref[head, 1:2, 256 * k : 256 * k + 256] = fold_diagonals(padded)
            sums_ref[head, 2:3, :256] = jnp.sum(d_strip[head, :, :256], axis=0, keepdims=True)
            sums_ref[head, 2:3, 256:] = jnp.sum(d_strip[head, :, 640:], axis=0, keepdims=True)


def attend_back_call(valid, projected, d_mixed, mixed, log_total, both, base, count):
    pages = projected.shape[1] // count
    pairs = H // 2
    both_t = both.T

    def part(index):
        return pl.BlockSpec((None, count, 128), lambda pair, page: (index, page, pair))

    wide = pl.BlockSpec((count, 128), lambda pair, page: (page, pair))
    return pl.pallas_call(
        attend_back_kernel,
        grid=(pairs, pages),
        in_specs=[
            pl.BlockSpec(memory_space=pltpu.SMEM),
            part(0),
            part(1),
            part(2),
            wide,
            wide,
            pl.BlockSpec((1, 1, 8, count), lambda pair, page: (page, pair, 0, 0)),
            pl.BlockSpec((count, 2 * NB), lambda pair, page: (page, 0)),
            pl.BlockSpec((2 * NB, count), lambda pair, page: (0, page)),
            pl.BlockSpec((2, 8, 512), lambda pair, page: (pair, 0, 0)),
        ],
        out_specs=[
            pl.BlockSpec((3, count, 128), lambda pair, page: (0, page, pair)),
            pl.BlockSpec((2, 8, 512), lambda pair, page: (pair, 0, 0)),
        ],
        out_shape=[
            jax.ShapeDtypeStruct(projected.shape, BF),
            jax.ShapeDtypeStruct((H, 8, 512), F32),
        ],
        scratch_shapes=[
            pltpu.VMEM((2, 128, count + 384), F32),
            pltpu.VMEM((2, 2, NB, NB), BF),
            pltpu.VMEM((2, 128, count + 384), F32),
            pltpu.VMEM((2, 2, NB, NB), F32),
        ],
        compiler_params=params_of(),
        name="attend_back",
        cost_estimate=cost(41),
    )(valid, projected, projected, projected, d_mixed, mixed, log_total, both, both_t, base)


def gelu_parts(before):
    size = jnp.abs(before) * (0.5**0.5)
    denominator = 1.0 + 0.3275911 * size
    t = pl.reciprocal(denominator, approx=True)
    t = t * (2.0 - denominator * t)
    bell = jnp.exp(-0.5 * before * before)
    tail = t * (
        0.5 * 0.254829592
        + t
        * (
            0.5 * -0.284496736
            + t * (0.5 * 1.421413741 + t * (0.5 * -1.453152027 + t * (0.5 * 1.061405429)))
        )
    )
    tail = tail * bell
    below = jnp.where(before >= 0.0, 1.0 - tail, tail)
    return before * below, below + before * (bell * 0.3989422804014327)


def normalize(rows):
    center = rows - jnp.mean(rows, axis=-1, keepdims=True)
    spread = jnp.mean(center * center, axis=-1, keepdims=True)
    scale = lax.rsqrt(spread + EPSILON)
    return center * scale, scale


def normalize_back(grad, hat, scale, gain):
    scaled = grad * gain
    first = jnp.mean(scaled, axis=-1, keepdims=True)
    second = jnp.mean(scaled * hat, axis=-1, keepdims=True)
    return scale * (scaled - first - hat * second)


def add_sums(ref, index, value, fresh):
    total = jnp.sum(value, axis=0, keepdims=True)
    ref[index : index + 1] = jnp.where(fresh, total, ref[index : index + 1] + total)


def whole_spec(shape):
    return pl.BlockSpec(shape, lambda *_: (0,) * len(shape))


def smem():
    return pl.BlockSpec(memory_space=pltpu.SMEM)


def weight_specs(stacks, rows, first):
    nz, _, width = stacks[0].shape
    return [pl.BlockSpec((nz, rows, width), lambda i: (0, first + i, 0))] * len(stacks)


def project_kernel(count, one_ref, two_ref, raw_ref, both_ref, space_ref, coef_ref, *refs):
    stacks, (out_ref, wide_ref, normed_ref, inputs_ref, joint_ref, plain_ref) = refs[:count], refs[count:]
    step = pl.program_id(0)

    @pl.when(step == 0)
    def _():
        normed = (raw_ref[...].astype(F32) - coef_ref[0:1]) * coef_ref[1:2]
        inputs = normed * coef_ref[2:3] + coef_ref[3:4]
        normed_ref[...] = normed
        inputs_ref[...] = inputs
        plain_ref[...] = inputs.astype(BF)
        joint_ref[...] = (inputs + dot(both_ref[...], space_ref[...])).astype(BF)

    if two_ref.shape[0] == 1:
        place(one_ref, stacks, wide_ref.at[0])
    else:
        place(one_ref, stacks[: count // 2], wide_ref.at[0])
        place(two_ref, stacks[count // 2 :], wide_ref.at[0], wide_ref.shape[3] // 2)
    width = raw_ref.shape[1]
    weight = wide_ref[0].reshape(width, width)
    rows = jnp.where(step == 2, plain_ref[...], joint_ref[...])
    factor = jnp.where(step == 0, HD ** (-0.5), 1.0)
    out_ref[0] = (dot(rows, weight) * factor).astype(BF)


def project_call(sources, stacks, rows, raw, both, space, coefs):
    tokens, width = raw.shape
    chips = sources[0].shape[0]
    whole = whole_spec((tokens, width))
    return pl.pallas_call(
        functools.partial(project_kernel, len(stacks)),
        grid=(3,),
        in_specs=[smem(), smem(), whole, whole_spec(both.shape), whole_spec(space.shape)]
        + [whole_spec(coefs.shape)]
        + weight_specs(stacks, rows, 0),
        out_specs=[
            pl.BlockSpec((1, tokens, width), lambda i: (i, 0, 0)),
            pl.BlockSpec((1, chips, rows, width), lambda i: (i, 0, 0, 0)),
            whole,
            whole,
            whole,
            whole,
        ],
        out_shape=[
            jax.ShapeDtypeStruct((3, tokens, width), BF),
            jax.ShapeDtypeStruct((3, chips, rows, width), BF),
            jax.ShapeDtypeStruct((tokens, width), F32),
            jax.ShapeDtypeStruct((tokens, width), F32),
            jax.ShapeDtypeStruct((tokens, width), BF),
            jax.ShapeDtypeStruct((tokens, width), BF),
        ],
        compiler_params=params_of(),
        name="project",
        cost_estimate=cost(12),
    )(*sources, raw, both, space, coefs, *stacks)


def output_kernel(count, where_ref, mixed_ref, keep_ref, *refs):
    stacks, (att_ref, low_ref, wide_ref) = refs[:count], refs[count:]
    place(where_ref, stacks, wide_ref)
    width = mixed_ref.shape[1]
    att = dot(mixed_ref[...], wide_ref[...].reshape(width, width)) * keep_ref[...]
    att_ref[...] = att
    low_ref[...] = att.astype(BF)


def output_call(where, stacks, rows, mixed, keep):
    tokens, width = mixed.shape
    nz = stacks[0].shape[0]
    chips = len(stacks) * nz
    return pl.pallas_call(
        functools.partial(output_kernel, len(stacks)),
        grid=(1,),
        in_specs=[smem(), whole_spec((tokens, width)), whole_spec((tokens, 1))]
        + weight_specs(stacks, rows, 8),
        out_specs=[
            whole_spec((tokens, width)),
            whole_spec((tokens, width)),
            whole_spec((chips, rows, width)),
        ],
        out_shape=[
            jax.ShapeDtypeStruct((tokens, width), F32),
            jax.ShapeDtypeStruct((tokens, width), BF),
            jax.ShapeDtypeStruct((chips, rows, width), BF),
        ],
        compiler_params=params_of(),
        name="output",
        cost_estimate=cost(5),
    )(where, mixed, keep, *stacks)


def feed_kernel(count, where_ref, inputs_ref, own_ref, other_ref, vec_ref, bias_ref, *refs):
    stacks = refs[:count]
    u_ref, low_ref, hat_ref, scale_ref, active_ref, slope_ref, wide_ref = refs[count:]
    half = inputs_ref.shape[0] // 2

    @pl.when(pl.program_id(0) == 0)
    def _():
        for page in range(2):
            here = pl.ds(half * page, half)
            there = pl.ds(half * (1 - page), half)
            rows = inputs_ref[here, :] + own_ref[here, :] + other_ref[there, :].astype(F32)
            hat, scale = normalize(rows)
            u = hat * vec_ref[2:3] + vec_ref[3:4]
            u_ref[here, :] = u
            low_ref[here, :] = u.astype(BF)
            hat_ref[here, :] = hat
            scale_ref[here, :] = scale

    place(where_ref, stacks, wide_ref.at[0])
    width = inputs_ref.shape[1]
    weight = wide_ref[0].reshape(width, width)
    before = dot(low_ref[...], weight) + bias_ref[...]
    active, slope = gelu_parts(before)
    active_ref[...] = active.astype(BF)
    slope_ref[...] = slope.astype(BF)


def feed_call(where, stacks, rows, inputs, own, other, vecs, bias):
    tokens, width = inputs.shape
    hidden = bias.shape[1]
    nz = stacks[0].shape[0]
    chips = len(stacks) * nz
    whole = whole_spec((tokens, width))
    block = pl.BlockSpec((tokens, width), lambda i: (0, i))
    return pl.pallas_call(
        functools.partial(feed_kernel, len(stacks)),
        grid=(hidden // width,),
        in_specs=[smem(), whole, whole, whole, whole_spec(vecs.shape)]
        + [pl.BlockSpec((1, width), lambda i: (0, i))]
        + weight_specs(stacks, rows, 4),
        out_specs=[
            whole,
            whole,
            whole,
            whole_spec((tokens, 1)),
            block,
            block,
            pl.BlockSpec((1, chips, rows, width), lambda i: (i, 0, 0, 0)),
        ],
        out_shape=[
            jax.ShapeDtypeStruct((tokens, width), F32),
            jax.ShapeDtypeStruct((tokens, width), BF),
            jax.ShapeDtypeStruct((tokens, width), F32),
            jax.ShapeDtypeStruct((tokens, 1), F32),
            jax.ShapeDtypeStruct((tokens, hidden), BF),
            jax.ShapeDtypeStruct((tokens, hidden), BF),
            jax.ShapeDtypeStruct((hidden // width, chips, rows, width), BF),
        ],
        compiler_params=params_of(),
        name="feed",
        cost_estimate=cost(24),
    )(where, inputs, own, other, vecs, bias, *stacks)


def close_kernel(count, where_ref, active_ref, u_ref, cot_ref, keep_ref, vec_ref, *refs):
    stacks = refs[:count]
    out_ref, dy_ref, low_ref, sums_ref, wide_ref = refs[count:]
    step = pl.program_id(0)

    @pl.when(step == 0)
    def _():
        place(where_ref, stacks, wide_ref)

    weight = wide_ref[...].reshape(-1, u_ref.shape[1])
    rows = u_ref[...] + (dot(active_ref[...], weight) + vec_ref[6:7])
    hat, scale = normalize(rows)
    gain = vec_ref[4:5]
    keep = keep_ref[...]
    out_ref[...] = ((hat * gain + vec_ref[5:6]) * keep).astype(BF)
    cot = cot_ref[...].astype(F32) * keep
    dy = normalize_back(cot, hat, scale, gain)
    low = dy.astype(BF)
    dy_ref[...] = dy
    low_ref[...] = low
    add_sums(sums_ref, 0, cot * hat, step == 0)
    add_sums(sums_ref, 1, cot, step == 0)
    add_sums(sums_ref, 2, low.astype(F32), step == 0)


def close_call(where, stacks, rows, active, u, cot, keep, vecs):
    tokens, width = u.shape
    hidden = active.shape[1]
    nz = stacks[0].shape[0]
    groups = 4
    chips = len(stacks) * nz
    steps = 4
    block = pl.BlockSpec((tokens // steps, width), lambda i: (i, 0))
    return pl.pallas_call(
        functools.partial(close_kernel, len(stacks)),
        grid=(steps,),
        in_specs=[
            smem(),
            pl.BlockSpec((tokens // steps, hidden), lambda i: (i, 0)),
            block,
            block,
            pl.BlockSpec((tokens // steps, 1), lambda i: (i, 0)),
            whole_spec(vecs.shape),
        ]
        + [whole_spec((nz, groups * rows, width))] * len(stacks),
        out_specs=[
            block,
            block,
            block,
            whole_spec((8, width)),
            whole_spec((chips, groups * rows, width)),
        ],
        out_shape=[
            jax.ShapeDtypeStruct((tokens, width), BF),
            jax.ShapeDtypeStruct((tokens, width), F32),
            jax.ShapeDtypeStruct((tokens, width), BF),
            jax.ShapeDtypeStruct((8, width), F32),
            jax.ShapeDtypeStruct((chips, groups * rows, width), BF),
        ],
        compiler_params=params_of(),
        name="close",
        cost_estimate=cost(13),
    )(where, active, u, cot, keep, vecs, *stacks)


def store_slots(slots_ref, out_ref, total, first=0):
    rows = out_ref.shape[1]
    for index in range(total.shape[0] // rows):
        part = total[index * rows : index * rows + rows].astype(BF)
        out_ref[slots_ref[first + index]] = part


def second_kernel(slots_ref, active_ref, low_ref, out_ref):
    total = dot(active_ref[...].T, low_ref[...])
    count = total.shape[0] // out_ref.shape[1]
    store_slots(slots_ref, out_ref, total, pl.program_id(0) * count)


def second_call(slots, active, low, chips):
    tokens, width = low.shape
    hidden = active.shape[1]
    return pl.pallas_call(
        second_kernel,
        grid=(hidden // width,),
        in_specs=[
            smem(),
            pl.BlockSpec((tokens, width), lambda i: (0, i)),
            whole_spec((tokens, width)),
        ],
        out_specs=whole_spec((chips, hidden // chips, width)),
        out_shape=jax.ShapeDtypeStruct((chips, hidden // chips, width), BF),
        compiler_params=params_of(),
        name="second",
        cost_estimate=cost(10),
    )(slots, active, low)


def feed_back_kernel(
    slots_ref, rows_ref, low_ref, second_ref, first_ref, slope_ref, dy_ref, hat_ref, scale_ref, vec_ref,
    dpre_ref, dlow_ref, dfirst_ref, dbias_ref, sums_ref, rows_t, total_ref,
):
    step = pl.program_id(0)

    @pl.when(step == 0)
    def _():
        rows_t[...] = rows_ref[...].T
        total_ref[...] = dy_ref[...]

    d_active = dot_nt(low_ref[...], second_ref[...])
    d_before = (slope_ref[...].astype(F32) * d_active).astype(BF)
    dbias_ref[...] = jnp.sum(d_before.astype(F32), axis=0, keepdims=True)
    total_ref[...] += dot_nt(d_before, first_ref[0])
    store_slots(slots_ref, dfirst_ref, dot(rows_t[...], d_before))

    @pl.when(step == pl.num_programs(0) - 1)
    def _():
        grad = total_ref[...]
        hat = hat_ref[...]
        d_pre = normalize_back(grad, hat, scale_ref[...], vec_ref[2:3])
        dpre_ref[...] = d_pre
        dlow_ref[...] = d_pre.astype(BF)
        add_sums(sums_ref, 0, grad * hat, True)
        add_sums(sums_ref, 1, grad, True)


def feed_back_call(slots, rows, low, second, first, slope, dy, hat, scale, vecs, chips):
    tokens, width = rows.shape
    hidden = second.shape[0]
    piece = width // chips
    whole = whole_spec((tokens, width))
    return pl.pallas_call(
        feed_back_kernel,
        grid=(hidden // width,),
        in_specs=[
            smem(),
            whole,
            whole,
            pl.BlockSpec((width, width), lambda i: (i, 0)),
            pl.BlockSpec((1, width, width), lambda i: (i, 0, 0)),
            pl.BlockSpec((tokens, width), lambda i: (0, i)),
            whole,
            whole,
            whole_spec((tokens, 1)),
            whole_spec(vecs.shape),
        ],
        out_specs=[
            whole,
            whole,
            pl.BlockSpec((chips, piece, width), lambda i: (0, 0, i)),
            pl.BlockSpec((1, width), lambda i: (0, i)),
            whole_spec((8, width)),
        ],
        out_shape=[
            jax.ShapeDtypeStruct((tokens, width), F32),
            jax.ShapeDtypeStruct((tokens, width), BF),
            jax.ShapeDtypeStruct((chips, piece, hidden), BF),
            jax.ShapeDtypeStruct((1, hidden), F32),
            jax.ShapeDtypeStruct((8, width), F32),
        ],
        scratch_shapes=[pltpu.VMEM((width, tokens), BF), pltpu.VMEM((tokens, width), F32)],
        compiler_params=params_of(),
        name="feed_back",
        cost_estimate=cost(26),
    )(slots, rows, low, second, first, slope, dy, hat, scale, vecs)


def middle_kernel(slots_ref, own_ref, other_ref, keep_ref, mixed_ref, weight_ref, dmixed_ref, dw_ref, low_ref):
    half = own_ref.shape[0] // 2
    for page in range(2):
        here = pl.ds(half * page, half)
        there = pl.ds(half * (1 - page), half)
        merged = (own_ref[here, :] + other_ref[there, :].astype(F32)) * keep_ref[here, :]
        low_ref[here, :] = merged.astype(BF)
    low = low_ref[...]
    dmixed_ref[...] = dot_nt(low, weight_ref[...]).astype(BF)
    store_slots(slots_ref, dw_ref, dot(mixed_ref[...].T, low))


def middle_call(slots, own, other, keep, mixed, weight, chips):
    tokens, width = own.shape
    whole = whole_spec((tokens, width))
    piece = (chips, width // chips, width)
    return pl.pallas_call(
        middle_kernel,
        grid=(1,),
        in_specs=[smem(), whole, whole, whole_spec((tokens, 1)), whole, whole_spec((width, width))],
        out_specs=[whole, whole_spec(piece)],
        out_shape=[jax.ShapeDtypeStruct((tokens, width), BF), jax.ShapeDtypeStruct(piece, BF)],
        scratch_shapes=[pltpu.VMEM((tokens, width), BF)],
        compiler_params=params_of(),
        name="middle",
        cost_estimate=cost(8),
    )(slots, own, other, keep, mixed, weight)


def grads_kernel(
    slots_ref, joint_ref, plain_ref, grad_ref, weight_ref, dpre_ref, normed_ref, both_ref, coef_ref,
    dw_ref, rows_ref, sums_ref, left_t, total_ref,
):
    step = pl.program_id(0)
    space_size = both_ref.shape[1]

    @pl.when(step == 0)
    def _():
        left_t[...] = joint_ref[...].T

    @pl.when(step == 2)
    def _():
        left_t[...] = plain_ref[...].T

    grad = grad_ref[0]
    chips = dw_ref.shape[0]
    piece = left_t.shape[0] // chips
    near = space_size // (2 * chips)

    total = dot(left_t[...], grad)

    def store(index):
        for chip in range(chips):
            low = total[chip * piece : chip * piece + piece].astype(BF)
            dw_ref[slots_ref[chip], index * piece : index * piece + piece] = low

    for index in range(3):
        pl.when(step == index)(functools.partial(store, index))
    part = dot_nt(grad, weight_ref[0])

    @pl.when(step == 0)
    def _():
        total_ref[...] = part

    @pl.when(step == 1)
    def _():
        joint = total_ref[...] + part
        total_ref[...] = joint + dpre_ref[...]
        space = dot(both_ref[...].T, joint.astype(BF)).astype(BF)
        for chip in range(chips):
            for k in range(2):
                begin = k * space_size // 2 + chip * near
                start = 3 * piece + k * near
                dw_ref[slots_ref[chip], start : start + near] = space[begin : begin + near]

    @pl.when(step == 2)
    def _():
        dx = total_ref[...] + part
        rows_ref[...] = dx * coef_ref[2:3] * coef_ref[1:2]
        add_sums(sums_ref, 0, dx * normed_ref[...], True)
        add_sums(sums_ref, 1, dx, True)


def grads_call(slots, joint, plain, grad, weight, d_pre, normed, both, coefs, chips):
    tokens, width = joint.shape
    whole = whole_spec((tokens, width))
    height = 3 * (width // chips) + both.shape[1] // chips
    return pl.pallas_call(
        grads_kernel,
        grid=(3,),
        in_specs=[
            smem(),
            whole,
            whole,
            pl.BlockSpec((1, tokens, width), lambda i: (i, 0, 0)),
            pl.BlockSpec((1, width, width), lambda i: (i, 0, 0)),
            whole,
            whole,
            whole_spec(both.shape),
            whole_spec(coefs.shape),
        ],
        out_specs=[
            whole_spec((chips, height, width)),
            whole,
            whole_spec((8, width)),
        ],
        out_shape=[
            jax.ShapeDtypeStruct((chips, height, width), BF),
            jax.ShapeDtypeStruct((tokens, width), F32),
            jax.ShapeDtypeStruct((8, width), F32),
        ],
        scratch_shapes=[pltpu.VMEM((width, tokens), BF), pltpu.VMEM((tokens, width), F32)],
        compiler_params=params_of(),
        name="grads",
        cost_estimate=cost(12),
    )(slots, joint, plain, grad, weight, d_pre, normed, both, coefs)


def adam(weight, grad, first, second, rate, decay):
    first_new = BETA_ONE * first + (1 - BETA_ONE) * grad
    second_new = BETA_TWO * second + (1 - BETA_TWO) * grad * grad
    ratio = (
        first_new / (1 - BETA_ONE**STEP) / (jnp.sqrt(second_new / (1 - BETA_TWO**STEP)) + ADAM_EPS)
    )
    return (first_new, second_new, weight - rate * (ratio + decay * weight))


def body(
    visual, text, lengths, text_boxes, cot_visual, cot_text,
    attn_w, ffn_in, ffn_out, bias_in, vectors, pos_tables, spatial,
    attn_mom, attn_sec, in_mom, in_sec, out_mom, out_sec, bias_mom, bias_sec,
    vec_mom, vec_sec, pos_mom, pos_sec, spatial_mom, spatial_sec,
):
    core = lax.axis_index("c")
    seen = core == 0
    nz, ny, nx = (lax.axis_size(a) for a in CHIP)
    chips = nz * ny * nx
    devices = 2 * chips
    _, count, width = visual.shape
    tokens = 2 * count

    def mine_of(first, second):
        return jnp.where(seen, first, second)

    def trade(first, second):
        return mine_of(first, second), swap(mine_of(second, first))

    def by_core(own, other):
        return jnp.where(seen, jnp.stack([own, other]), jnp.stack([other, own]))

    attn_low = attn_w.astype(BF)
    in_low = ffn_in.astype(BF)
    out_low = ffn_out.astype(BF)
    attn_own, attn_other = trade(attn_low[0], attn_low[1])
    in_own, in_other = trade(in_low[0], in_low[1])
    out_own, out_other = trade(out_low[0], out_low[1])
    rows_a = attn_w.shape[2]
    rows_o = ffn_out.shape[1]
    hidden = ffn_in.shape[2]
    attn_piece = jnp.where(
        seen,
        jnp.concatenate([attn_own, attn_other], axis=1),
        jnp.concatenate([attn_other, attn_own], axis=1),
    )
    in_piece = by_core(in_own, in_other).reshape(2 * rows_a, hidden)
    out_piece = by_core(out_own, out_other).reshape(2 * rows_o, width)
    in_cut = in_piece.reshape(2 * rows_a, -1, width).transpose(1, 0, 2)
    out_cut = out_piece.reshape(-1, 2 * rows_a, width)

    raw_own = visual[0].astype(F32)
    sums = jnp.stack([jnp.sum(raw_own, axis=0), jnp.sum(raw_own * raw_own, axis=0)])
    vec_rows = [
        jnp.stack([vectors[0], vectors[1]] + [vectors[k + 2 * s] for k in (2, 3, 6, 7)] + [vectors[10 + s]])
        for s in range(2)
    ]

    def packed(s):
        def row(values):
            flat = values.reshape(1, -1)
            return jnp.pad(flat, ((0, 0), (0, -flat.shape[1] % width))).reshape(-1, width)

        return jnp.concatenate(
            [row(pos_tables[s].astype(BF)), row(jnp.concatenate(
                [part.reshape(1, -1) for part in split_three(vec_rows[s]) + split_three(bias_in[s])], axis=1
            ))], axis=0
        )

    pack_zero, pack_one = packed(0), packed(1)
    small_rows = pack_zero.shape[0]
    space = spatial.astype(BF).reshape(-1, width)
    space_rows = space.shape[0]
    pack_own, pack_other = trade(pack_zero, pack_one)
    space_other, sums_other = swap((space, sums))
    pack_both = by_core(pack_own, pack_other).reshape(2 * small_rows, width)
    space_both = by_core(space, space_other).reshape(2 * space_rows, width)
    small = jnp.concatenate(
        [space_both, pack_both, jnp.concatenate(split_three(sums + sums_other), axis=0)], axis=0
    )
    pad = -(small.shape[0] + 6 * rows_a) % 16
    first = jnp.concatenate(
        [attn_piece[:3].reshape(6 * rows_a, width), jnp.pad(small, ((0, pad), (0, 0)))], axis=0
    )
    rest = jnp.concatenate([out_cut, in_cut, attn_piece[3:]], axis=0).reshape(-1, width)
    wide_rest = lax.all_gather(rest, CHIP)
    halves, sources = relay(first)
    weight_rows = 6 * rows_a
    gathered = jnp.concatenate(
        [in_order(halves[k], sources[k], weight_rows, first.shape[0]) for k in range(2)], axis=2
    )
    wide_spatial = gathered[:, : 2 * space_rows].reshape(chips, 2, 2, -1, width)
    wide_spatial = wide_spatial.transpose(2, 0, 1, 3, 4).reshape(2 * NB, width)
    packs = gathered[:, 2 * space_rows : 2 * space_rows + 2 * small_rows]
    packs = packs.reshape(devices, small_rows, width)
    pos_size = pos_tables[0].size
    pos_lines = -(-pos_size // width)
    tables = packs[:, :pos_lines].reshape(devices, -1)[:, :pos_size]
    tables = tables.reshape(devices, 3, H, -1).transpose(1, 2, 0, 3).reshape(3, H, NR).astype(F32)
    params = packs[:, pos_lines:].reshape(devices, -1)
    vec_size = vec_rows[0].size
    bias_size = bias_in[0].size
    wide_vec = join_three([params[:, vec_size * k : vec_size * (k + 1)] for k in range(3)])
    wide_vec = wide_vec.reshape(devices, 7, -1).transpose(1, 0, 2).reshape(7, width)
    wide_bias = join_three(
        [params[:, 3 * vec_size + bias_size * k : 3 * vec_size + bias_size * (k + 1)] for k in range(3)]
    ).reshape(1, hidden)
    parts = gathered[:, 2 * space_rows + 2 * small_rows :]
    sums = jnp.sum(join_three([parts[:, 2 * k : 2 * k + 2] for k in range(3)]), axis=0)

    data_own, data_other = trade(visual[0], text[0])
    cot_own, cot_other = trade(cot_visual[0], cot_text[0])
    length_other, boxes_other = swap((lengths, text_boxes))
    total = count * devices
    mean = sums[0] / total
    variance = sums[1] / total - mean * mean
    inverse = lax.rsqrt(variance + EPSILON)
    stream_mean = jnp.where(seen, mean, 0.0)
    stream_inverse = jnp.where(seen, inverse, 1.0)
    stream_gain = jnp.where(seen, wide_vec[0], 1.0)
    stream_shift = jnp.where(seen, wide_vec[1], 0.0)
    raw = jnp.concatenate([data_own, data_other], axis=0)
    coefs = jnp.stack([stream_mean, stream_inverse, stream_gain, stream_shift])
    coefs = jnp.pad(coefs, ((0, 4), (0, 0)))
    position = jnp.arange(count, dtype=jnp.int32)
    lengths_both = jnp.concatenate([lengths, length_other])
    keep_pages = (position[None, :] < lengths_both[:, None]).astype(F32).reshape(tokens, 1)
    keep_rows = jnp.where(seen, 1.0, keep_pages)
    valid = jnp.where(seen, count, lengths_both).astype(jnp.int32)
    grid_x = position % VCOLS * (NB // VCOLS) + NB // VCOLS // 2
    grid_y = position // VCOLS * (NB // VROWS) + NB // VROWS // 2
    boxes = jnp.concatenate([text_boxes, boxes_other], axis=0)
    boxes = jnp.where(seen, jnp.stack([grid_x, grid_y])[None], boxes)
    both = jnp.concatenate(
        [
            (boxes[:, k, :].reshape(tokens, 1) == jnp.arange(NB)[None, :]).astype(BF)
            for k in range(2)
        ],
        axis=1,
    )
    base = base_rows(tables)

    rows_one = rows_rest = 2 * rows_a
    where_rest = jnp.arange(chips, dtype=jnp.int32)
    if rows_one % 16:
        whole_one = [in_order(halves[k], sources[k], 0, weight_rows) for k in range(2)]
        whole_one, rows_one = grouped(jnp.concatenate(whole_one, axis=2), rows_one, 3)
        wide_one, sources = [whole_one], [jnp.zeros((1,), jnp.int32)] * 2
        wide_rest, rows_rest = grouped(wide_rest, rows_rest, 5, 2 * rows_o)
        where_rest = jnp.zeros((1,), jnp.int32)
    else:
        wide_one = halves[0] + halves[1]
    wide_rest = [wide_rest]
    vecs = jnp.pad(wide_vec, ((0, 1), (0, 0)))

    projected, weight_qkv, normed, inputs, joint, plain = project_call(
        sources, wide_one, rows_one, raw, both, wide_spatial, coefs
    )
    mixed, log_total = attend_call(valid, projected, both, base, count)
    att, att_low, weight_out = output_call(where_rest, wide_rest, rows_rest, mixed, keep_rows)
    att_other = swap(att_low)

    u, u_low, hat_one, scale_one, active, slope, weight_in = feed_call(
        where_rest, wide_rest, rows_rest, inputs, att, att_other, vecs, wide_bias
    )
    cot = jnp.concatenate([cot_own, cot_other], axis=0)
    out, dy, dff, close_sums, weight_second = close_call(
        where_rest, wide_rest, rows_rest, active, u, cot, keep_rows, vecs
    )

    slots = slot_table()
    d_out = second_call(jnp.arange(chips, dtype=jnp.int32), active, dff, chips)
    d_pre, d_pre_low, d_in, d_bias, pre_sums = feed_back_call(
        slots, u_low, after(dff, d_out), weight_second.reshape(hidden, width),
        weight_in.reshape(-1, width, width), slope, dy, hat_one, scale_one, vecs, chips,
    )
    d_pre_other = swap(d_pre_low)

    d_mixed, d_last = middle_call(
        slots, d_pre, d_pre_other, keep_rows, mixed, weight_out.reshape(width, width), chips
    )
    d_projected, table_parts = attend_back_call(
        valid, projected, d_mixed, mixed, log_total, both, base, count
    )
    column_in = scatter_plane(d_in, d_projected)
    column_last = scatter_plane(d_last, d_projected)
    d_first, grad_rows, norm_sums = grads_call(
        slots, joint, plain, after(d_projected, (column_in, column_last)), weight_qkv.reshape(3, width, width), d_pre, normed,
        both, coefs, chips,
    )

    sum_out = lax.psum_scatter(d_out, CHIP).astype(F32)
    sum_in = scatter_line(column_in)
    sum_last = scatter_line(column_last)
    sum_first = scatter_line(scatter_plane(d_first))
    sum_attn = jnp.concatenate(
        [sum_first[: 6 * rows_a].reshape(3, 2 * rows_a, width), sum_last[None]], axis=0
    )

    def own_rows(value, axis):
        first, second = jnp.split(value, 2, axis=axis)
        return trade(first, second)

    def by_stream(own, other):
        return jnp.where(seen, jnp.stack([own, other]), jnp.stack([other, own]))

    own_space, other_space = own_rows(sum_first[6 * rows_a :].reshape(2, 2, -1, width), 1)
    grad_spatial = (own_space + other_space).reshape(spatial.shape)
    is_norm = jnp.where(seen, 1.0, 0.0)
    little = jnp.concatenate(
        [
            norm_sums[:2] * is_norm, pre_sums[:2], close_sums[:3], jnp.zeros((1, width), F32),
            d_bias.reshape(-1, width), table_sums(table_parts).reshape(-1, width),
        ],
        axis=0,
    ).astype(BF)
    little = jnp.pad(little, ((0, -little.shape[0] % 8), (0, 0)))
    little = functools.reduce(jnp.add, [part.astype(F32) for part in around(little)]).astype(BF)
    little = functools.reduce(jnp.add, [part.astype(F32) for part in line_of(little)])
    little = by_stream(little, swap(little))
    member = 2 * chip_of(0, 0, 0) + core
    vec_sum = lax.dynamic_slice_in_dim(little[:, :7], member * vectors.shape[1], vectors.shape[1], 2)
    grad_vec = jnp.stack(
        [vec_sum[0, 0], vec_sum[0, 1]]
        + [vec_sum[s, k + m] for k in (2, 4) for s in range(2) for m in range(2)]
        + [vec_sum[0, 6], vec_sum[1, 6]]
    )
    bias_lines = hidden // width
    bias_sum = little[:, 8 : 8 + bias_lines].reshape(2, hidden)
    grad_bias = lax.dynamic_slice_in_dim(bias_sum, member * bias_in.shape[1], bias_in.shape[1], 1)
    pos_sum = little[:, 8 + bias_lines : 8 + bias_lines + 3 * H * NR // width].reshape(2, 3, H, NR)
    grad_pos = lax.dynamic_slice_in_dim(pos_sum, member * pos_tables.shape[3], pos_tables.shape[3], 3)

    squares = jnp.sum(sum_out * sum_out) + jnp.sum(sum_in * sum_in) + jnp.sum(sum_attn * sum_attn)
    for grad in (grad_spatial, grad_pos, grad_vec, grad_bias):
        squares = squares + jnp.sum(grad * grad)
    tile = jnp.full((8, 128), squares, F32)
    tile = tile + swap(tile)
    tile = functools.reduce(jnp.add, around(tile))
    norm = functools.reduce(jnp.add, line_of(tile))
    grad_norm = jnp.sqrt(norm[0, 0])
    factor = CLIP / jnp.maximum(grad_norm, CLIP)

    grad_attn = by_stream(*own_rows(sum_attn, 1))
    grad_in = by_stream(*own_rows(sum_in, 0))
    grad_out = by_stream(*own_rows(sum_out, 0))

    out_own, out_other = out[:count], swap(out[count:])
    grad_own, grad_other = grad_rows[:count], swap(grad_rows[count:])
    out_visual = mine_of(out_own, out_other)[None]
    out_text = mine_of(out_other, out_own)[None]
    grad_visual = mine_of(grad_own, grad_other)[None]
    grad_text = mine_of(grad_other, grad_own)[None]

    params = (attn_w, ffn_in, ffn_out, bias_in, vectors, pos_tables, spatial)
    grads = (grad_attn, grad_in, grad_out, grad_bias, grad_vec, grad_pos, grad_spatial)
    states = (
        (attn_mom, attn_sec), (in_mom, in_sec), (out_mom, out_sec), (bias_mom, bias_sec),
        (vec_mom, vec_sec), (pos_mom, pos_sec), (spatial_mom, spatial_sec),
    )
    rates = (RATE_ATTN, RATE_FEED, RATE_FEED, RATE_OTHER, RATE_OTHER, RATE_OTHER, RATE_OTHER)
    decays = (DECAY, DECAY, DECAY, 0.0, 0.0, 0.0, DECAY)
    results = [out_visual, out_text, grad_visual, grad_text, grad_norm]
    for index, (weight, grad, state, rate, decay) in enumerate(
        zip(params, grads, states, rates, decays)
    ):
        new = adam(weight, grad * factor, state[0], state[1], rate, decay)
        results.extend(new)
        if index < 3:
            results.append(new[2].astype(BF))
    return tuple(results)


def solution(mesh):
    devices = mesh.devices.reshape(-1)
    chips = devices.size // 2
    deep = 4 if chips % 4 == 0 else 1
    side = int(round((chips // deep) ** 0.5))
    if deep * side * side != chips:
        deep, side = chips, 1
    fine = Mesh(devices.reshape(deep, side, side, 2), AXES)
    every = AXES
    data = P(every, None, None)
    in_specs = (
        data, data, P(every), data, data, data,
        P(None, None, every, None), P(None, every, None), P(None, every, None),
        P(None, every), P(None, every), P(None, None, None, every), P(None, every, None),
        P(None, None, every, None), P(None, None, every, None),
        P(None, every, None), P(None, every, None), P(None, every, None), P(None, every, None),
        P(None, every), P(None, every), P(None, every), P(None, every),
        P(None, None, None, every), P(None, None, None, every),
        P(None, every, None), P(None, every, None),
    )
    weights = P(None, None, every, None)
    rows = P(None, every, None)
    flat = P(None, every)
    last = P(None, None, None, every)
    out_specs = (
        (data, data, data, data, P())
        + (weights,) * 4 + (rows,) * 8 + (flat,) * 6 + (last,) * 3 + (rows,) * 3
    )
    return jax.shard_map(body, mesh=fine, in_specs=in_specs, out_specs=out_specs, check_vma=False)
```

```python
import functools

import jax
import jax.numpy as jnp
import numpy as np
from jax import lax
from jax.experimental import pallas as pl
from jax.experimental.pallas import tpu as pltpu
from jax.sharding import Mesh
from jax.sharding import PartitionSpec as P

H = 12
HD = 64
VROWS = 16
VCOLS = 32
NB = 128
NR = 128
STEP = 10

EPSILON = 1e-05
NEGATIVE = -1000000000.0
CLIP = 1.0
BETA_ONE = 0.9
BETA_TWO = 0.95
ADAM_EPS = 1e-08
DECAY = 0.1
RATE_ATTN = 0.15
RATE_FEED = 0.04
RATE_OTHER = 0.2

BF = jnp.bfloat16
F32 = jnp.float32
AXES = ("z", "y", "x", "c")
CHIP = ("z", "y", "x")
VMEM_LIMIT = 56 * 1024 * 1024
NT = (((1,), (1,)), ((), ()))


def cost(microseconds):
    return pl.CostEstimate(
        flops=int(microseconds * 1.1e9), bytes_accessed=int(microseconds * 3.5e6), transcendentals=0
    )


def params_of():
    return pltpu.CompilerParams(vmem_limit_bytes=VMEM_LIMIT)


def held(others):
    return [pl.BlockSpec(memory_space=pl.ANY)] * len(others)


def waiting(kernel, count, others):
    def run(*refs):
        kernel(*refs[:count], *refs[count + others :])

    return run


def dot(left, right):
    return jnp.dot(left, right, preferred_element_type=F32)


def dot_nt(left, right):
    return lax.dot_general(left, right, NT, preferred_element_type=F32)


def swap(value):
    return lax.ppermute(value, "c", [(0, 1), (1, 0)])


def shift(value, axis, step):
    size = lax.axis_size(axis)
    return lax.ppermute(value, axis, [(i, (i + step) % size) for i in range(size)])


def diagonal(value, step_y, step_x):
    ny, nx = lax.axis_size("y"), lax.axis_size("x")
    pairs = [
        (y * nx + x, (y + step_y) % ny * nx + (x + step_x) % nx)
        for y in range(ny)
        for x in range(nx)
    ]
    return lax.ppermute(value, ("y", "x"), pairs)


def after(value, others):
    return lax.optimization_barrier((value, others))[0]


def chip_of(dz, dy, dx):
    nz, ny, nx = (lax.axis_size(a) for a in CHIP)
    z = (lax.axis_index("z") - dz) % nz
    y = (lax.axis_index("y") - dy) % ny
    x = (lax.axis_index("x") - dx) % nx
    return (z * ny + y) * nx + x


def around(value):
    steps = [(y, x) for y in range(lax.axis_size("y")) for x in range(lax.axis_size("x"))]
    return [value] + [diagonal(value, sy, sx) for sy, sx in steps[1:]]


def plane_steps():
    return [(y, x) for y in range(lax.axis_size("y")) for x in range(lax.axis_size("x"))]


def line_of(piece):
    return [piece] + [shift(piece, "z", k) for k in range(1, lax.axis_size("z"))]


def sources_of():
    nz = lax.axis_size("z")
    return jnp.stack([chip_of(k, sy, sx) for sy, sx in plane_steps() for k in range(nz)]).astype(
        jnp.int32
    )


def relay(piece):
    line = jnp.stack(line_of(piece))
    nz = line.shape[0]
    sizes = {"x": lax.axis_size("x"), "y": lax.axis_size("y")}
    half = line.shape[-1] // 2
    halves, sources = [], []
    for part, (first, second) in enumerate((("x", "y"), ("y", "x"))):
        moved = line[..., half * part : half * part + half]
        near = jnp.concatenate([moved] + [shift(moved, first, k) for k in range(1, sizes[first])], axis=0)
        halves.append([near] + [shift(near, second, k) for k in range(1, sizes[second])])
        sources.append(
            [
                chip_of(k, two, one) if first == "x" else chip_of(k, one, two)
                for two in range(sizes[second])
                for one in range(sizes[first])
                for k in range(nz)
            ]
        )
    return halves, [jnp.stack(source).astype(jnp.int32) for source in sources]


def inverse_of(where):
    return jnp.zeros_like(where).at[where].set(jnp.arange(where.shape[0], dtype=jnp.int32))


def in_order(stacks, where, begin, end):
    found = jnp.concatenate([part[:, begin:end] for part in stacks], axis=0)
    return jnp.take(found, inverse_of(where), axis=0)


def grouped(whole, rows, groups, lead=0):
    width = whole.shape[2]
    first = whole[:, :lead].reshape(-1, width)
    others = whole[:, lead:].reshape(-1, groups, rows, width).transpose(1, 0, 2, 3).reshape(-1, width)
    return jnp.concatenate([first, others], axis=0)[None], others.shape[0] // groups


def place(where_ref, refs, target, begin=0):
    count, _, width = refs[0].shape
    for index, ref in enumerate(refs):
        for k in range(count):
            target[where_ref[index * count + k], :, begin : begin + width] = ref[k]


def slot_table(turned=False):
    nz, ny, nx = (lax.axis_size(a) for a in CHIP)
    chips = jnp.arange(nz * ny * nx)
    zr = (chips // (ny * nx) - lax.axis_index("z")) % nz
    yr = (chips // nx % ny - lax.axis_index("y")) % ny
    xr = (chips % nx - lax.axis_index("x")) % nx
    if turned:
        return ((xr * ny + yr) * nz + zr).astype(jnp.int32)
    return ((yr * nx + xr) * nz + zr).astype(jnp.int32)


def sum_kernel(count, *refs):
    total = refs[0][...].astype(F32)
    for ref in refs[1:count]:
        total = total + ref[...].astype(F32)
    refs[-1][...] = total.astype(refs[-1].dtype)


def sum_call(own, moved, others, kind=BF):
    shape = moved[0].shape
    steps = 2 if shape[0] % 2 == 0 else 1
    block = pl.BlockSpec((shape[0] // steps,) + shape[1:], lambda i: (i, 0, 0))
    return pl.pallas_call(
        functools.partial(sum_kernel, 1 + len(moved)),
        grid=(steps,),
        in_specs=[block] * (1 + len(moved)) + held(others),
        out_specs=block,
        out_shape=jax.ShapeDtypeStruct(shape, kind),
        compiler_params=params_of(),
        name="sum",
        cost_estimate=cost(2),
    )(own, *moved, *others)


def scatter_plane(slots, others=()):
    nz = lax.axis_size("z")
    moved = [
        diagonal(slots[nz * index : nz * index + nz], sy, sx)
        for index, (sy, sx) in enumerate(plane_steps())
        if index
    ]
    return sum_call(slots, moved, others)


def scatter_step(slots, axis, others=()):
    size = lax.axis_size(axis)
    count = slots.shape[0] // size
    moved = [shift(slots[count * k : count * k + count], axis, k) for k in range(1, size)]
    return sum_call(slots, moved, others)


def scatter_line(column, others=None):
    if others is not None:
        moved = [shift(column[k : k + 1], "z", k) for k in range(1, lax.axis_size("z"))]
        return sum_call(column, moved, others, F32)[0]
    total = column[0].astype(F32)
    for k in range(1, lax.axis_size("z")):
        total = total + shift(column[k], "z", k).astype(F32)
    return total


def split_three(value):
    high = lax.reduce_precision(value, 8, 7)
    rest = value - high
    mid = lax.reduce_precision(rest, 8, 7)
    return [high.astype(BF), mid.astype(BF), (rest - mid).astype(BF)]


def join_three(parts):
    high, mid, small = (part.astype(F32) for part in parts)
    return high + (mid + small)


def base_rows(tables):
    half = NR // 2
    low, high = tables[:, :, :1], tables[:, :, -1:]
    one = tables.shape[:2]

    def many(edge, count):
        return jnp.broadcast_to(edge, one + (count,))

    line = jnp.concatenate(
        [many(high, NB - half + 1), tables[:, :, ::-1], many(low, 255 - half), many(high, 128)],
        axis=2,
    )[0]
    plane = jnp.concatenate(
        [tables[:, :, half:], many(high, NB - half), many(low, NB - half), tables[:, :, :half]], axis=2
    )
    pair = jnp.concatenate([plane[1], plane[2]], axis=1)
    rows = jnp.stack([line, pair], axis=1)
    return jnp.pad(rows, ((0, 0), (0, 6), (0, 0)))


def sum_map():
    half = NR // 2
    found = np.zeros((3, 512, 3, NR), np.float32)

    def entry(distance):
        return min(max(distance, -half), half - 1) + half

    for k in range(512):
        found[0, k, 0, entry(128 - k if k < 384 else 640 - k)] = 1.0
        lane = k % 256
        found[1, k, 1 + k // 256, entry(-lane if lane < 128 else 256 - lane)] = 1.0
        found[2, k, 0, NR - 1 if k < 256 else 0] = 1.0
    return found.reshape(3 * 512, 3 * NR)


def table_sums(sums):
    flat = sums[:, :3].reshape(sums.shape[0], -1)
    return jnp.dot(flat, jnp.asarray(sum_map()), precision=lax.Precision.HIGHEST)


def build_tables(base, strip, planes, head):
    line = jnp.broadcast_to(base[head, 0:1, :], (128, 512))
    middle = pltpu.roll(line, 0, 1, stride=1, stride_axis=0)[:, :384]
    strip[head, :, 256:640] = middle
    strip[head, :, :256] = jnp.broadcast_to(base[head, 0:1, 0:1], (128, 256))
    strip[head, :, 640:] = jnp.broadcast_to(base[head, 0:1, 383:384], (128, 256))
    for k in range(2):
        row = jnp.broadcast_to(base[head, 1:2, 256 * k : 256 * k + 256], (128, 256))
        rolled = pltpu.roll(row, 0, 1, stride=1, stride_axis=0)
        planes[head, k] = rolled[:, :128].astype(BF)


def left_side(both, planes, head):
    return jnp.concatenate(
        [
            dot(both[:, :NB], planes[head, 0]).astype(BF),
            dot(both[:, NB:], planes[head, 1]).astype(BF),
        ],
        axis=1,
    )


def head_lanes(value, head):
    lanes = lax.broadcasted_iota(jnp.int32, value.shape, 1)
    return jnp.where((lanes >= HD) == (head == 1), value, jnp.zeros_like(value))


def scores_t(key_side, query_side, strip, head, valid):
    count = key_side.shape[0]
    raw = dot_nt(key_side, query_side)
    blocks = []
    for block in range(count // 128):
        start = 384 - 128 * block
        part = raw[128 * block : 128 * block + 128] + strip[head, :, start : start + count]
        rows = lax.broadcasted_iota(jnp.int32, (128, count), 0) + 128 * block
        blocks.append(jnp.where(rows < valid, part, NEGATIVE))
    return blocks


def attend_kernel(valid_ref, q_ref, k_ref, v_ref, both_ref, base_ref, mixed_ref, log_ref, strip, planes):
    page = pl.program_id(1)

    @pl.when(page == 0)
    def _():
        for head in range(2):
            build_tables(base_ref, strip, planes, head)

    valid = valid_ref[page]
    both = both_ref[...]
    key_side = jnp.concatenate([both, k_ref[...]], axis=1)
    values_t = v_ref[...].T
    mixed = []
    for head in range(2):
        query_side = jnp.concatenate(
            [left_side(both, planes, head), head_lanes(q_ref[...], head)], axis=1
        )
        blocks = scores_t(key_side, query_side, strip, head, valid)
        highest = functools.reduce(
            jnp.maximum, [jnp.max(block, axis=0, keepdims=True) for block in blocks]
        )
        raised = [jnp.exp(block - highest) for block in blocks]
        total = functools.reduce(
            jnp.add, [jnp.sum(part, axis=0, keepdims=True) for part in raised]
        )
        inverse = 1.0 / total
        probs = jnp.concatenate([(part * inverse).astype(BF) for part in raised], axis=0)
        mixed.append(dot(values_t[HD * head : HD * head + HD], probs))
        log_ref[0, 0, head : head + 1, :] = highest + jnp.log(total)
    mixed_ref[...] = jnp.concatenate(mixed, axis=0).T.astype(BF)


def attend_call(valid, projected, both, base, count):
    pages = projected.shape[1] // count
    pairs = H // 2

    def part(index):
        return pl.BlockSpec((None, count, 128), lambda pair, page: (index, page, pair))

    return pl.pallas_call(
        attend_kernel,
        grid=(pairs, pages),
        in_specs=[
            pl.BlockSpec(memory_space=pltpu.SMEM),
            part(0),
            part(1),
            part(2),
            pl.BlockSpec((count, 2 * NB), lambda pair, page: (page, 0)),
            pl.BlockSpec((2, 8, 512), lambda pair, page: (pair, 0, 0)),
        ],
        out_specs=[
            pl.BlockSpec((count, 128), lambda pair, page: (page, pair)),
            pl.BlockSpec((1, 1, 8, count), lambda pair, page: (page, pair, 0, 0)),
        ],
        out_shape=[
            jax.ShapeDtypeStruct(projected.shape[1:], BF),
            jax.ShapeDtypeStruct((pages, pairs, 8, count), F32),
        ],
        scratch_shapes=[
            pltpu.VMEM((2, 128, count + 384), F32),
            pltpu.VMEM((2, 2, NB, NB), BF),
        ],
        compiler_params=params_of(),
        name="attend",
        cost_estimate=cost(28),
    )(valid, projected, projected, projected, both, base)


def fold_diagonals(value):
    rows, lanes = value.shape
    while rows > 1:
        rows //= 2
        value = value[:rows] + pltpu.roll(value[rows:], lanes - rows, 1)
    return value


def attend_back_kernel(
    valid_ref, q_ref, k_ref, v_ref, dm_ref, mixed_ref, log_ref, both_ref, both_t_ref, base_ref,
    grad_ref, sums_ref, strip, planes, d_strip, d_planes,
):
    page = pl.program_id(1)

    @pl.when(page == 0)
    def _():
        for head in range(2):
            build_tables(base_ref, strip, planes, head)
        d_strip[...] = jnp.zeros_like(d_strip)
        d_planes[...] = jnp.zeros_like(d_planes)

    valid = valid_ref[page]
    both = both_ref[...]
    both_t = both_t_ref[...]
    count = both.shape[0]
    key_side = jnp.concatenate([both, k_ref[...]], axis=1)
    values = v_ref[...]
    keys_t = k_ref[...].T
    d_mixed_t = dm_ref[...].T
    weighted = d_mixed_t.astype(F32) * mixed_ref[...].T.astype(F32)
    rows = lax.broadcasted_iota(jnp.int32, d_mixed_t.shape, 0)
    d_keys = d_values = None
    d_queries = []
    for head in range(2):
        masked_q = head_lanes(q_ref[...], head)
        query_side = jnp.concatenate([left_side(both, planes, head), masked_q], axis=1)
        blocks = scores_t(key_side, query_side, strip, head, valid)
        log_total = log_ref[0, 0, head : head + 1, :]
        inner = jnp.sum(weighted[HD * head : HD * head + HD], axis=0, keepdims=True)
        d_mixed_head = jnp.where(
            (rows >= HD) == (head == 1), d_mixed_t, jnp.zeros_like(d_mixed_t)
        )
        d_probs = dot(values, d_mixed_head)
        probs_low, scores_low = [], []
        for index, block in enumerate(blocks):
            probs = jnp.exp(block - log_total)
            d_scores = probs * (d_probs[128 * index : 128 * index + 128] - inner)
            start = 384 - 128 * index
            d_strip[head, :, start : start + count] += d_scores
            probs_low.append(probs.astype(BF))
            scores_low.append(d_scores.astype(BF))
        probs_low = jnp.concatenate(probs_low, axis=0)
        scores_low = jnp.concatenate(scores_low, axis=0)
        part_v = dot(probs_low, head_lanes(dm_ref[...], head))
        mixed_k = dot(scores_low, jnp.concatenate([both, masked_q], axis=1))
        part_k = mixed_k[:, 2 * NB :]
        d_values = part_v if d_values is None else d_values + part_v
        d_keys = part_k if d_keys is None else d_keys + part_k
        d_queries.append(dot(keys_t[HD * head : HD * head + HD], scores_low))
        for k in range(2):
            side = mixed_k[:, NB * k : NB * k + NB].astype(BF)
            d_planes[head, k] += dot(both_t[NB * k : NB * k + NB], side)
    grad_ref[0] = (jnp.concatenate(d_queries, axis=0).T * HD ** (-0.5)).astype(BF)
    grad_ref[1] = d_keys.astype(BF)
    grad_ref[2] = d_values.astype(BF)

    @pl.when(page == pl.num_programs(1) - 1)
    def _():
        blank = jnp.zeros((128, 128), F32)
        for head in range(2):
            middle = jnp.concatenate([d_strip[head, :, 256:640], blank], axis=1)
            sums_ref[head, 0:1, :] = fold_diagonals(middle)
            for k in range(2):
                padded = jnp.concatenate([d_planes[head, k], blank], axis=1)
                sums_ref[head, 1:2, 256 * k : 256 * k + 256] = fold_diagonals(padded)
            sums_ref[head, 2:3, :256] = jnp.sum(d_strip[head, :, :256], axis=0, keepdims=True)
            sums_ref[head, 2:3, 256:] = jnp.sum(d_strip[head, :, 640:], axis=0, keepdims=True)


def attend_back_call(valid, projected, d_mixed, mixed, log_total, both, both_t, base, count, first, pairs, others=()):
    pages = projected.shape[1] // count

    def part(index):
        return pl.BlockSpec((None, count, 128), lambda pair, page: (index, page, first + pair))

    wide = pl.BlockSpec((count, 128), lambda pair, page: (page, first + pair))
    return pl.pallas_call(
        waiting(attend_back_kernel, 10, len(others)),
        grid=(pairs, pages),
        in_specs=[
            pl.BlockSpec(memory_space=pltpu.SMEM),
            part(0),
            part(1),
            part(2),
            wide,
            wide,
            pl.BlockSpec((1, 1, 8, count), lambda pair, page: (page, first + pair, 0, 0)),
            pl.BlockSpec((count, 2 * NB), lambda pair, page: (page, 0)),
            pl.BlockSpec((2 * NB, count), lambda pair, page: (0, page)),
            pl.BlockSpec((2, 8, 512), lambda pair, page: (first + pair, 0, 0)),
        ]
        + held(others),
        out_specs=[
            pl.BlockSpec((3, count, 128), lambda pair, page: (0, page, pair)),
            pl.BlockSpec((2, 8, 512), lambda pair, page: (pair, 0, 0)),
        ],
        out_shape=[
            jax.ShapeDtypeStruct(projected.shape[:2] + (128 * pairs,), BF),
            jax.ShapeDtypeStruct((2 * pairs, 8, 512), F32),
        ],
        scratch_shapes=[
            pltpu.VMEM((2, 128, count + 384), F32),
            pltpu.VMEM((2, 2, NB, NB), BF),
            pltpu.VMEM((2, 128, count + 384), F32),
            pltpu.VMEM((2, 2, NB, NB), F32),
        ],
        compiler_params=params_of(),
        name="attend_back",
        cost_estimate=cost(7 * pairs),
    )(valid, projected, projected, projected, d_mixed, mixed, log_total, both, both_t, base, *others)


def gelu_parts(before):
    size = jnp.abs(before) * (0.5**0.5)
    denominator = 1.0 + 0.3275911 * size
    t = pl.reciprocal(denominator, approx=True)
    t = t * (2.0 - denominator * t)
    bell = jnp.exp(-0.5 * before * before)
    tail = t * (
        0.5 * 0.254829592
        + t
        * (
            0.5 * -0.284496736
            + t * (0.5 * 1.421413741 + t * (0.5 * -1.453152027 + t * (0.5 * 1.061405429)))
        )
    )
    tail = tail * bell
    below = jnp.where(before >= 0.0, 1.0 - tail, tail)
    return before * below, below + before * (bell * 0.3989422804014327)


def normalize(rows):
    center = rows - jnp.mean(rows, axis=-1, keepdims=True)
    spread = jnp.mean(center * center, axis=-1, keepdims=True)
    scale = lax.rsqrt(spread + EPSILON)
    return center * scale, scale


def normalize_back(grad, hat, scale, gain):
    scaled = grad * gain
    first = jnp.mean(scaled, axis=-1, keepdims=True)
    second = jnp.mean(scaled * hat, axis=-1, keepdims=True)
    return scale * (scaled - first - hat * second)


def add_sums(ref, index, value, fresh):
    total = jnp.sum(value, axis=0, keepdims=True)
    ref[index : index + 1] = jnp.where(fresh, total, ref[index : index + 1] + total)


def whole_spec(shape):
    return pl.BlockSpec(shape, lambda *_: (0,) * len(shape))


def smem():
    return pl.BlockSpec(memory_space=pltpu.SMEM)


def weight_specs(stacks, rows, first):
    nz, _, width = stacks[0].shape
    return [pl.BlockSpec((nz, rows, width), lambda i: (0, first + i, 0))] * len(stacks)


def project_kernel(count, one_ref, two_ref, raw_ref, both_ref, space_ref, coef_ref, *refs):
    stacks, (out_ref, wide_ref, normed_ref, inputs_ref, joint_ref, plain_ref) = refs[:count], refs[count:]
    step = pl.program_id(0)

    @pl.when(step == 0)
    def _():
        normed = (raw_ref[...].astype(F32) - coef_ref[0:1]) * coef_ref[1:2]
        inputs = normed * coef_ref[2:3] + coef_ref[3:4]
        normed_ref[...] = normed
        inputs_ref[...] = inputs
        plain_ref[...] = inputs.astype(BF)
        joint_ref[...] = (inputs + dot(both_ref[...], space_ref[...])).astype(BF)

    if two_ref.shape[0] == 1:
        place(one_ref, stacks, wide_ref.at[0])
    else:
        place(one_ref, stacks[: count // 2], wide_ref.at[0])
        place(two_ref, stacks[count // 2 :], wide_ref.at[0], wide_ref.shape[3] // 2)
    width = raw_ref.shape[1]
    weight = wide_ref[0].reshape(width, width)
    rows = jnp.where(step == 2, plain_ref[...], joint_ref[...])
    factor = jnp.where(step == 0, HD ** (-0.5), 1.0)
    out_ref[0] = (dot(rows, weight) * factor).astype(BF)


def project_call(sources, stacks, rows, raw, both, space, coefs):
    tokens, width = raw.shape
    chips = sources[0].shape[0]
    whole = whole_spec((tokens, width))
    return pl.pallas_call(
        functools.partial(project_kernel, len(stacks)),
        grid=(3,),
        in_specs=[smem(), smem(), whole, whole_spec(both.shape), whole_spec(space.shape)]
        + [whole_spec(coefs.shape)]
        + weight_specs(stacks, rows, 0),
        out_specs=[
            pl.BlockSpec((1, tokens, width), lambda i: (i, 0, 0)),
            pl.BlockSpec((1, chips, rows, width), lambda i: (i, 0, 0, 0)),
            whole,
            whole,
            whole,
            whole,
        ],
        out_shape=[
            jax.ShapeDtypeStruct((3, tokens, width), BF),
            jax.ShapeDtypeStruct((3, chips, rows, width), BF),
            jax.ShapeDtypeStruct((tokens, width), F32),
            jax.ShapeDtypeStruct((tokens, width), F32),
            jax.ShapeDtypeStruct((tokens, width), BF),
            jax.ShapeDtypeStruct((tokens, width), BF),
        ],
        compiler_params=params_of(),
        name="project",
        cost_estimate=cost(12),
    )(*sources, raw, both, space, coefs, *stacks)


def output_kernel(count, where_ref, mixed_ref, keep_ref, *refs):
    stacks, (att_ref, low_ref, wide_ref) = refs[:count], refs[count:]
    place(where_ref, stacks, wide_ref)
    width = mixed_ref.shape[1]
    att = dot(mixed_ref[...], wide_ref[...].reshape(width, width)) * keep_ref[...]
    att_ref[...] = att
    low_ref[...] = att.astype(BF)


def output_call(where, stacks, rows, mixed, keep, others):
    tokens, width = mixed.shape
    nz = stacks[0].shape[0]
    chips = len(stacks) * nz
    return pl.pallas_call(
        waiting(functools.partial(output_kernel, len(stacks)), 3 + len(stacks), len(others)),
        grid=(1,),
        in_specs=[smem(), whole_spec((tokens, width)), whole_spec((tokens, 1))]
        + weight_specs(stacks, rows, 8)
        + held(others),
        out_specs=[
            whole_spec((tokens, width)),
            whole_spec((tokens, width)),
            whole_spec((chips, rows, width)),
        ],
        out_shape=[
            jax.ShapeDtypeStruct((tokens, width), F32),
            jax.ShapeDtypeStruct((tokens, width), BF),
            jax.ShapeDtypeStruct((chips, rows, width), BF),
        ],
        compiler_params=params_of(),
        name="output",
        cost_estimate=cost(5),
    )(where, mixed, keep, *stacks, *others)


def feed_kernel(count, where_ref, inputs_ref, own_ref, other_ref, vec_ref, bias_ref, *refs):
    stacks = refs[:count]
    u_ref, low_ref, hat_ref, scale_ref, active_ref, slope_ref, wide_ref = refs[count:]
    half = inputs_ref.shape[0] // 2

    @pl.when(pl.program_id(0) == 0)
    def _():
        for page in range(2):
            here = pl.ds(half * page, half)
            there = pl.ds(half * (1 - page), half)
            rows = inputs_ref[here, :] + own_ref[here, :] + other_ref[there, :].astype(F32)
            hat, scale = normalize(rows)
            u = hat * vec_ref[2:3] + vec_ref[3:4]
            u_ref[here, :] = u
            low_ref[here, :] = u.astype(BF)
            hat_ref[here, :] = hat
            scale_ref[here, :] = scale

    place(where_ref, stacks, wide_ref.at[0])
    width = inputs_ref.shape[1]
    weight = wide_ref[0].reshape(width, width)
    before = dot(low_ref[...], weight) + bias_ref[...]
    active, slope = gelu_parts(before)
    active_ref[...] = active.astype(BF)
    slope_ref[...] = slope.astype(BF)


def feed_call(where, stacks, rows, inputs, own, other, vecs, bias):
    tokens, width = inputs.shape
    hidden = bias.shape[1]
    nz = stacks[0].shape[0]
    chips = len(stacks) * nz
    whole = whole_spec((tokens, width))
    block = pl.BlockSpec((tokens, width), lambda i: (0, i))
    return pl.pallas_call(
        functools.partial(feed_kernel, len(stacks)),
        grid=(hidden // width,),
        in_specs=[smem(), whole, whole, whole, whole_spec(vecs.shape)]
        + [pl.BlockSpec((1, width), lambda i: (0, i))]
        + weight_specs(stacks, rows, 4),
        out_specs=[
            whole,
            whole,
            whole,
            whole_spec((tokens, 1)),
            block,
            block,
            pl.BlockSpec((1, chips, rows, width), lambda i: (i, 0, 0, 0)),
        ],
        out_shape=[
            jax.ShapeDtypeStruct((tokens, width), F32),
            jax.ShapeDtypeStruct((tokens, width), BF),
            jax.ShapeDtypeStruct((tokens, width), F32),
            jax.ShapeDtypeStruct((tokens, 1), F32),
            jax.ShapeDtypeStruct((tokens, hidden), BF),
            jax.ShapeDtypeStruct((tokens, hidden), BF),
            jax.ShapeDtypeStruct((hidden // width, chips, rows, width), BF),
        ],
        compiler_params=params_of(),
        name="feed",
        cost_estimate=cost(24),
    )(where, inputs, own, other, vecs, bias, *stacks)


def close_kernel(count, where_ref, active_ref, u_ref, cot_ref, keep_ref, vec_ref, *refs):
    stacks = refs[:count]
    out_ref, dy_ref, low_ref, sums_ref, wide_ref = refs[count:]
    step = pl.program_id(0)

    @pl.when(step == 0)
    def _():
        place(where_ref, stacks, wide_ref)

    weight = wide_ref[...].reshape(-1, u_ref.shape[1])
    rows = u_ref[...] + (dot(active_ref[...], weight) + vec_ref[6:7])
    hat, scale = normalize(rows)
    gain = vec_ref[4:5]
    keep = keep_ref[...]
    out_ref[...] = ((hat * gain + vec_ref[5:6]) * keep).astype(BF)
    cot = cot_ref[...].astype(F32) * keep
    dy = normalize_back(cot, hat, scale, gain)
    low = dy.astype(BF)
    dy_ref[...] = dy
    low_ref[...] = low
    add_sums(sums_ref, 0, cot * hat, step == 0)
    add_sums(sums_ref, 1, cot, step == 0)
    add_sums(sums_ref, 2, low.astype(F32), step == 0)


def close_call(where, stacks, rows, active, u, cot, keep, vecs):
    tokens, width = u.shape
    hidden = active.shape[1]
    nz = stacks[0].shape[0]
    groups = 4
    chips = len(stacks) * nz
    steps = 4
    block = pl.BlockSpec((tokens // steps, width), lambda i: (i, 0))
    return pl.pallas_call(
        functools.partial(close_kernel, len(stacks)),
        grid=(steps,),
        in_specs=[
            smem(),
            pl.BlockSpec((tokens // steps, hidden), lambda i: (i, 0)),
            block,
            block,
            pl.BlockSpec((tokens // steps, 1), lambda i: (i, 0)),
            whole_spec(vecs.shape),
        ]
        + [whole_spec((nz, groups * rows, width))] * len(stacks),
        out_specs=[
            block,
            block,
            block,
            whole_spec((8, width)),
            whole_spec((chips, groups * rows, width)),
        ],
        out_shape=[
            jax.ShapeDtypeStruct((tokens, width), BF),
            jax.ShapeDtypeStruct((tokens, width), F32),
            jax.ShapeDtypeStruct((tokens, width), BF),
            jax.ShapeDtypeStruct((8, width), F32),
            jax.ShapeDtypeStruct((chips, groups * rows, width), BF),
        ],
        compiler_params=params_of(),
        name="close",
        cost_estimate=cost(13),
    )(where, active, u, cot, keep, vecs, *stacks)


def store_slots(slots_ref, out_ref, total, first=0):
    rows = out_ref.shape[1]
    for index in range(total.shape[0] // rows):
        part = total[index * rows : index * rows + rows].astype(BF)
        out_ref[slots_ref[first + index]] = part


def second_kernel(slots_ref, active_ref, low_ref, out_ref):
    total = dot(active_ref[...].T, low_ref[...])
    count = total.shape[0] // out_ref.shape[1]
    store_slots(slots_ref, out_ref, total, pl.program_id(0) * count)


def second_call(slots, active, low, chips):
    tokens, width = low.shape
    hidden = active.shape[1]
    return pl.pallas_call(
        second_kernel,
        grid=(hidden // width,),
        in_specs=[
            smem(),
            pl.BlockSpec((tokens, width), lambda i: (0, i)),
            whole_spec((tokens, width)),
        ],
        out_specs=whole_spec((chips, hidden // chips, width)),
        out_shape=jax.ShapeDtypeStruct((chips, hidden // chips, width), BF),
        compiler_params=params_of(),
        name="second",
        cost_estimate=cost(10),
    )(slots, active, low)


def feed_back_kernel(
    slots_ref, rows_ref, low_ref, second_ref, first_ref, slope_ref, dy_ref, hat_ref, scale_ref, vec_ref,
    dpre_ref, dlow_ref, dfirst_ref, dbias_ref, sums_ref, rows_t, total_ref,
):
    step = pl.program_id(0)

    @pl.when(step == 0)
    def _():
        rows_t[...] = rows_ref[...].T
        total_ref[...] = dy_ref[...]

    d_active = dot_nt(low_ref[...], second_ref[...])
    d_before = (slope_ref[...].astype(F32) * d_active).astype(BF)
    dbias_ref[0] = jnp.sum(d_before.astype(F32), axis=0, keepdims=True)
    total_ref[...] += dot_nt(d_before, first_ref[0])
    total = dot(rows_t[...], d_before)
    chips, piece = dfirst_ref.shape[0], dfirst_ref.shape[1] // 2
    half = dfirst_ref.shape[2]
    for chip in range(chips):
        part = total[chip * piece : chip * piece + piece].astype(BF)
        dfirst_ref[slots_ref[chip], :piece] = part[:, :half]
        dfirst_ref[slots_ref[chip], piece:] = part[:, half:]

    @pl.when(step == pl.num_programs(0) - 1)
    def _():
        grad = total_ref[...]
        hat = hat_ref[...]
        d_pre = normalize_back(grad, hat, scale_ref[...], vec_ref[2:3])
        dpre_ref[...] = d_pre
        dlow_ref[...] = d_pre.astype(BF)
        add_sums(sums_ref, 0, grad * hat, True)
        add_sums(sums_ref, 1, grad, True)


def feed_back_call(slots, rows, low, second, first, slope, dy, hat, scale, vecs, chips, others):
    tokens, width = rows.shape
    hidden = second.shape[0]
    piece = width // chips
    whole = whole_spec((tokens, width))
    return pl.pallas_call(
        waiting(feed_back_kernel, 10, len(others)),
        grid=(hidden // width,),
        in_specs=[
            smem(),
            whole,
            whole,
            pl.BlockSpec((width, width), lambda i: (i, 0)),
            pl.BlockSpec((1, width, width), lambda i: (i, 0, 0)),
            pl.BlockSpec((tokens, width), lambda i: (0, i)),
            whole,
            whole,
            whole_spec((tokens, 1)),
            whole_spec(vecs.shape),
        ]
        + held(others),
        out_specs=[
            whole,
            whole,
            pl.BlockSpec((chips, 2 * piece, width // 2), lambda i: (0, i, 0)),
            pl.BlockSpec((1, 1, width), lambda i: (i, 0, 0)),
            whole_spec((8, width)),
        ],
        out_shape=[
            jax.ShapeDtypeStruct((tokens, width), F32),
            jax.ShapeDtypeStruct((tokens, width), BF),
            jax.ShapeDtypeStruct((chips, 2 * piece * (hidden // width), width // 2), BF),
            jax.ShapeDtypeStruct((hidden // width, 1, width), F32),
            jax.ShapeDtypeStruct((8, width), F32),
        ],
        scratch_shapes=[pltpu.VMEM((width, tokens), BF), pltpu.VMEM((tokens, width), F32)],
        compiler_params=params_of(),
        name="feed_back",
        cost_estimate=cost(26),
    )(slots, rows, low, second, first, slope, dy, hat, scale, vecs, *others)


def middle_kernel(own_ref, other_ref, keep_ref, weight_ref, dmixed_ref, low_ref):
    half = own_ref.shape[0] // 2
    for page in range(2):
        here = pl.ds(half * page, half)
        there = pl.ds(half * (1 - page), half)
        merged = (own_ref[here, :] + other_ref[there, :].astype(F32)) * keep_ref[here, :]
        low_ref[here, :] = merged.astype(BF)
    dmixed_ref[...] = dot_nt(low_ref[...], weight_ref[...]).astype(BF)


def middle_call(own, other, keep, weight):
    tokens, width = own.shape
    whole = whole_spec((tokens, width))
    return pl.pallas_call(
        middle_kernel,
        grid=(1,),
        in_specs=[whole, whole, whole_spec((tokens, 1)), whole_spec((width, width))],
        out_specs=[whole, whole],
        out_shape=[jax.ShapeDtypeStruct((tokens, width), BF)] * 2,
        compiler_params=params_of(),
        name="middle",
        cost_estimate=cost(6),
    )(own, other, keep, weight)


def turn_kernel(joint_ref, plain_ref, mixed_ref, both_ref, lefts_ref, both_t_ref):
    for index, ref in enumerate((joint_ref, plain_ref, mixed_ref)):
        lefts_ref[index] = ref[...].T
    both_t_ref[...] = both_ref[...].T


def turn_call(joint, plain, mixed, both):
    tokens, width = joint.shape
    whole = whole_spec((tokens, width))
    return pl.pallas_call(
        turn_kernel,
        grid=(1,),
        in_specs=[whole, whole, whole, whole_spec(both.shape)],
        out_specs=[whole_spec((3, width, tokens)), whole_spec(both.shape[::-1])],
        out_shape=[
            jax.ShapeDtypeStruct((3, width, tokens), BF),
            jax.ShapeDtypeStruct(both.shape[::-1], BF),
        ],
        compiler_params=params_of(),
        name="turn",
        cost_estimate=cost(8),
    )(joint, plain, mixed, both)


def store_rows(slots_ref, out_ref, start, total):
    chips = out_ref.shape[0]
    piece = total.shape[0] // chips
    for chip in range(chips):
        low = total[chip * piece : chip * piece + piece].astype(BF)
        out_ref[slots_ref[chip], start : start + piece] = low


def grads_one_kernel(slots_ref, turned_ref, left_ref, grad_ref, datt_ref, dwa_ref, dwb_ref):
    step = pl.program_id(0)
    total = dot(left_ref[0], jnp.where(step < 3, grad_ref[0], datt_ref[...]))
    pl.when(step < 2)(functools.partial(store_rows, turned_ref, dwa_ref, 0, total))
    pl.when(step >= 2)(functools.partial(store_rows, slots_ref, dwb_ref, 0, total))


def grads_one_call(slots, turned, lefts, grad, datt, chips):
    _, width, tokens = lefts.shape
    half = width // 2
    piece = width // chips
    return pl.pallas_call(
        grads_one_kernel,
        grid=(5,),
        in_specs=[
            smem(),
            smem(),
            pl.BlockSpec((1, width, tokens), lambda i: (jnp.where(i < 2, 0, jnp.minimum(i - 1, 2)), 0, 0)),
            pl.BlockSpec((1, tokens, half), lambda i: (jnp.minimum(i, 2), 0, 0)),
            pl.BlockSpec((tokens, half), lambda i: (0, jnp.maximum(i - 3, 0))),
        ],
        out_specs=[
            pl.BlockSpec((chips, None, piece, half), lambda i: (0, jnp.minimum(i, 1), 0, 0)),
            pl.BlockSpec((chips, None, piece, half), lambda i: (0, jnp.maximum(i - 2, 0), 0, 0)),
        ],
        out_shape=[
            jax.ShapeDtypeStruct((chips, 2, piece, half), BF),
            jax.ShapeDtypeStruct((chips, 3, piece, half), BF),
        ],
        compiler_params=params_of(),
        name="grads_one",
        cost_estimate=cost(9),
    )(slots, turned, lefts, grad, datt)


def grads_two_kernel(
    slots_ref, turned_ref, left_ref, near_ref, grad_ref, weight_ref, dpre_ref, normed_ref, both_t_ref,
    coef_ref, early_ref, dwa_ref, dwb_ref, rows_ref, total_ref,
):
    step = pl.program_id(0)
    chips, half = dwa_ref.shape[0], dwa_ref.shape[2]
    piece = dwa_ref.shape[1] // 2
    space_size = both_t_ref.shape[0]
    near = space_size // (2 * chips)
    grad = grad_ref[0]
    total = dot(left_ref[0], grad)
    part = dot_nt(jnp.concatenate([near_ref[0], grad], axis=1), weight_ref[0])

    @pl.when(step == 0)
    def _():
        store_rows(turned_ref, dwa_ref, 0, total)
        total_ref[...] = part

    @pl.when(step == 1)
    def _():
        store_rows(turned_ref, dwa_ref, piece, total)
        joint = total_ref[...] + part
        total_ref[...] = joint + dpre_ref[...]
        space = dot(both_t_ref[...], joint.astype(BF)).astype(BF)
        for chip in range(chips):
            for k in range(2):
                begin = k * space_size // 2 + chip * near
                for side in range(2):
                    start = piece + (2 * side + k) * near
                    dwb_ref[slots_ref[chip], start : start + near] = space[
                        begin : begin + near, half * side : half * side + half
                    ]

    @pl.when(step == 2)
    def _():
        store_rows(slots_ref, dwb_ref, 0, total)
        dx = total_ref[...] + part
        rows_ref[...] = dx * coef_ref[2:3] * coef_ref[1:2]
        gain = jnp.sum(dx * normed_ref[...], axis=0, keepdims=True) * coef_ref[4:5]
        shift_row = jnp.sum(dx, axis=0, keepdims=True) * coef_ref[4:5]
        early = early_ref[...]
        place_row = lax.broadcasted_iota(jnp.int32, early.shape, 0)
        early = jnp.where(place_row == 0, gain, jnp.where(place_row == 1, shift_row, early)).astype(BF)
        start = piece + 4 * near
        count = early.shape[0]
        for chip in range(chips):
            for side in range(2):
                dwb_ref[chip, start + count * side : start + count * side + count] = early[
                    :, half * side : half * side + half
                ]


def grads_two_call(slots, turned, lefts, near, grad, weight, d_pre, normed, both_t, coefs, early, chips, others):
    _, width, tokens = lefts.shape
    half = width // 2
    whole = whole_spec((tokens, width))
    piece = width // chips
    tall = piece + 2 * (both_t.shape[0] // chips) + 2 * early.shape[0]
    return pl.pallas_call(
        waiting(grads_two_kernel, 11, len(others)),
        grid=(3,),
        in_specs=[
            smem(),
            smem(),
            pl.BlockSpec((1, width, tokens), lambda i: (i // 2, 0, 0)),
            pl.BlockSpec((1, tokens, half), lambda i: (i, 0, 0)),
            pl.BlockSpec((1, tokens, half), lambda i: (i, 0, 0)),
            pl.BlockSpec((1, width, width), lambda i: (i, 0, 0)),
            whole,
            whole,
            whole_spec(both_t.shape),
            whole_spec(coefs.shape),
            whole_spec(early.shape),
        ]
        + held(others),
        out_specs=[whole_spec((chips, 2 * piece, half)), whole_spec((chips, tall, half)), whole],
        out_shape=[
            jax.ShapeDtypeStruct((chips, 2 * piece, half), BF),
            jax.ShapeDtypeStruct((chips, tall, half), BF),
            jax.ShapeDtypeStruct((tokens, width), F32),
        ],
        scratch_shapes=[pltpu.VMEM((tokens, width), F32)],
        compiler_params=params_of(),
        name="grads_two",
        cost_estimate=cost(10),
    )(slots, turned, lefts, near, grad, weight, d_pre, normed, both_t, coefs, early, *others)


def adam(weight, grad, first, second, rate, decay):
    first_new = BETA_ONE * first + (1 - BETA_ONE) * grad
    second_new = BETA_TWO * second + (1 - BETA_TWO) * grad * grad
    ratio = (
        first_new / (1 - BETA_ONE**STEP) / (jnp.sqrt(second_new / (1 - BETA_TWO**STEP)) + ADAM_EPS)
    )
    return (first_new, second_new, weight - rate * (ratio + decay * weight))


def late_kernel(chips, piece, near, squares_ref, *refs):
    out_ref = refs[-1]
    total = refs[0][0].astype(F32)
    for ref in refs[1:-1]:
        total = total + ref[0].astype(F32)
    count = total.shape[0]
    out_ref[:count] = total
    weights = total[: 3 * piece]
    little = total[3 * piece + 4 * near :]
    squares = jnp.sum(weights * weights) + jnp.sum(little * little) / chips + squares_ref[0]
    out_ref[count:] = jnp.full((8, total.shape[1]), squares)


def late_call(column, squares, chips, piece, near):
    nz, count, half = column.shape
    moved = [shift(column[k : k + 1], "z", k) for k in range(1, nz)]
    block = whole_spec((1, count, half))
    return pl.pallas_call(
        functools.partial(late_kernel, chips, piece, near),
        grid=(1,),
        in_specs=[smem()] + [block] * nz,
        out_specs=whole_spec((count + 8, half)),
        out_shape=jax.ShapeDtypeStruct((count + 8, half), F32),
        compiler_params=params_of(),
        name="late",
        cost_estimate=cost(2),
    )(squares.reshape(1), column, *moved)


def chip_squares_kernel(begin, end, own_ref, other_ref, out_ref):
    space = own_ref[begin:end] + other_ref[begin:end]
    count = own_ref.shape[0] - 8
    both = own_ref[count:, :128] + other_ref[count:, :128]
    out_ref[...] = both + jnp.sum(space * space)


def chip_squares_call(own, other, begin, end):
    return pl.pallas_call(
        functools.partial(chip_squares_kernel, begin, end),
        grid=(1,),
        in_specs=[whole_spec(own.shape)] * 2,
        out_specs=whole_spec((8, 128)),
        out_shape=jax.ShapeDtypeStruct((8, 128), F32),
        compiler_params=params_of(),
        name="chip_squares",
        cost_estimate=cost(1),
    )(own, other)


def adam_kernel(piece, near, norm_ref, seen_ref, *refs):
    seen = seen_ref[0] == 1
    factor = CLIP / jnp.maximum(jnp.sqrt(norm_ref[0:1, 0:1]), CLIP)
    own_one, other_one, own_late, other_late = refs[:4]
    attn, feed_in, feed_out = refs[4:7], refs[7:12], refs[12:17]
    small = (refs[17:21], refs[21:25], refs[25:29])
    space, outs = refs[29:32], refs[32:]
    mine = piece // 2

    def pick(first, second):
        return jnp.where(seen, first, second)

    def step(weight, grad, first, second, rate, decay, targets, at):
        new = adam(weight[at], grad * factor, first[at], second[at], rate, decay)
        for target, value in zip(targets, new):
            target[at] = value
        if len(targets) == 4:
            targets[3][at] = new[2].astype(BF)

    def late_rows(ref, index):
        top = ref[piece * index : piece * index + mine]
        return pick(top, ref[piece * index + mine : piece * index + piece])

    half = own_one.shape[2]
    for stream in range(2):
        first = (lambda a, b: pick(a, b)) if stream == 0 else (lambda a, b: pick(b, a))
        for matrix in range(4):
            left = first(own_one[matrix], other_one[matrix])
            if matrix < 3:
                right = first(late_rows(own_late, matrix), late_rows(other_late, matrix))
            else:
                right = first(own_one[4], other_one[4])
            for side, grad in enumerate((left, right)):
                at = (stream, matrix, slice(None), slice(half * side, half * side + half))
                step(attn[0], grad, attn[1], attn[2], RATE_ATTN, DECAY, outs[:4], at)
        for group, target in ((feed_in, outs[4:8]), (feed_out, outs[8:12])):
            grad = first(group[3][...], group[4][...])
            step(group[0], grad, group[1], group[2], RATE_FEED, DECAY, target, (stream,))
    for index, group in enumerate(small):
        targets = outs[12 + 3 * index : 15 + 3 * index]
        step(group[0], group[3][...], group[1], group[2], RATE_OTHER, 0.0, targets, (slice(None),))
    for k in range(2):
        for side in range(2):
            begin = 3 * piece + (2 * side + k) * near
            total = own_late[begin : begin + near] + other_late[begin : begin + near]
            grad = pick(total[: near // 2], total[near // 2 :])
            at = (k, slice(None), slice(half * side, half * side + half))
            step(space[0], grad, space[1], space[2], RATE_OTHER, DECAY, outs[21:24], at)


def adam_call(norm, seen, piece, near, parts, groups):
    inputs = list(parts)
    shapes = []
    for index, group in enumerate(groups):
        inputs += group
        shapes += [jax.ShapeDtypeStruct(group[0].shape, F32)] * 3
        if index < 3:
            shapes.append(jax.ShapeDtypeStruct(group[0].shape, BF))
    return pl.pallas_call(
        functools.partial(adam_kernel, piece, near),
        grid=(1,),
        in_specs=[whole_spec(norm.shape), smem()]
        + [pl.BlockSpec(memory_space=pltpu.VMEM)] * len(inputs),
        out_specs=[whole_spec(shape.shape) for shape in shapes],
        out_shape=shapes,
        compiler_params=params_of(),
        name="adam",
        cost_estimate=cost(9),
    )(norm, seen, *inputs)


def body(
    visual, text, lengths, text_boxes, cot_visual, cot_text,
    attn_w, ffn_in, ffn_out, bias_in, vectors, pos_tables, spatial,
    attn_mom, attn_sec, in_mom, in_sec, out_mom, out_sec, bias_mom, bias_sec,
    vec_mom, vec_sec, pos_mom, pos_sec, spatial_mom, spatial_sec,
):
    core = lax.axis_index("c")
    seen = core == 0
    nz, ny, nx = (lax.axis_size(a) for a in CHIP)
    chips = nz * ny * nx
    devices = 2 * chips
    _, count, width = visual.shape
    tokens = 2 * count

    def mine_of(first, second):
        return jnp.where(seen, first, second)

    def trade(first, second):
        return mine_of(first, second), swap(mine_of(second, first))

    def by_core(own, other):
        return jnp.where(seen, jnp.stack([own, other]), jnp.stack([other, own]))

    attn_low = attn_w.astype(BF)
    in_low = ffn_in.astype(BF)
    out_low = ffn_out.astype(BF)
    attn_own, attn_other = trade(attn_low[0], attn_low[1])
    in_own, in_other = trade(in_low[0], in_low[1])
    out_own, out_other = trade(out_low[0], out_low[1])
    rows_a = attn_w.shape[2]
    rows_o = ffn_out.shape[1]
    hidden = ffn_in.shape[2]
    attn_piece = jnp.where(
        seen,
        jnp.concatenate([attn_own, attn_other], axis=1),
        jnp.concatenate([attn_other, attn_own], axis=1),
    )
    in_piece = by_core(in_own, in_other).reshape(2 * rows_a, hidden)
    out_piece = by_core(out_own, out_other).reshape(2 * rows_o, width)
    in_cut = in_piece.reshape(2 * rows_a, -1, width).transpose(1, 0, 2)
    out_cut = out_piece.reshape(-1, 2 * rows_a, width)

    raw_own = visual[0].astype(F32)
    sums = jnp.stack([jnp.sum(raw_own, axis=0), jnp.sum(raw_own * raw_own, axis=0)])
    vec_rows = [
        jnp.stack([vectors[0], vectors[1]] + [vectors[k + 2 * s] for k in (2, 3, 6, 7)] + [vectors[10 + s]])
        for s in range(2)
    ]

    def packed(s):
        def row(values):
            flat = values.reshape(1, -1)
            return jnp.pad(flat, ((0, 0), (0, -flat.shape[1] % width))).reshape(-1, width)

        return jnp.concatenate(
            [row(pos_tables[s].astype(BF)), row(jnp.concatenate(
                [part.reshape(1, -1) for part in split_three(vec_rows[s]) + split_three(bias_in[s])], axis=1
            ))], axis=0
        )

    pack_zero, pack_one = packed(0), packed(1)
    small_rows = pack_zero.shape[0]
    space = spatial.astype(BF).reshape(-1, width)
    space_rows = space.shape[0]
    pack_own, pack_other = trade(pack_zero, pack_one)
    space_other, sums_other = swap((space, sums))
    pack_both = by_core(pack_own, pack_other).reshape(2 * small_rows, width)
    space_both = by_core(space, space_other).reshape(2 * space_rows, width)
    small = jnp.concatenate(
        [space_both, pack_both, jnp.concatenate(split_three(sums + sums_other), axis=0)], axis=0
    )
    pad = -(small.shape[0] + 6 * rows_a) % 16
    first = jnp.concatenate(
        [attn_piece[:3].reshape(6 * rows_a, width), jnp.pad(small, ((0, pad), (0, 0)))], axis=0
    )
    rest = jnp.concatenate([out_cut, in_cut, attn_piece[3:]], axis=0).reshape(-1, width)
    wide_rest = lax.all_gather(rest, CHIP)
    halves, sources = relay(first)
    weight_rows = 6 * rows_a
    gathered = jnp.concatenate(
        [in_order(halves[k], sources[k], weight_rows, first.shape[0]) for k in range(2)], axis=2
    )
    wide_spatial = gathered[:, : 2 * space_rows].reshape(chips, 2, 2, -1, width)
    wide_spatial = wide_spatial.transpose(2, 0, 1, 3, 4).reshape(2 * NB, width)
    packs = gathered[:, 2 * space_rows : 2 * space_rows + 2 * small_rows]
    packs = packs.reshape(devices, small_rows, width)
    pos_size = pos_tables[0].size
    pos_lines = -(-pos_size // width)
    tables = packs[:, :pos_lines].reshape(devices, -1)[:, :pos_size]
    tables = tables.reshape(devices, 3, H, -1).transpose(1, 2, 0, 3).reshape(3, H, NR).astype(F32)
    params = packs[:, pos_lines:].reshape(devices, -1)
    vec_size = vec_rows[0].size
    bias_size = bias_in[0].size
    wide_vec = join_three([params[:, vec_size * k : vec_size * (k + 1)] for k in range(3)])
    wide_vec = wide_vec.reshape(devices, 7, -1).transpose(1, 0, 2).reshape(7, width)
    wide_bias = join_three(
        [params[:, 3 * vec_size + bias_size * k : 3 * vec_size + bias_size * (k + 1)] for k in range(3)]
    ).reshape(1, hidden)
    parts = gathered[:, 2 * space_rows + 2 * small_rows :]
    sums = jnp.sum(join_three([parts[:, 2 * k : 2 * k + 2] for k in range(3)]), axis=0)

    data_own, data_other = trade(visual[0], text[0])
    cot_own, cot_other = trade(cot_visual[0], cot_text[0])
    length_other, boxes_other = swap((lengths, text_boxes))
    total = count * devices
    mean = sums[0] / total
    variance = sums[1] / total - mean * mean
    inverse = lax.rsqrt(variance + EPSILON)
    stream_mean = jnp.where(seen, mean, 0.0)
    stream_inverse = jnp.where(seen, inverse, 1.0)
    stream_gain = jnp.where(seen, wide_vec[0], 1.0)
    stream_shift = jnp.where(seen, wide_vec[1], 0.0)
    raw = jnp.concatenate([data_own, data_other], axis=0)
    coefs = jnp.stack(
        [stream_mean, stream_inverse, stream_gain, stream_shift]
        + [jnp.full((width,), jnp.where(seen, 1.0, 0.0))]
    )
    coefs = jnp.pad(coefs, ((0, 3), (0, 0)))
    position = jnp.arange(count, dtype=jnp.int32)
    lengths_both = jnp.concatenate([lengths, length_other])
    keep_pages = (position[None, :] < lengths_both[:, None]).astype(F32).reshape(tokens, 1)
    keep_rows = jnp.where(seen, 1.0, keep_pages)
    valid = jnp.where(seen, count, lengths_both).astype(jnp.int32)
    grid_x = position % VCOLS * (NB // VCOLS) + NB // VCOLS // 2
    grid_y = position // VCOLS * (NB // VROWS) + NB // VROWS // 2
    boxes = jnp.concatenate([text_boxes, boxes_other], axis=0)
    boxes = jnp.where(seen, jnp.stack([grid_x, grid_y])[None], boxes)
    both = jnp.concatenate(
        [
            (boxes[:, k, :].reshape(tokens, 1) == jnp.arange(NB)[None, :]).astype(BF)
            for k in range(2)
        ],
        axis=1,
    )
    base = base_rows(tables)

    rows_one = rows_rest = 2 * rows_a
    where_rest = jnp.arange(chips, dtype=jnp.int32)
    if rows_one % 16:
        whole_one = [in_order(halves[k], sources[k], 0, weight_rows) for k in range(2)]
        whole_one, rows_one = grouped(jnp.concatenate(whole_one, axis=2), rows_one, 3)
        wide_one, sources = [whole_one], [jnp.zeros((1,), jnp.int32)] * 2
        wide_rest, rows_rest = grouped(wide_rest, rows_rest, 5, 2 * rows_o)
        where_rest = jnp.zeros((1,), jnp.int32)
    else:
        wide_one = halves[0] + halves[1]
    wide_rest = [wide_rest]
    vecs = jnp.pad(wide_vec, ((0, 1), (0, 0)))

    projected, weight_qkv, normed, inputs, joint, plain = project_call(
        sources, wide_one, rows_one, raw, both, wide_spatial, coefs
    )
    mixed, log_total = attend_call(valid, projected, both, base, count)
    lefts, both_t = turn_call(joint, plain, mixed, both)
    att, att_low, weight_out = output_call(
        where_rest, wide_rest, rows_rest, mixed, keep_rows, (lefts,)
    )
    att_other = swap(att_low)

    u, u_low, hat_one, scale_one, active, slope, weight_in = feed_call(
        where_rest, wide_rest, rows_rest, inputs, att, att_other, vecs, wide_bias
    )
    cot = jnp.concatenate([cot_own, cot_other], axis=0)
    out, dy, dff, close_sums, weight_second = close_call(
        where_rest, wide_rest, rows_rest, active, u, cot, keep_rows, vecs
    )

    slots = slot_table()
    d_out = second_call(jnp.arange(chips, dtype=jnp.int32), active, dff, chips)
    d_pre, d_pre_low, d_in, d_bias, pre_sums = feed_back_call(
        slots, u_low, dff, weight_second.reshape(hidden, width),
        weight_in.reshape(-1, width, width), slope, dy, hat_one, scale_one, vecs, chips,
        (d_out,),
    )
    d_pre_other = swap(d_pre_low)

    d_mixed, d_att = middle_call(d_pre, d_pre_other, keep_rows, weight_out.reshape(width, width))
    weight_qkv = weight_qkv.reshape(3, width, width)
    back = functools.partial(attend_back_call, valid)
    shared = (both, both_t, base, count)
    half_one, tables_one = back(projected, d_mixed, mixed, log_total, *shared, 0, H // 4)
    turned = slot_table(True)
    one_a, one_b = grads_one_call(slots, turned, lefts, half_one, d_att, chips)
    one_a, one_b = one_a.reshape(chips, -1, width // 2), one_b.reshape(chips, -1, width // 2)
    half_two, tables_two = back(
        projected, d_mixed, mixed, log_total, *shared, H // 4, H // 4, (one_b,)
    )
    column_in = scatter_plane(d_in, (half_two,))
    near_a = scatter_step(one_a, "x", (half_two,))
    near_b = scatter_step(one_b, "y", (half_two,))
    early = jnp.concatenate(
        [
            jnp.zeros((2, width), F32), pre_sums[:2], close_sums[:3], jnp.zeros((1, width), F32),
            d_bias.reshape(-1, width),
            table_sums(jnp.concatenate([tables_one, tables_two], axis=0)).reshape(-1, width),
        ],
        axis=0,
    )
    little_rows = early.shape[0]
    early = jnp.pad(early, ((0, -little_rows % 8), (0, 0)))
    d_two, d_three, grad_rows = grads_two_call(
        slots, turned, lefts, half_one, half_two, weight_qkv, d_pre, normed,
        both_t, coefs, early, chips, (column_in, near_a, near_b),
    )

    piece = 2 * rows_a
    half = width // 2
    sum_out = lax.psum_scatter(d_out, CHIP).astype(F32)
    sum_in = scatter_line(column_in, (d_two,))
    column_one = jnp.concatenate([scatter_step(near_a, "y", (d_two,)), scatter_step(near_b, "x", (d_two,))], axis=1)
    near_two = scatter_step(d_two, "x", (sum_in, column_one))
    near_three = scatter_step(d_three, "y", (sum_in, column_one))
    sum_in = sum_in.reshape(-1, piece, half).transpose(1, 0, 2).reshape(piece, hidden)
    sum_one = scatter_line(column_one)
    column_late = jnp.concatenate(
        [scatter_step(near_two, "y", (sum_one,)), scatter_step(near_three, "x", (sum_one,))], axis=1
    )
    sum_one = sum_one.reshape(5, piece, half)
    near = both.shape[1] // chips
    squares = jnp.sum(sum_out * sum_out) + jnp.sum(sum_in * sum_in) + jnp.sum(sum_one * sum_one)
    own_late = late_call(column_late, squares, chips, piece, near // 2)
    other_late = swap(own_late)

    def own_rows(value, axis):
        first, second = jnp.split(value, 2, axis=axis)
        return trade(first, second)

    def by_stream(own, other):
        return jnp.where(seen, jnp.stack([own, other]), jnp.stack([other, own]))

    def little_of(late):
        rows = late[3 * piece + 2 * near : late.shape[0] - 8].reshape(2, -1, half)
        return jnp.concatenate([rows[0], rows[1]], axis=-1)

    little = by_stream(little_of(own_late), little_of(other_late))
    member = 2 * chip_of(0, 0, 0) + core
    vec_sum = lax.dynamic_slice_in_dim(little[:, :7], member * vectors.shape[1], vectors.shape[1], 2)
    grad_vec = jnp.stack(
        [vec_sum[0, 0], vec_sum[0, 1]]
        + [vec_sum[s, k + m] for k in (2, 4) for s in range(2) for m in range(2)]
        + [vec_sum[0, 6], vec_sum[1, 6]]
    )
    bias_lines = hidden // width
    bias_sum = little[:, 8 : 8 + bias_lines].reshape(2, hidden)
    grad_bias = lax.dynamic_slice_in_dim(bias_sum, member * bias_in.shape[1], bias_in.shape[1], 1)
    pos_sum = little[:, 8 + bias_lines : little_rows].reshape(2, H, 3, NR).transpose(0, 2, 1, 3)
    grad_pos = lax.dynamic_slice_in_dim(pos_sum, member * pos_tables.shape[3], pos_tables.shape[3], 3)

    tile = chip_squares_call(own_late, other_late, 3 * piece, 3 * piece + 2 * near)
    tile = functools.reduce(jnp.add, around(tile))
    norm = functools.reduce(jnp.add, line_of(tile))
    grad_norm = jnp.sqrt(norm[0, 0])

    out_own, out_other = out[:count], swap(out[count:])
    grad_own, grad_other = grad_rows[:count], swap(grad_rows[count:])
    out_visual = mine_of(out_own, out_other)[None]
    out_text = mine_of(out_other, out_own)[None]
    grad_visual = mine_of(grad_own, grad_other)[None]
    grad_text = mine_of(grad_other, grad_own)[None]

    def turned_pos(value):
        return jnp.swapaxes(value, 2, 3)

    groups = (
        (attn_w, attn_mom, attn_sec),
        (ffn_in, in_mom, in_sec) + tuple(own_rows(sum_in, 0)),
        (ffn_out, out_mom, out_sec) + tuple(own_rows(sum_out, 0)),
        (bias_in, bias_mom, bias_sec, grad_bias),
        (vectors, vec_mom, vec_sec, grad_vec),
        tuple(turned_pos(part) for part in (pos_tables, pos_mom, pos_sec, grad_pos)),
        (spatial, spatial_mom, spatial_sec),
    )
    new = adam_call(
        norm, seen.astype(jnp.int32).reshape(1), piece, near // 2,
        (*own_rows(sum_one, 1), own_late, other_late), groups,
    )
    results = [out_visual, out_text, grad_visual, grad_text, grad_norm] + list(new)
    for index in range(5 + 18, 5 + 21):
        results[index] = turned_pos(results[index])
    return tuple(results)


def solution(mesh):
    devices = mesh.devices.reshape(-1)
    chips = devices.size // 2
    deep = 4 if chips % 4 == 0 else 1
    side = int(round((chips // deep) ** 0.5))
    if deep * side * side != chips:
        deep, side = chips, 1
    fine = Mesh(devices.reshape(deep, side, side, 2), AXES)
    every = AXES
    data = P(every, None, None)
    in_specs = (
        data, data, P(every), data, data, data,
        P(None, None, every, None), P(None, every, None), P(None, every, None),
        P(None, every), P(None, every), P(None, None, None, every), P(None, every, None),
        P(None, None, every, None), P(None, None, every, None),
        P(None, every, None), P(None, every, None), P(None, every, None), P(None, every, None),
        P(None, every), P(None, every), P(None, every), P(None, every),
        P(None, None, None, every), P(None, None, None, every),
        P(None, every, None), P(None, every, None),
    )
    weights = P(None, None, every, None)
    rows = P(None, every, None)
    flat = P(None, every)
    last = P(None, None, None, every)
    out_specs = (
        (data, data, data, data, P())
        + (weights,) * 4 + (rows,) * 8 + (flat,) * 6 + (last,) * 3 + (rows,) * 3
    )
    return jax.shard_map(body, mesh=fine, in_specs=in_specs, out_specs=out_specs, check_vma=False)
```

```python
import functools

import jax
import jax.numpy as jnp
import numpy as np
from jax import lax
from jax.experimental import pallas as pl
from jax.experimental.pallas import tpu as pltpu
from jax.sharding import Mesh
from jax.sharding import PartitionSpec as P

H = 12
HD = 64
VROWS = 16
VCOLS = 32
NB = 128
NR = 128
STEP = 10

EPSILON = 1e-05
NEGATIVE = -1000000000.0
CLIP = 1.0
BETA_ONE = 0.9
BETA_TWO = 0.95
ADAM_EPS = 1e-08
DECAY = 0.1
RATE_ATTN = 0.15
RATE_FEED = 0.04
RATE_OTHER = 0.2

BF = jnp.bfloat16
F32 = jnp.float32
AXES = ("z", "y", "x", "c")
CHIP = ("z", "y", "x")
BLOCK = 64
VMEM_LIMIT = 56 * 1024 * 1024
NT = (((1,), (1,)), ((), ()))


def cost(microseconds):
    return pl.CostEstimate(
        flops=int(microseconds * 0.1e9), bytes_accessed=int(microseconds * 3.2 * 0.1e6), transcendentals=0
    )


def params_of():
    return pltpu.CompilerParams(vmem_limit_bytes=VMEM_LIMIT)


def held(others):
    return [pl.BlockSpec(memory_space=pl.ANY)] * len(others)


def waiting(kernel, count, others):
    def run(*refs):
        kernel(*refs[:count], *refs[count + others :])

    return run


def dot(left, right):
    return jnp.dot(left, right, preferred_element_type=F32)


def dot_nt(left, right):
    return lax.dot_general(left, right, NT, preferred_element_type=F32)


def swap(value):
    return lax.ppermute(value, "c", [(0, 1), (1, 0)])


def shift(value, axis, step):
    size = lax.axis_size(axis)
    return lax.ppermute(value, axis, [(i, (i + step) % size) for i in range(size)])


def diagonal(value, step_y, step_x):
    ny, nx = lax.axis_size("y"), lax.axis_size("x")
    pairs = [
        (y * nx + x, (y + step_y) % ny * nx + (x + step_x) % nx)
        for y in range(ny)
        for x in range(nx)
    ]
    return lax.ppermute(value, ("y", "x"), pairs)


def after(value, others):
    return lax.optimization_barrier((value, others))[0]


def chip_of(dz, dy, dx):
    nz, ny, nx = (lax.axis_size(a) for a in CHIP)
    z = (lax.axis_index("z") - dz) % nz
    y = (lax.axis_index("y") - dy) % ny
    x = (lax.axis_index("x") - dx) % nx
    return (z * ny + y) * nx + x


def around(value):
    steps = [(y, x) for y in range(lax.axis_size("y")) for x in range(lax.axis_size("x"))]
    return [value] + [diagonal(value, sy, sx) for sy, sx in steps[1:]]


def plane_steps():
    return [(y, x) for y in range(lax.axis_size("y")) for x in range(lax.axis_size("x"))]


def line_of(piece):
    return [piece] + [shift(piece, "z", k) for k in range(1, lax.axis_size("z"))]


def sources_of():
    nz = lax.axis_size("z")
    return jnp.stack([chip_of(k, sy, sx) for sy, sx in plane_steps() for k in range(nz)]).astype(
        jnp.int32
    )


def relay(piece):
    line = jnp.stack(line_of(piece))
    nz = line.shape[0]
    sizes = {"x": lax.axis_size("x"), "y": lax.axis_size("y")}
    half = line.shape[-1] // 2
    halves, sources = [], []
    for part, (first, second) in enumerate((("x", "y"), ("y", "x"))):
        moved = line[..., half * part : half * part + half]
        near = jnp.concatenate([moved] + [shift(moved, first, k) for k in range(1, sizes[first])], axis=0)
        halves.append([near] + [shift(near, second, k) for k in range(1, sizes[second])])
        sources.append(
            [
                chip_of(k, two, one) if first == "x" else chip_of(k, one, two)
                for two in range(sizes[second])
                for one in range(sizes[first])
                for k in range(nz)
            ]
        )
    return halves, [jnp.stack(source).astype(jnp.int32) for source in sources]


def inverse_of(where):
    spots = jnp.arange(where.shape[0], dtype=jnp.int32)
    return jnp.sum(jnp.where(where[None, :] == spots[:, None], spots[None, :], 0), axis=1)


def in_order(stacks, where, begin, end):
    found = jnp.concatenate([part[:, begin:end] for part in stacks], axis=0)
    return jnp.take(found, inverse_of(where), axis=0)


def grouped(whole, rows, groups, lead=0):
    width = whole.shape[2]
    first = whole[:, :lead].reshape(-1, width)
    others = whole[:, lead:].reshape(-1, groups, rows, width).transpose(1, 0, 2, 3).reshape(-1, width)
    return jnp.concatenate([first, others], axis=0)[None], others.shape[0] // groups


def place(where_ref, refs, target, begin=0):
    count, _, width = refs[0].shape
    for index, ref in enumerate(refs):
        for k in range(count):
            target[where_ref[index * count + k], :, begin : begin + width] = ref[k]


def slot_table(turned=False):
    nz, ny, nx = (lax.axis_size(a) for a in CHIP)
    chips = jnp.arange(nz * ny * nx)
    zr = (chips // (ny * nx) - lax.axis_index("z")) % nz
    yr = (chips // nx % ny - lax.axis_index("y")) % ny
    xr = (chips % nx - lax.axis_index("x")) % nx
    if turned:
        return ((xr * ny + yr) * nz + zr).astype(jnp.int32)
    return ((yr * nx + xr) * nz + zr).astype(jnp.int32)


def sum_kernel(count, *refs):
    total = refs[0][...].astype(F32)
    for ref in refs[1:count]:
        total = total + ref[...].astype(F32)
    refs[-1][...] = total.astype(refs[-1].dtype)


def sum_call(own, moved, others, kind=BF):
    shape = moved[0].shape
    steps = 2 if shape[0] % 2 == 0 else 1
    block = pl.BlockSpec((shape[0] // steps,) + shape[1:], lambda i: (i, 0, 0))
    return pl.pallas_call(
        functools.partial(sum_kernel, 1 + len(moved)),
        grid=(steps,),
        in_specs=[block] * (1 + len(moved)) + held(others),
        out_specs=block,
        out_shape=jax.ShapeDtypeStruct(shape, kind),
        compiler_params=params_of(),
        name="sum",
        cost_estimate=cost(2),
    )(own, *moved, *others)


def scatter_plane(slots, others=()):
    nz = lax.axis_size("z")
    moved = [
        diagonal(slots[nz * index : nz * index + nz], sy, sx)
        for index, (sy, sx) in enumerate(plane_steps())
        if index
    ]
    return sum_call(slots, moved, others)


def scatter_step(slots, axis, others=()):
    size = lax.axis_size(axis)
    count = slots.shape[0] // size
    moved = [shift(slots[count * k : count * k + count], axis, k) for k in range(1, size)]
    return sum_call(slots, moved, others)


def scatter_line(column, others=None):
    if others is not None:
        moved = [shift(column[k : k + 1], "z", k) for k in range(1, lax.axis_size("z"))]
        return sum_call(column, moved, others, F32)[0]
    total = column[0].astype(F32)
    for k in range(1, lax.axis_size("z")):
        total = total + shift(column[k], "z", k).astype(F32)
    return total


def split_three(value):
    high = lax.reduce_precision(value, 8, 7)
    rest = value - high
    mid = lax.reduce_precision(rest, 8, 7)
    return [high.astype(BF), mid.astype(BF), (rest - mid).astype(BF)]


def join_three(parts):
    high, mid, small = (part.astype(F32) for part in parts)
    return high + (mid + small)


def base_rows(tables):
    half = NR // 2
    low, high = tables[:, :, :1], tables[:, :, -1:]
    one = tables.shape[:2]

    def many(edge, count):
        return jnp.broadcast_to(edge, one + (count,))

    line = jnp.concatenate(
        [many(high, NB - half + 1), tables[:, :, ::-1], many(low, 255 - half), many(high, 128)],
        axis=2,
    )[0]
    plane = jnp.concatenate(
        [tables[:, :, half:], many(high, NB - half), many(low, NB - half), tables[:, :, :half]], axis=2
    )
    pair = jnp.concatenate([plane[1], plane[2]], axis=1)
    rows = jnp.stack([line, pair], axis=1)
    return jnp.pad(rows, ((0, 0), (0, 6), (0, 0)))


def sum_map():
    half = NR // 2
    found = np.zeros((3, 512, 3, NR), np.float32)

    def entry(distance):
        return min(max(distance, -half), half - 1) + half

    for k in range(512):
        found[0, k, 0, entry(128 - k if k < 384 else 640 - k)] = 1.0
        lane = k % 256
        found[1, k, 1 + k // 256, entry(-lane if lane < 128 else 256 - lane)] = 1.0
        found[2, k, 0, NR - 1 if k < 256 else 0] = 1.0
    return found.reshape(3 * 512, 3 * NR)


def table_sums(sums):
    flat = sums[:, :3].reshape(sums.shape[0], -1)
    return jnp.dot(flat, jnp.asarray(sum_map()), precision=lax.Precision.HIGHEST)


def build_tables(base, strip, planes, head):
    line = jnp.broadcast_to(base[head, 0:1, :], (128, 512))
    middle = pltpu.roll(line, 0, 1, stride=1, stride_axis=0)[:, :384]
    strip[head, :, 256:640] = middle
    strip[head, :, :256] = jnp.broadcast_to(base[head, 0:1, 0:1], (128, 256))
    strip[head, :, 640:] = jnp.broadcast_to(base[head, 0:1, 383:384], (128, 256))
    for k in range(2):
        row = jnp.broadcast_to(base[head, 1:2, 256 * k : 256 * k + 256], (128, 256))
        rolled = pltpu.roll(row, 0, 1, stride=1, stride_axis=0)
        planes[head, k] = rolled[:, :128].astype(BF)


def left_side(both, planes, head):
    return jnp.concatenate(
        [
            dot(both[:, :NB], planes[head, 0]).astype(BF),
            dot(both[:, NB:], planes[head, 1]).astype(BF),
        ],
        axis=1,
    )


def head_lanes(value, head):
    lanes = lax.broadcasted_iota(jnp.int32, value.shape, 1)
    return jnp.where((lanes >= HD) == (head == 1), value, jnp.zeros_like(value))


def scores_t(raw, strip, head, valid):
    count = raw.shape[0]
    blocks = []
    for begin in range(0, count, BLOCK):
        block, row = divmod(begin, 128)
        start = 384 - 128 * block
        part = raw[begin : begin + BLOCK] + strip[head, row : row + BLOCK, start : start + count]
        rows = lax.broadcasted_iota(jnp.int32, (BLOCK, count), 0) + begin
        blocks.append(jnp.where(rows < valid, part, NEGATIVE))
    return blocks


def attend_kernel(valid_ref, q_ref, k_ref, v_ref, both_ref, base_ref, mixed_ref, log_ref, strip, planes):
    page = pl.program_id(1)

    @pl.when(page == 0)
    def _():
        for head in range(2):
            build_tables(base_ref, strip, planes, head)

    valid = valid_ref[page]
    both = both_ref[...]
    key_side = jnp.concatenate([both, k_ref[...]], axis=1)
    values_t = v_ref[...].T
    mixed = []
    raws = []
    for head in range(2):
        query_side = jnp.concatenate(
            [left_side(both, planes, head), head_lanes(q_ref[...], head)], axis=1
        )
        raws.append(dot_nt(key_side, query_side))
    for head in range(2):
        blocks = scores_t(raws[head], strip, head, valid)
        highest = jnp.max(functools.reduce(jnp.maximum, blocks), axis=0, keepdims=True)
        total, raised = None, []
        for block in blocks:
            part = jnp.exp(block - highest)
            total = part if total is None else total + part
            raised.append(part.astype(BF))
        total = jnp.sum(total, axis=0, keepdims=True)
        product = dot(values_t[HD * head : HD * head + HD], jnp.concatenate(raised, axis=0))
        mixed.append(product * (1.0 / total))
        log_ref[0, 0, head : head + 1, :] = highest + jnp.log(total)
    mixed_ref[...] = jnp.concatenate(mixed, axis=0).T.astype(BF)


def attend_call(valid, projected, both, base, count):
    pages = projected.shape[1] // count
    pairs = H // 2

    def part(index):
        return pl.BlockSpec((None, count, 128), lambda pair, page: (index, page, pair))

    return pl.pallas_call(
        attend_kernel,
        grid=(pairs, pages),
        in_specs=[
            pl.BlockSpec(memory_space=pltpu.SMEM),
            part(0),
            part(1),
            part(2),
            pl.BlockSpec((count, 2 * NB), lambda pair, page: (page, 0)),
            pl.BlockSpec((2, 8, 512), lambda pair, page: (pair, 0, 0)),
        ],
        out_specs=[
            pl.BlockSpec((count, 128), lambda pair, page: (page, pair)),
            pl.BlockSpec((1, 1, 8, count), lambda pair, page: (page, pair, 0, 0)),
        ],
        out_shape=[
            jax.ShapeDtypeStruct(projected.shape[1:], BF),
            jax.ShapeDtypeStruct((pages, pairs, 8, count), F32),
        ],
        scratch_shapes=[
            pltpu.VMEM((2, 128, count + 384), F32),
            pltpu.VMEM((2, 2, NB, NB), BF),
        ],
        compiler_params=params_of(),
        name="attend",
        cost_estimate=cost(28),
    )(valid, projected, projected, projected, both, base)


def fold_diagonals(value):
    rows, lanes = value.shape
    while rows > 1:
        rows //= 2
        value = value[:rows] + pltpu.roll(value[rows:], lanes - rows, 1)
    return value


def attend_back_kernel(
    valid_ref, q_ref, k_ref, v_ref, dm_ref, mixed_ref, log_ref, both_ref, both_t_ref, base_ref,
    grad_ref, sums_ref, strip, planes, d_strip, d_planes,
):
    page = pl.program_id(1)

    @pl.when(page == 0)
    def _():
        for head in range(2):
            build_tables(base_ref, strip, planes, head)
        d_strip[...] = jnp.zeros_like(d_strip)
        d_planes[...] = jnp.zeros_like(d_planes)

    valid = valid_ref[page]
    both = both_ref[...]
    both_t = both_t_ref[...]
    count = both.shape[0]
    key_side = jnp.concatenate([both, k_ref[...]], axis=1)
    values = v_ref[...]
    keys_t = k_ref[...].T
    d_mixed_t = dm_ref[...].T
    weighted = d_mixed_t.astype(F32) * mixed_ref[...].T.astype(F32)
    rows = lax.broadcasted_iota(jnp.int32, d_mixed_t.shape, 0)
    d_keys = d_values = None
    d_queries, masked, raws, d_all = [], [], [], []
    for head in range(2):
        masked.append(head_lanes(q_ref[...], head))
        query_side = jnp.concatenate([left_side(both, planes, head), masked[head]], axis=1)
        raws.append(dot_nt(key_side, query_side))
        d_mixed_head = jnp.where(
            (rows >= HD) == (head == 1), d_mixed_t, jnp.zeros_like(d_mixed_t)
        )
        d_all.append(dot(values, d_mixed_head))
    for head in range(2):
        masked_q, d_probs = masked[head], d_all[head]
        blocks = scores_t(raws[head], strip, head, valid)
        log_total = log_ref[0, 0, head : head + 1, :]
        inner = jnp.sum(weighted[HD * head : HD * head + HD], axis=0, keepdims=True)
        probs_low, scores_low = [], []
        for index, block in enumerate(blocks):
            begin = BLOCK * index
            row = begin % 128
            probs = jnp.exp(block - log_total)
            d_scores = probs * (d_probs[begin : begin + BLOCK] - inner)
            start = 384 - begin // 128 * 128
            d_strip[head, row : row + BLOCK, start : start + count] += d_scores
            probs_low.append(probs.astype(BF))
            scores_low.append(d_scores.astype(BF))
        probs_low = jnp.concatenate(probs_low, axis=0)
        scores_low = jnp.concatenate(scores_low, axis=0)
        part_v = dot(probs_low, head_lanes(dm_ref[...], head))
        mixed_k = dot(scores_low, jnp.concatenate([both, masked_q], axis=1))
        part_k = mixed_k[:, 2 * NB :]
        d_values = part_v if d_values is None else d_values + part_v
        d_keys = part_k if d_keys is None else d_keys + part_k
        d_queries.append(dot(keys_t[HD * head : HD * head + HD], scores_low))
        for k in range(2):
            side = mixed_k[:, NB * k : NB * k + NB].astype(BF)
            d_planes[head, k] += dot(both_t[NB * k : NB * k + NB], side)
    grad_ref[0] = (jnp.concatenate(d_queries, axis=0).T * HD ** (-0.5)).astype(BF)
    grad_ref[1] = d_keys.astype(BF)
    grad_ref[2] = d_values.astype(BF)

    @pl.when(page == pl.num_programs(1) - 1)
    def _():
        blank = jnp.zeros((128, 128), F32)
        for head in range(2):
            middle = jnp.concatenate([d_strip[head, :, 256:640], blank], axis=1)
            sums_ref[head, 0:1, :] = fold_diagonals(middle)
            for k in range(2):
                padded = jnp.concatenate([d_planes[head, k], blank], axis=1)
                sums_ref[head, 1:2, 256 * k : 256 * k + 256] = fold_diagonals(padded)
            sums_ref[head, 2:3, :256] = jnp.sum(d_strip[head, :, :256], axis=0, keepdims=True)
            sums_ref[head, 2:3, 256:] = jnp.sum(d_strip[head, :, 640:], axis=0, keepdims=True)


def attend_back_call(valid, projected, d_mixed, mixed, log_total, both, both_t, base, count, first, pairs, others=()):
    pages = projected.shape[1] // count

    def part(index):
        return pl.BlockSpec((None, count, 128), lambda pair, page: (index, page, first + pair))

    wide = pl.BlockSpec((count, 128), lambda pair, page: (page, first + pair))
    return pl.pallas_call(
        waiting(attend_back_kernel, 10, len(others)),
        grid=(pairs, pages),
        in_specs=[
            pl.BlockSpec(memory_space=pltpu.SMEM),
            part(0),
            part(1),
            part(2),
            wide,
            wide,
            pl.BlockSpec((1, 1, 8, count), lambda pair, page: (page, first + pair, 0, 0)),
            pl.BlockSpec((count, 2 * NB), lambda pair, page: (page, 0)),
            pl.BlockSpec((2 * NB, count), lambda pair, page: (0, page)),
            pl.BlockSpec((2, 8, 512), lambda pair, page: (first + pair, 0, 0)),
        ]
        + held(others),
        out_specs=[
            pl.BlockSpec((3, count, 128), lambda pair, page: (0, page, pair)),
            pl.BlockSpec((2, 8, 512), lambda pair, page: (pair, 0, 0)),
        ],
        out_shape=[
            jax.ShapeDtypeStruct(projected.shape[:2] + (128 * pairs,), BF),
            jax.ShapeDtypeStruct((2 * pairs, 8, 512), F32),
        ],
        scratch_shapes=[
            pltpu.VMEM((2, 128, count + 384), F32),
            pltpu.VMEM((2, 2, NB, NB), BF),
            pltpu.VMEM((2, 128, count + 384), F32),
            pltpu.VMEM((2, 2, NB, NB), F32),
        ],
        compiler_params=params_of(),
        name="attend_back",
        cost_estimate=cost(7 * pairs),
    )(valid, projected, projected, projected, d_mixed, mixed, log_total, both, both_t, base, *others)


def gelu_parts(before):
    bell = jnp.exp(-0.5 * before * before)
    below = 0.5 + 0.5 * lax.erf(before * (0.5**0.5))
    return before * below, below + before * (bell * 0.3989422804014327)


def normalize(rows):
    center = rows - jnp.mean(rows, axis=-1, keepdims=True)
    spread = jnp.mean(center * center, axis=-1, keepdims=True)
    scale = lax.rsqrt(spread + EPSILON)
    return center * scale, scale


def normalize_back(grad, hat, scale, gain):
    scaled = grad * gain
    first = jnp.mean(scaled, axis=-1, keepdims=True)
    second = jnp.mean(scaled * hat, axis=-1, keepdims=True)
    return scale * (scaled - first - hat * second)


def add_sums(ref, index, value, fresh):
    total = jnp.sum(value, axis=0, keepdims=True)
    ref[index : index + 1] = jnp.where(fresh, total, ref[index : index + 1] + total)


def whole_spec(shape):
    return pl.BlockSpec(shape, lambda *_: (0,) * len(shape))


def smem():
    return pl.BlockSpec(memory_space=pltpu.SMEM)


def weight_specs(stacks, rows, first):
    nz, _, width = stacks[0].shape
    return [pl.BlockSpec((nz, rows, width), lambda i: (0, first + i, 0))] * len(stacks)


def project_kernel(count, one_ref, two_ref, raw_ref, both_ref, space_ref, coef_ref, *refs):
    stacks, (out_ref, wide_ref, normed_ref, inputs_ref, joint_ref, plain_ref) = refs[:count], refs[count:]
    step = pl.program_id(0)

    @pl.when(step == 0)
    def _():
        normed = (raw_ref[...].astype(F32) - coef_ref[0:1]) * coef_ref[1:2]
        inputs = normed * coef_ref[2:3] + coef_ref[3:4]
        normed_ref[...] = normed
        inputs_ref[...] = inputs
        plain_ref[...] = inputs.astype(BF)
        joint_ref[...] = (inputs + dot(both_ref[...], space_ref[...])).astype(BF)

    if two_ref.shape[0] == 1:
        place(one_ref, stacks, wide_ref.at[0])
    else:
        place(one_ref, stacks[: count // 2], wide_ref.at[0])
        place(two_ref, stacks[count // 2 :], wide_ref.at[0], wide_ref.shape[3] // 2)
    width = raw_ref.shape[1]
    weight = wide_ref[0].reshape(width, width)
    rows = jnp.where(step == 2, plain_ref[...], joint_ref[...])
    factor = jnp.where(step == 0, HD ** (-0.5), 1.0)
    out_ref[0] = (dot(rows, weight) * factor).astype(BF)


def project_call(sources, stacks, rows, raw, both, space, coefs):
    tokens, width = raw.shape
    chips = sources[0].shape[0]
    whole = whole_spec((tokens, width))
    return pl.pallas_call(
        functools.partial(project_kernel, len(stacks)),
        grid=(3,),
        in_specs=[smem(), smem(), whole, whole_spec(both.shape), whole_spec(space.shape)]
        + [whole_spec(coefs.shape)]
        + weight_specs(stacks, rows, 0),
        out_specs=[
            pl.BlockSpec((1, tokens, width), lambda i: (i, 0, 0)),
            pl.BlockSpec((1, chips, rows, width), lambda i: (i, 0, 0, 0)),
            whole,
            whole,
            whole,
            whole,
        ],
        out_shape=[
            jax.ShapeDtypeStruct((3, tokens, width), BF),
            jax.ShapeDtypeStruct((3, chips, rows, width), BF),
            jax.ShapeDtypeStruct((tokens, width), F32),
            jax.ShapeDtypeStruct((tokens, width), F32),
            jax.ShapeDtypeStruct((tokens, width), BF),
            jax.ShapeDtypeStruct((tokens, width), BF),
        ],
        compiler_params=params_of(),
        name="project",
        cost_estimate=cost(12),
    )(*sources, raw, both, space, coefs, *stacks)


def output_kernel(count, where_ref, mixed_ref, keep_ref, *refs):
    stacks, (att_ref, low_ref, wide_ref) = refs[:count], refs[count:]
    place(where_ref, stacks, wide_ref)
    width = mixed_ref.shape[1]
    att = dot(mixed_ref[...], wide_ref[...].reshape(width, width)) * keep_ref[...]
    att_ref[...] = att
    low_ref[...] = att.astype(BF)


def output_call(where, stacks, rows, mixed, keep, others):
    tokens, width = mixed.shape
    nz = stacks[0].shape[0]
    chips = len(stacks) * nz
    return pl.pallas_call(
        waiting(functools.partial(output_kernel, len(stacks)), 3 + len(stacks), len(others)),
        grid=(1,),
        in_specs=[smem(), whole_spec((tokens, width)), whole_spec((tokens, 1))]
        + weight_specs(stacks, rows, 8)
        + held(others),
        out_specs=[
            whole_spec((tokens, width)),
            whole_spec((tokens, width)),
            whole_spec((chips, rows, width)),
        ],
        out_shape=[
            jax.ShapeDtypeStruct((tokens, width), F32),
            jax.ShapeDtypeStruct((tokens, width), BF),
            jax.ShapeDtypeStruct((chips, rows, width), BF),
        ],
        compiler_params=params_of(),
        name="output",
        cost_estimate=cost(5),
    )(where, mixed, keep, *stacks, *others)


def feed_kernel(count, where_ref, inputs_ref, own_ref, other_ref, vec_ref, bias_ref, *refs):
    stacks = refs[:count]
    u_ref, low_ref, hat_ref, scale_ref, active_ref, slope_ref, wide_ref = refs[count:]
    half = inputs_ref.shape[0] // 2

    @pl.when(pl.program_id(0) == 0)
    def _():
        for page in range(2):
            here = pl.ds(half * page, half)
            there = pl.ds(half * (1 - page), half)
            rows = inputs_ref[here, :] + own_ref[here, :] + other_ref[there, :].astype(F32)
            hat, scale = normalize(rows)
            u = hat * vec_ref[2:3] + vec_ref[3:4]
            u_ref[here, :] = u
            low_ref[here, :] = u.astype(BF)
            hat_ref[here, :] = hat
            scale_ref[here, :] = scale

    place(where_ref, stacks, wide_ref.at[0])
    width = inputs_ref.shape[1]
    weight = wide_ref[0].reshape(width, width)
    count = low_ref.shape[0] // 4
    for part in range(4):
        here = pl.ds(count * part, count)
        before = dot(low_ref[here, :], weight) + bias_ref[...]
        active, slope = gelu_parts(before)
        active_ref[here, :] = active.astype(BF)
        slope_ref[here, :] = slope.astype(BF)


def feed_call(where, stacks, rows, inputs, own, other, vecs, bias):
    tokens, width = inputs.shape
    hidden = bias.shape[1]
    nz = stacks[0].shape[0]
    chips = len(stacks) * nz
    whole = whole_spec((tokens, width))
    block = pl.BlockSpec((tokens, width), lambda i: (0, i))
    return pl.pallas_call(
        functools.partial(feed_kernel, len(stacks)),
        grid=(hidden // width,),
        in_specs=[smem(), whole, whole, whole, whole_spec(vecs.shape)]
        + [pl.BlockSpec((1, width), lambda i: (0, i))]
        + weight_specs(stacks, rows, 4),
        out_specs=[
            whole,
            whole,
            whole,
            whole_spec((tokens, 1)),
            block,
            block,
            pl.BlockSpec((1, chips, rows, width), lambda i: (i, 0, 0, 0)),
        ],
        out_shape=[
            jax.ShapeDtypeStruct((tokens, width), F32),
            jax.ShapeDtypeStruct((tokens, width), BF),
            jax.ShapeDtypeStruct((tokens, width), F32),
            jax.ShapeDtypeStruct((tokens, 1), F32),
            jax.ShapeDtypeStruct((tokens, hidden), BF),
            jax.ShapeDtypeStruct((tokens, hidden), BF),
            jax.ShapeDtypeStruct((hidden // width, chips, rows, width), BF),
        ],
        compiler_params=params_of(),
        name="feed",
        cost_estimate=cost(24),
    )(where, inputs, own, other, vecs, bias, *stacks)


def close_kernel(count, where_ref, active_ref, u_ref, cot_ref, keep_ref, vec_ref, *refs):
    stacks = refs[:count]
    out_ref, dy_ref, low_ref, sums_ref, wide_ref = refs[count:]
    step = pl.program_id(0)

    @pl.when(step == 0)
    def _():
        place(where_ref, stacks, wide_ref)

    weight = wide_ref[...].reshape(-1, u_ref.shape[1])
    rows = u_ref[...] + (dot(active_ref[...], weight) + vec_ref[6:7])
    hat, scale = normalize(rows)
    gain = vec_ref[4:5]
    keep = keep_ref[...]
    out_ref[...] = ((hat * gain + vec_ref[5:6]) * keep).astype(BF)
    cot = cot_ref[...].astype(F32) * keep
    dy = normalize_back(cot, hat, scale, gain)
    low = dy.astype(BF)
    dy_ref[...] = dy
    low_ref[...] = low
    add_sums(sums_ref, 0, cot * hat, step == 0)
    add_sums(sums_ref, 1, cot, step == 0)
    add_sums(sums_ref, 2, low.astype(F32), step == 0)


def close_call(where, stacks, rows, active, u, cot, keep, vecs):
    tokens, width = u.shape
    hidden = active.shape[1]
    nz = stacks[0].shape[0]
    groups = 4
    chips = len(stacks) * nz
    steps = 4
    block = pl.BlockSpec((tokens // steps, width), lambda i: (i, 0))
    return pl.pallas_call(
        functools.partial(close_kernel, len(stacks)),
        grid=(steps,),
        in_specs=[
            smem(),
            pl.BlockSpec((tokens // steps, hidden), lambda i: (i, 0)),
            block,
            block,
            pl.BlockSpec((tokens // steps, 1), lambda i: (i, 0)),
            whole_spec(vecs.shape),
        ]
        + [whole_spec((nz, groups * rows, width))] * len(stacks),
        out_specs=[
            block,
            block,
            block,
            whole_spec((8, width)),
            whole_spec((chips, groups * rows, width)),
        ],
        out_shape=[
            jax.ShapeDtypeStruct((tokens, width), BF),
            jax.ShapeDtypeStruct((tokens, width), F32),
            jax.ShapeDtypeStruct((tokens, width), BF),
            jax.ShapeDtypeStruct((8, width), F32),
            jax.ShapeDtypeStruct((chips, groups * rows, width), BF),
        ],
        compiler_params=params_of(),
        name="close",
        cost_estimate=cost(13),
    )(where, active, u, cot, keep, vecs, *stacks)


def store_slots(slots_ref, out_ref, total, first=0):
    rows = out_ref.shape[1]
    for index in range(total.shape[0] // rows):
        part = total[index * rows : index * rows + rows].astype(BF)
        out_ref[slots_ref[first + index]] = part


def second_kernel(slots_ref, active_ref, low_ref, out_ref):
    total = dot(active_ref[...].T, low_ref[...])
    count = total.shape[0] // out_ref.shape[1]
    store_slots(slots_ref, out_ref, total, pl.program_id(0) * count)


def second_call(slots, active, low, chips):
    tokens, width = low.shape
    hidden = active.shape[1]
    return pl.pallas_call(
        second_kernel,
        grid=(hidden // width,),
        in_specs=[
            smem(),
            pl.BlockSpec((tokens, width), lambda i: (0, i)),
            whole_spec((tokens, width)),
        ],
        out_specs=whole_spec((chips, hidden // chips, width)),
        out_shape=jax.ShapeDtypeStruct((chips, hidden // chips, width), BF),
        compiler_params=params_of(),
        name="second",
        cost_estimate=cost(10),
    )(slots, active, low)


def feed_back_kernel(
    slots_ref, rows_ref, low_ref, second_ref, first_ref, slope_ref, dy_ref, hat_ref, scale_ref, vec_ref,
    dpre_ref, dlow_ref, dfirst_ref, dbias_ref, sums_ref, rows_t, total_ref,
):
    step = pl.program_id(0)

    @pl.when(step == 0)
    def _():
        rows_t[...] = rows_ref[...].T
        total_ref[...] = dy_ref[...]

    d_active = dot_nt(low_ref[...], second_ref[...])
    d_before = (slope_ref[...].astype(F32) * d_active).astype(BF)
    dbias_ref[0] = jnp.sum(d_before.astype(F32), axis=0, keepdims=True)
    total_ref[...] += dot_nt(d_before, first_ref[0])
    total = dot(rows_t[...], d_before)
    chips, piece = dfirst_ref.shape[0], dfirst_ref.shape[1] // 2
    half = dfirst_ref.shape[2]
    for chip in range(chips):
        part = total[chip * piece : chip * piece + piece].astype(BF)
        dfirst_ref[slots_ref[chip], :piece] = part[:, :half]
        dfirst_ref[slots_ref[chip], piece:] = part[:, half:]

    @pl.when(step == pl.num_programs(0) - 1)
    def _():
        grad = total_ref[...]
        hat = hat_ref[...]
        d_pre = normalize_back(grad, hat, scale_ref[...], vec_ref[2:3])
        dpre_ref[...] = d_pre
        dlow_ref[...] = d_pre.astype(BF)
        add_sums(sums_ref, 0, grad * hat, True)
        add_sums(sums_ref, 1, grad, True)


def feed_back_call(slots, rows, low, second, first, slope, dy, hat, scale, vecs, chips, others):
    tokens, width = rows.shape
    hidden = second.shape[0]
    piece = width // chips
    whole = whole_spec((tokens, width))
    return pl.pallas_call(
        waiting(feed_back_kernel, 10, len(others)),
        grid=(hidden // width,),
        in_specs=[
            smem(),
            whole,
            whole,
            pl.BlockSpec((width, width), lambda i: (i, 0)),
            pl.BlockSpec((1, width, width), lambda i: (i, 0, 0)),
            pl.BlockSpec((tokens, width), lambda i: (0, i)),
            whole,
            whole,
            whole_spec((tokens, 1)),
            whole_spec(vecs.shape),
        ]
        + held(others),
        out_specs=[
            whole,
            whole,
            pl.BlockSpec((chips, 2 * piece, width // 2), lambda i: (0, i, 0)),
            pl.BlockSpec((1, 1, width), lambda i: (i, 0, 0)),
            whole_spec((8, width)),
        ],
        out_shape=[
            jax.ShapeDtypeStruct((tokens, width), F32),
            jax.ShapeDtypeStruct((tokens, width), BF),
            jax.ShapeDtypeStruct((chips, 2 * piece * (hidden // width), width // 2), BF),
            jax.ShapeDtypeStruct((hidden // width, 1, width), F32),
            jax.ShapeDtypeStruct((8, width), F32),
        ],
        scratch_shapes=[pltpu.VMEM((width, tokens), BF), pltpu.VMEM((tokens, width), F32)],
        compiler_params=params_of(),
        name="feed_back",
        cost_estimate=cost(26),
    )(slots, rows, low, second, first, slope, dy, hat, scale, vecs, *others)


def middle_kernel(own_ref, other_ref, keep_ref, weight_ref, dmixed_ref, low_ref):
    half = own_ref.shape[0] // 2
    for page in range(2):
        here = pl.ds(half * page, half)
        there = pl.ds(half * (1 - page), half)
        merged = (own_ref[here, :] + other_ref[there, :].astype(F32)) * keep_ref[here, :]
        low_ref[here, :] = merged.astype(BF)
    dmixed_ref[...] = dot_nt(low_ref[...], weight_ref[...]).astype(BF)


def middle_call(own, other, keep, weight):
    tokens, width = own.shape
    whole = whole_spec((tokens, width))
    return pl.pallas_call(
        middle_kernel,
        grid=(1,),
        in_specs=[whole, whole, whole_spec((tokens, 1)), whole_spec((width, width))],
        out_specs=[whole, whole],
        out_shape=[jax.ShapeDtypeStruct((tokens, width), BF)] * 2,
        compiler_params=params_of(),
        name="middle",
        cost_estimate=cost(6),
    )(own, other, keep, weight)


def turn_kernel(joint_ref, plain_ref, mixed_ref, both_ref, lefts_ref, both_t_ref):
    for index, ref in enumerate((joint_ref, plain_ref, mixed_ref)):
        lefts_ref[index] = ref[...].T
    both_t_ref[...] = both_ref[...].T


def turn_call(joint, plain, mixed, both):
    tokens, width = joint.shape
    whole = whole_spec((tokens, width))
    return pl.pallas_call(
        turn_kernel,
        grid=(1,),
        in_specs=[whole, whole, whole, whole_spec(both.shape)],
        out_specs=[whole_spec((3, width, tokens)), whole_spec(both.shape[::-1])],
        out_shape=[
            jax.ShapeDtypeStruct((3, width, tokens), BF),
            jax.ShapeDtypeStruct(both.shape[::-1], BF),
        ],
        compiler_params=params_of(),
        name="turn",
        cost_estimate=cost(8),
    )(joint, plain, mixed, both)


def store_rows(slots_ref, out_ref, start, total):
    chips = out_ref.shape[0]
    piece = total.shape[0] // chips
    for chip in range(chips):
        low = total[chip * piece : chip * piece + piece].astype(BF)
        out_ref[slots_ref[chip], start : start + piece] = low


def grads_one_kernel(slots_ref, turned_ref, left_ref, grad_ref, datt_ref, dwa_ref, dwb_ref):
    step = pl.program_id(0)
    total = dot(left_ref[0], jnp.where(step < 3, grad_ref[0], datt_ref[...]))
    pl.when(step < 2)(functools.partial(store_rows, turned_ref, dwa_ref, 0, total))
    pl.when(step >= 2)(functools.partial(store_rows, slots_ref, dwb_ref, 0, total))


def grads_one_call(slots, turned, lefts, grad, datt, chips):
    _, width, tokens = lefts.shape
    half = width // 2
    piece = width // chips
    return pl.pallas_call(
        grads_one_kernel,
        grid=(5,),
        in_specs=[
            smem(),
            smem(),
            pl.BlockSpec((1, width, tokens), lambda i: (jnp.where(i < 2, 0, jnp.minimum(i - 1, 2)), 0, 0)),
            pl.BlockSpec((1, tokens, half), lambda i: (jnp.minimum(i, 2), 0, 0)),
            pl.BlockSpec((tokens, half), lambda i: (0, jnp.maximum(i - 3, 0))),
        ],
        out_specs=[
            pl.BlockSpec((chips, None, piece, half), lambda i: (0, jnp.minimum(i, 1), 0, 0)),
            pl.BlockSpec((chips, None, piece, half), lambda i: (0, jnp.maximum(i - 2, 0), 0, 0)),
        ],
        out_shape=[
            jax.ShapeDtypeStruct((chips, 2, piece, half), BF),
            jax.ShapeDtypeStruct((chips, 3, piece, half), BF),
        ],
        compiler_params=params_of(),
        name="grads_one",
        cost_estimate=cost(9),
    )(slots, turned, lefts, grad, datt)


def grads_two_kernel(
    slots_ref, turned_ref, left_ref, near_ref, grad_ref, weight_ref, dpre_ref, normed_ref, both_t_ref,
    coef_ref, early_ref, dwa_ref, dwb_ref, rows_ref, total_ref,
):
    step = pl.program_id(0)
    chips, half = dwa_ref.shape[0], dwa_ref.shape[2]
    piece = dwa_ref.shape[1] // 2
    space_size = both_t_ref.shape[0]
    near = space_size // (2 * chips)
    grad = grad_ref[0]
    total = dot(left_ref[0], grad)
    part = dot_nt(jnp.concatenate([near_ref[0], grad], axis=1), weight_ref[0])

    @pl.when(step == 0)
    def _():
        store_rows(turned_ref, dwa_ref, 0, total)
        total_ref[...] = part

    @pl.when(step == 1)
    def _():
        store_rows(turned_ref, dwa_ref, piece, total)
        joint = total_ref[...] + part
        total_ref[...] = joint + dpre_ref[...]
        space = dot(both_t_ref[...], joint.astype(BF)).astype(BF)
        for chip in range(chips):
            for k in range(2):
                begin = k * space_size // 2 + chip * near
                for side in range(2):
                    start = piece + (2 * side + k) * near
                    dwb_ref[slots_ref[chip], start : start + near] = space[
                        begin : begin + near, half * side : half * side + half
                    ]

    @pl.when(step == 2)
    def _():
        store_rows(slots_ref, dwb_ref, 0, total)
        dx = total_ref[...] + part
        rows_ref[...] = dx * coef_ref[2:3] * coef_ref[1:2]
        gain = jnp.sum(dx * normed_ref[...], axis=0, keepdims=True) * coef_ref[4:5]
        shift_row = jnp.sum(dx, axis=0, keepdims=True) * coef_ref[4:5]
        early = early_ref[...]
        place_row = lax.broadcasted_iota(jnp.int32, early.shape, 0)
        early = jnp.where(place_row == 0, gain, jnp.where(place_row == 1, shift_row, early)).astype(BF)
        start = piece + 4 * near
        count = early.shape[0]
        for chip in range(chips):
            for side in range(2):
                dwb_ref[chip, start + count * side : start + count * side + count] = early[
                    :, half * side : half * side + half
                ]


def grads_two_call(slots, turned, lefts, near, grad, weight, d_pre, normed, both_t, coefs, early, chips, others):
    _, width, tokens = lefts.shape
    half = width // 2
    whole = whole_spec((tokens, width))
    piece = width // chips
    tall = piece + 2 * (both_t.shape[0] // chips) + 2 * early.shape[0]
    return pl.pallas_call(
        waiting(grads_two_kernel, 11, len(others)),
        grid=(3,),
        in_specs=[
            smem(),
            smem(),
            pl.BlockSpec((1, width, tokens), lambda i: (i // 2, 0, 0)),
            pl.BlockSpec((1, tokens, half), lambda i: (i, 0, 0)),
            pl.BlockSpec((1, tokens, half), lambda i: (i, 0, 0)),
            pl.BlockSpec((1, width, width), lambda i: (i, 0, 0)),
            whole,
            whole,
            whole_spec(both_t.shape),
            whole_spec(coefs.shape),
            whole_spec(early.shape),
        ]
        + held(others),
        out_specs=[whole_spec((chips, 2 * piece, half)), whole_spec((chips, tall, half)), whole],
        out_shape=[
            jax.ShapeDtypeStruct((chips, 2 * piece, half), BF),
            jax.ShapeDtypeStruct((chips, tall, half), BF),
            jax.ShapeDtypeStruct((tokens, width), F32),
        ],
        scratch_shapes=[pltpu.VMEM((tokens, width), F32)],
        compiler_params=params_of(),
        name="grads_two",
        cost_estimate=cost(10),
    )(slots, turned, lefts, near, grad, weight, d_pre, normed, both_t, coefs, early, *others)


def adam(weight, grad, first, second, rate, decay):
    first_new = BETA_ONE * first + (1 - BETA_ONE) * grad
    second_new = BETA_TWO * second + (1 - BETA_TWO) * grad * grad
    ratio = (
        first_new / (1 - BETA_ONE**STEP) / (jnp.sqrt(second_new / (1 - BETA_TWO**STEP)) + ADAM_EPS)
    )
    return (first_new, second_new, weight - rate * (ratio + decay * weight))


def late_kernel(chips, piece, near, squares_ref, *refs):
    out_ref = refs[-1]
    total = refs[0][0].astype(F32)
    for ref in refs[1:-1]:
        total = total + ref[0].astype(F32)
    count = total.shape[0]
    out_ref[:count] = total
    weights = total[: 3 * piece]
    little = total[3 * piece + 4 * near :]
    squares = jnp.sum(weights * weights) + jnp.sum(little * little) / chips + squares_ref[0]
    out_ref[count:] = jnp.full((8, total.shape[1]), squares)


def late_call(column, squares, chips, piece, near):
    nz, count, half = column.shape
    moved = [shift(column[k : k + 1], "z", k) for k in range(1, nz)]
    block = whole_spec((1, count, half))
    return pl.pallas_call(
        functools.partial(late_kernel, chips, piece, near),
        grid=(1,),
        in_specs=[smem()] + [block] * nz,
        out_specs=whole_spec((count + 8, half)),
        out_shape=jax.ShapeDtypeStruct((count + 8, half), F32),
        compiler_params=params_of(),
        name="late",
        cost_estimate=cost(2),
    )(squares.reshape(1), column, *moved)


def chip_squares_kernel(begin, end, own_ref, other_ref, out_ref):
    space = own_ref[begin:end] + other_ref[begin:end]
    count = own_ref.shape[0] - 8
    both = own_ref[count:, :128] + other_ref[count:, :128]
    out_ref[...] = both + jnp.sum(space * space)


def chip_squares_call(own, other, begin, end):
    return pl.pallas_call(
        functools.partial(chip_squares_kernel, begin, end),
        grid=(1,),
        in_specs=[whole_spec(own.shape)] * 2,
        out_specs=whole_spec((8, 128)),
        out_shape=jax.ShapeDtypeStruct((8, 128), F32),
        compiler_params=params_of(),
        name="chip_squares",
        cost_estimate=cost(1),
    )(own, other)


def adam_kernel(piece, near, norm_ref, seen_ref, *refs):
    seen = seen_ref[0] == 1
    factor = CLIP / jnp.maximum(jnp.sqrt(norm_ref[0:1, 0:1]), CLIP)
    own_one, other_one, own_late, other_late = refs[:4]
    attn, feed_in, feed_out = refs[4:7], refs[7:12], refs[12:17]
    small = (refs[17:21], refs[21:25], refs[25:29])
    space, outs = refs[29:32], refs[32:]
    mine = piece // 2

    def pick(first, second):
        return jnp.where(seen, first, second)

    def step(weight, grad, first, second, rate, decay, targets, at):
        new = adam(weight[at], grad * factor, first[at], second[at], rate, decay)
        for target, value in zip(targets, new):
            target[at] = value
        if len(targets) == 4:
            targets[3][at] = new[2].astype(BF)

    def late_rows(ref, index):
        top = ref[piece * index : piece * index + mine]
        return pick(top, ref[piece * index + mine : piece * index + piece])

    half = own_one.shape[2]
    for stream in range(2):
        first = (lambda a, b: pick(a, b)) if stream == 0 else (lambda a, b: pick(b, a))
        for matrix in range(4):
            left = first(own_one[matrix], other_one[matrix])
            if matrix < 3:
                right = first(late_rows(own_late, matrix), late_rows(other_late, matrix))
            else:
                right = first(own_one[4], other_one[4])
            for side, grad in enumerate((left, right)):
                at = (stream, matrix, slice(None), slice(half * side, half * side + half))
                step(attn[0], grad, attn[1], attn[2], RATE_ATTN, DECAY, outs[:4], at)
        for group, target in ((feed_in, outs[4:8]), (feed_out, outs[8:12])):
            grad = first(group[3][...], group[4][...])
            step(group[0], grad, group[1], group[2], RATE_FEED, DECAY, target, (stream,))
    for index, group in enumerate(small):
        targets = outs[12 + 3 * index : 15 + 3 * index]
        step(group[0], group[3][...], group[1], group[2], RATE_OTHER, 0.0, targets, (slice(None),))
    for k in range(2):
        for side in range(2):
            begin = 3 * piece + (2 * side + k) * near
            total = own_late[begin : begin + near] + other_late[begin : begin + near]
            grad = pick(total[: near // 2], total[near // 2 :])
            at = (k, slice(None), slice(half * side, half * side + half))
            step(space[0], grad, space[1], space[2], RATE_OTHER, DECAY, outs[21:24], at)


def adam_call(norm, seen, piece, near, parts, groups):
    inputs = list(parts)
    shapes = []
    for index, group in enumerate(groups):
        inputs += group
        shapes += [jax.ShapeDtypeStruct(group[0].shape, F32)] * 3
        if index < 3:
            shapes.append(jax.ShapeDtypeStruct(group[0].shape, BF))
    return pl.pallas_call(
        functools.partial(adam_kernel, piece, near),
        grid=(1,),
        in_specs=[whole_spec(norm.shape), smem()]
        + [pl.BlockSpec(memory_space=pltpu.VMEM)] * len(inputs),
        out_specs=[whole_spec(shape.shape) for shape in shapes],
        out_shape=shapes,
        compiler_params=params_of(),
        name="adam",
        cost_estimate=cost(9),
    )(norm, seen, *inputs)


def body(
    visual, text, lengths, text_boxes, cot_visual, cot_text,
    attn_w, ffn_in, ffn_out, bias_in, vectors, pos_tables, spatial,
    attn_mom, attn_sec, in_mom, in_sec, out_mom, out_sec, bias_mom, bias_sec,
    vec_mom, vec_sec, pos_mom, pos_sec, spatial_mom, spatial_sec,
):
    core = lax.axis_index("c")
    seen = core == 0
    nz, ny, nx = (lax.axis_size(a) for a in CHIP)
    chips = nz * ny * nx
    devices = 2 * chips
    _, count, width = visual.shape
    tokens = 2 * count

    def mine_of(first, second):
        return jnp.where(seen, first, second)

    def trade(first, second):
        return mine_of(first, second), swap(mine_of(second, first))

    def by_core(own, other):
        return jnp.where(seen, jnp.stack([own, other]), jnp.stack([other, own]))

    attn_low = attn_w.astype(BF)
    in_low = ffn_in.astype(BF)
    out_low = ffn_out.astype(BF)
    attn_own, attn_other = trade(attn_low[0], attn_low[1])
    in_own, in_other = trade(in_low[0], in_low[1])
    out_own, out_other = trade(out_low[0], out_low[1])
    rows_a = attn_w.shape[2]
    rows_o = ffn_out.shape[1]
    hidden = ffn_in.shape[2]
    attn_piece = jnp.where(
        seen,
        jnp.concatenate([attn_own, attn_other], axis=1),
        jnp.concatenate([attn_other, attn_own], axis=1),
    )
    in_piece = by_core(in_own, in_other).reshape(2 * rows_a, hidden)
    out_piece = by_core(out_own, out_other).reshape(2 * rows_o, width)
    in_cut = in_piece.reshape(2 * rows_a, -1, width).transpose(1, 0, 2)
    out_cut = out_piece.reshape(-1, 2 * rows_a, width)

    raw_own = visual[0].astype(F32)
    sums = jnp.stack([jnp.sum(raw_own, axis=0), jnp.sum(raw_own * raw_own, axis=0)])
    vec_rows = [
        jnp.stack([vectors[0], vectors[1]] + [vectors[k + 2 * s] for k in (2, 3, 6, 7)] + [vectors[10 + s]])
        for s in range(2)
    ]

    def packed(s):
        def row(values):
            flat = values.reshape(1, -1)
            return jnp.pad(flat, ((0, 0), (0, -flat.shape[1] % width))).reshape(-1, width)

        return jnp.concatenate(
            [row(pos_tables[s].astype(BF)), row(jnp.concatenate(
                [part.reshape(1, -1) for part in split_three(vec_rows[s]) + split_three(bias_in[s])], axis=1
            ))], axis=0
        )

    pack_zero, pack_one = packed(0), packed(1)
    small_rows = pack_zero.shape[0]
    space = spatial.astype(BF).reshape(-1, width)
    space_rows = space.shape[0]
    pack_own, pack_other = trade(pack_zero, pack_one)
    space_other, sums_other = swap((space, sums))
    pack_both = by_core(pack_own, pack_other).reshape(2 * small_rows, width)
    space_both = by_core(space, space_other).reshape(2 * space_rows, width)
    small = jnp.concatenate(
        [space_both, pack_both, jnp.concatenate(split_three(sums + sums_other), axis=0)], axis=0
    )
    pad = -(small.shape[0] + 6 * rows_a) % 16
    first = jnp.concatenate(
        [attn_piece[:3].reshape(6 * rows_a, width), jnp.pad(small, ((0, pad), (0, 0)))], axis=0
    )
    rest = jnp.concatenate([out_cut, in_cut, attn_piece[3:]], axis=0).reshape(-1, width)
    wide_rest = lax.all_gather(rest, CHIP)
    halves, sources = relay(first)
    weight_rows = 6 * rows_a
    gathered = jnp.concatenate(
        [in_order(halves[k], sources[k], weight_rows, first.shape[0]) for k in range(2)], axis=2
    )
    wide_spatial = gathered[:, : 2 * space_rows].reshape(chips, 2, 2, -1, width)
    wide_spatial = wide_spatial.transpose(2, 0, 1, 3, 4).reshape(2 * NB, width)
    packs = gathered[:, 2 * space_rows : 2 * space_rows + 2 * small_rows]
    packs = packs.reshape(devices, small_rows, width)
    pos_size = pos_tables[0].size
    pos_lines = -(-pos_size // width)
    tables = packs[:, :pos_lines].reshape(devices, -1)[:, :pos_size]
    tables = tables.reshape(devices, 3, H, -1).transpose(1, 2, 0, 3).reshape(3, H, NR).astype(F32)
    params = packs[:, pos_lines:].reshape(devices, -1)
    vec_size = vec_rows[0].size
    bias_size = bias_in[0].size
    wide_vec = join_three([params[:, vec_size * k : vec_size * (k + 1)] for k in range(3)])
    wide_vec = wide_vec.reshape(devices, 7, -1).transpose(1, 0, 2).reshape(7, width)
    wide_bias = join_three(
        [params[:, 3 * vec_size + bias_size * k : 3 * vec_size + bias_size * (k + 1)] for k in range(3)]
    ).reshape(1, hidden)
    parts = gathered[:, 2 * space_rows + 2 * small_rows :]
    sums = jnp.sum(join_three([parts[:, 2 * k : 2 * k + 2] for k in range(3)]), axis=0)

    data_own, data_other = trade(visual[0], text[0])
    cot_own, cot_other = trade(cot_visual[0], cot_text[0])
    length_other, boxes_other = swap((lengths, text_boxes))
    total = count * devices
    mean = sums[0] / total
    variance = sums[1] / total - mean * mean
    inverse = lax.rsqrt(variance + EPSILON)
    stream_mean = jnp.where(seen, mean, 0.0)
    stream_inverse = jnp.where(seen, inverse, 1.0)
    stream_gain = jnp.where(seen, wide_vec[0], 1.0)
    stream_shift = jnp.where(seen, wide_vec[1], 0.0)
    raw = jnp.concatenate([data_own, data_other], axis=0)
    coefs = jnp.stack(
        [stream_mean, stream_inverse, stream_gain, stream_shift]
        + [jnp.full((width,), jnp.where(seen, 1.0, 0.0))]
    )
    coefs = jnp.pad(coefs, ((0, 3), (0, 0)))
    position = jnp.arange(count, dtype=jnp.int32)
    lengths_both = jnp.concatenate([lengths, length_other])
    keep_pages = (position[None, :] < lengths_both[:, None]).astype(F32).reshape(tokens, 1)
    keep_rows = jnp.where(seen, 1.0, keep_pages)
    valid = jnp.where(seen, count, lengths_both).astype(jnp.int32)
    grid_x = position % VCOLS * (NB // VCOLS) + NB // VCOLS // 2
    grid_y = position // VCOLS * (NB // VROWS) + NB // VROWS // 2
    boxes = jnp.concatenate([text_boxes, boxes_other], axis=0)
    boxes = jnp.where(seen, jnp.stack([grid_x, grid_y])[None], boxes)
    both = jnp.concatenate(
        [
            (boxes[:, k, :].reshape(tokens, 1) == jnp.arange(NB)[None, :]).astype(BF)
            for k in range(2)
        ],
        axis=1,
    )
    base = base_rows(tables)

    rows_one = rows_rest = 2 * rows_a
    where_rest = jnp.arange(chips, dtype=jnp.int32)
    if rows_one % 16:
        whole_one = [in_order(halves[k], sources[k], 0, weight_rows) for k in range(2)]
        whole_one, rows_one = grouped(jnp.concatenate(whole_one, axis=2), rows_one, 3)
        wide_one, sources = [whole_one], [jnp.zeros((1,), jnp.int32)] * 2
        wide_rest, rows_rest = grouped(wide_rest, rows_rest, 5, 2 * rows_o)
        where_rest = jnp.zeros((1,), jnp.int32)
    else:
        wide_one = halves[0] + halves[1]
    wide_rest = [wide_rest]
    vecs = jnp.pad(wide_vec, ((0, 1), (0, 0)))

    projected, weight_qkv, normed, inputs, joint, plain = project_call(
        sources, wide_one, rows_one, raw, both, wide_spatial, coefs
    )
    mixed, log_total = attend_call(valid, projected, both, base, count)
    lefts, both_t = turn_call(joint, plain, mixed, both)
    att, att_low, weight_out = output_call(
        where_rest, wide_rest, rows_rest, mixed, keep_rows, (lefts,)
    )
    att_other = swap(att_low)

    u, u_low, hat_one, scale_one, active, slope, weight_in = feed_call(
        where_rest, wide_rest, rows_rest, inputs, att, att_other, vecs, wide_bias
    )
    cot = jnp.concatenate([cot_own, cot_other], axis=0)
    out, dy, dff, close_sums, weight_second = close_call(
        where_rest, wide_rest, rows_rest, active, u, cot, keep_rows, vecs
    )

    slots = slot_table()
    d_out = second_call(jnp.arange(chips, dtype=jnp.int32), active, dff, chips)
    d_pre, d_pre_low, d_in, d_bias, pre_sums = feed_back_call(
        slots, u_low, dff, weight_second.reshape(hidden, width),
        weight_in.reshape(-1, width, width), slope, dy, hat_one, scale_one, vecs, chips,
        (d_out,),
    )
    d_pre_other = swap(d_pre_low)

    d_mixed, d_att = middle_call(d_pre, d_pre_other, keep_rows, weight_out.reshape(width, width))
    weight_qkv = weight_qkv.reshape(3, width, width)
    back = functools.partial(attend_back_call, valid)
    shared = (both, both_t, base, count)
    half_one, tables_one = back(projected, d_mixed, mixed, log_total, *shared, 0, H // 4)
    turned = slot_table(True)
    one_a, one_b = grads_one_call(slots, turned, lefts, half_one, d_att, chips)
    one_a, one_b = one_a.reshape(chips, -1, width // 2), one_b.reshape(chips, -1, width // 2)
    half_two, tables_two = back(
        projected, d_mixed, mixed, log_total, *shared, H // 4, H // 4, (one_b,)
    )
    column_in = scatter_plane(d_in, (half_two,))
    near_a = scatter_step(one_a, "x", (half_two,))
    near_b = scatter_step(one_b, "y", (half_two,))
    early = jnp.concatenate(
        [
            jnp.zeros((2, width), F32), pre_sums[:2], close_sums[:3], jnp.zeros((1, width), F32),
            d_bias.reshape(-1, width),
            table_sums(jnp.concatenate([tables_one, tables_two], axis=0)).reshape(-1, width),
        ],
        axis=0,
    )
    little_rows = early.shape[0]
    early = jnp.pad(early, ((0, -little_rows % 8), (0, 0)))
    d_two, d_three, grad_rows = grads_two_call(
        slots, turned, lefts, half_one, half_two, weight_qkv, d_pre, normed,
        both_t, coefs, early, chips, (column_in, near_a, near_b),
    )

    piece = 2 * rows_a
    half = width // 2
    sum_out = lax.psum_scatter(d_out, CHIP).astype(F32)
    sum_in = scatter_line(column_in, (d_two,))
    column_one = jnp.concatenate([scatter_step(near_a, "y", (d_two,)), scatter_step(near_b, "x", (d_two,))], axis=1)
    near_two = scatter_step(d_two, "x", (sum_in, column_one))
    near_three = scatter_step(d_three, "y", (sum_in, column_one))
    sum_in = sum_in.reshape(-1, piece, half).transpose(1, 0, 2).reshape(piece, hidden)
    sum_one = scatter_line(column_one)
    column_late = jnp.concatenate(
        [scatter_step(near_two, "y", (sum_one,)), scatter_step(near_three, "x", (sum_one,))], axis=1
    )
    sum_one = sum_one.reshape(5, piece, half)
    near = both.shape[1] // chips
    squares = jnp.sum(sum_out * sum_out) + jnp.sum(sum_in * sum_in) + jnp.sum(sum_one * sum_one)
    own_late = late_call(column_late, squares, chips, piece, near // 2)
    other_late = swap(own_late)

    def own_rows(value, axis):
        first, second = jnp.split(value, 2, axis=axis)
        return trade(first, second)

    def by_stream(own, other):
        return jnp.where(seen, jnp.stack([own, other]), jnp.stack([other, own]))

    def little_of(late):
        rows = late[3 * piece + 2 * near : late.shape[0] - 8].reshape(2, -1, half)
        return jnp.concatenate([rows[0], rows[1]], axis=-1)

    little = by_stream(little_of(own_late), little_of(other_late))
    member = 2 * chip_of(0, 0, 0) + core
    vec_sum = lax.dynamic_slice_in_dim(little[:, :7], member * vectors.shape[1], vectors.shape[1], 2)
    grad_vec = jnp.stack(
        [vec_sum[0, 0], vec_sum[0, 1]]
        + [vec_sum[s, k + m] for k in (2, 4) for s in range(2) for m in range(2)]
        + [vec_sum[0, 6], vec_sum[1, 6]]
    )
    bias_lines = hidden // width
    bias_sum = little[:, 8 : 8 + bias_lines].reshape(2, hidden)
    grad_bias = lax.dynamic_slice_in_dim(bias_sum, member * bias_in.shape[1], bias_in.shape[1], 1)
    pos_sum = little[:, 8 + bias_lines : little_rows].reshape(2, H, 3, NR).transpose(0, 2, 1, 3)
    grad_pos = lax.dynamic_slice_in_dim(pos_sum, member * pos_tables.shape[3], pos_tables.shape[3], 3)

    tile = chip_squares_call(own_late, other_late, 3 * piece, 3 * piece + 2 * near)
    tile = functools.reduce(jnp.add, around(tile))
    norm = functools.reduce(jnp.add, line_of(tile))
    grad_norm = jnp.sqrt(norm[0, 0])

    out_own, out_other = out[:count], swap(out[count:])
    grad_own, grad_other = grad_rows[:count], swap(grad_rows[count:])
    out_visual = mine_of(out_own, out_other)[None]
    out_text = mine_of(out_other, out_own)[None]
    grad_visual = mine_of(grad_own, grad_other)[None]
    grad_text = mine_of(grad_other, grad_own)[None]

    def turned_pos(value):
        return jnp.swapaxes(value, 2, 3)

    groups = (
        (attn_w, attn_mom, attn_sec),
        (ffn_in, in_mom, in_sec) + tuple(own_rows(sum_in, 0)),
        (ffn_out, out_mom, out_sec) + tuple(own_rows(sum_out, 0)),
        (bias_in, bias_mom, bias_sec, grad_bias),
        (vectors, vec_mom, vec_sec, grad_vec),
        tuple(turned_pos(part) for part in (pos_tables, pos_mom, pos_sec, grad_pos)),
        (spatial, spatial_mom, spatial_sec),
    )
    new = adam_call(
        norm, seen.astype(jnp.int32).reshape(1), piece, near // 2,
        (*own_rows(sum_one, 1), own_late, other_late), groups,
    )
    results = [out_visual, out_text, grad_visual, grad_text, grad_norm] + list(new)
    for index in range(5 + 18, 5 + 21):
        results[index] = turned_pos(results[index])
    return tuple(results)


def solution(mesh):
    devices = mesh.devices.reshape(-1)
    chips = devices.size // 2
    deep = 4 if chips % 4 == 0 else 1
    side = int(round((chips // deep) ** 0.5))
    if deep * side * side != chips:
        deep, side = chips, 1
    fine = Mesh(devices.reshape(deep, side, side, 2), AXES)
    every = AXES
    data = P(every, None, None)
    in_specs = (
        data, data, P(every), data, data, data,
        P(None, None, every, None), P(None, every, None), P(None, every, None),
        P(None, every), P(None, every), P(None, None, None, every), P(None, every, None),
        P(None, None, every, None), P(None, None, every, None),
        P(None, every, None), P(None, every, None), P(None, every, None), P(None, every, None),
        P(None, every), P(None, every), P(None, every), P(None, every),
        P(None, None, None, every), P(None, None, None, every),
        P(None, every, None), P(None, every, None),
    )
    weights = P(None, None, every, None)
    rows = P(None, every, None)
    flat = P(None, every)
    last = P(None, None, None, every)
    out_specs = (
        (data, data, data, data, P())
        + (weights,) * 4 + (rows,) * 8 + (flat,) * 6 + (last,) * 3 + (rows,) * 3
    )
    return jax.shard_map(body, mesh=fine, in_specs=in_specs, out_specs=out_specs, check_vma=False)
```
